512 devices in a mesh: tm: 16 (over z), req: 32 (over y, x, core).
Axes of the slice: x: 4, y: 4, z: 16, core: 2. Of those that a mesh axis runs over, the one named last changes fastest.
Arguments:
- latents: float32 [16, 64, 4096], P('tm', None, 'req'), may hold values from -6 to 6
- time_terms: float32 [16, 4, 3072], replicated, may hold values from -4 to 4
- step_sizes: float32 [16], replicated, may hold values from 0.05 to 0.25
- doc_embed: bfloat16 [256, 3072], P('req', 'tm'), may hold values from -6 to 6
- pack_docs: int32 [256], P('req'), may hold values from 0 to 255, each once
- segment_ids: int32 [32, 128], P('req'), may hold values from 0 to 7, never falling along the last dimension, each value on 1 to 64 neighbouring positions
- w_in: bfloat16 [64, 3072], replicated, may hold values from -0.75 to 0.75
- w_qkv: bfloat16 [3072, 3, 16, 128], P(None, None, 'tm')
- query_gain: float32 [16, 128], P('tm'), may hold values from 0.5 to 6, as said below
- key_gain: float32 [16, 128], P('tm'), may hold values from 0.5 to 6, as said below
- w_proj: bfloat16 [16, 128, 3072], P('tm'), may hold values from -0.125 to 0.125
- w_final: bfloat16 [3072, 64], replicated, may hold values from -0.109375 to 0.109375
Outputs:
- new_latents: float32 [16, 64, 4096], P('tm', None, 'req')
The draws below stay inside these ranges and needn't reach their ends.
Inputs may be any that keep to these rules, and one draw needn't show every extreme that they name: `pack_docs`: a permutation of the documents; pack r holds the documents at positions r * 8 to (r + 1) * 8 - 1. `segment_ids`: in each pack the segment numbers never fall, every segment 0 to 7 is present with 1 to 64 slots, and one has exactly 64. `query_gain`: positive gains. `key_gain`: positive gains.
All inputs are finite; a program needn't handle non-finite values.
Results may differ from the reference program's by a relative error of at most 0.004.
Values may be sent and summed in bfloat16 or wider, within the bound.
No kernel may reach another device: no remote copies, remote signals or barrier semaphores. Data moves between devices by JAX's collectives and lax.ppermute only.
A program may use at most 64 MiB of HBM per device.

```python
import math
import jax
import jax.numpy as jnp
import numpy as np
from jax import lax

D = 3072
LAT = 64
HEAD = 128
HH = 16
PACK = 128
DOCS_DEV = 8
DOC_MOST = 64
TIMES = 16
TOKENS = 4096
TOTAL_DOCS = 256
N_REQ = 32


def gain_table(key, low, high):
    return jnp.exp(jax.random.uniform(key, (HH, HEAD), jnp.float32, math.log(low), math.log(high)))


def draw_query_gain(key, part):
    key = jax.random.fold_in(key, 11)
    return gain_table(key, 0.6, 1.8)


def draw_key_gain(key, part):
    key = jax.random.fold_in(key, 23)
    return gain_table(key, 0.6, 1.8)


def draw_w_qkv(key, part):
    key = jax.random.fold_in(key, 37)
    first = jax.random.fold_in(key, 0)
    base = jax.random.normal(first, (D, 3, HH, HEAD), jnp.float32) * D ** (-0.5)
    return base.astype(jnp.bfloat16)


def block_levels(key, dims, cuts, smallest, largest):
    def one(position, parts):
        draws = jax.random.uniform(jax.random.fold_in(jax.random.fold_in(key, 6), position), (parts,), jnp.float32, smallest / len(cuts), largest / len(cuts))
        return jnp.repeat(jnp.exp(draws), dims[position] // parts).reshape((-1,) + (1,) * (len(dims) - position - 1))

    loudness = one(*cuts[0])
    for cut in cuts[1:]:
        loudness = loudness * one(*cut)
    return loudness


def split_up(amount, total, most, skew):
    portions = [(1 << 20) // math.isqrt(rank ** skew) + 1 for rank in range(2, amount + 1)]
    surplus, holding = total - most - (amount - 1), [1] * (amount - 1)
    while surplus > 0:
        candidates = [i for i in range(amount - 1) if holding[i] < most]
        pool, budget = sum([portions[i] for i in candidates]), surplus
        for i in candidates:
            more = min(most - holding[i], max(1, budget * portions[i] // pool), surplus)
            holding[i] = holding[i] + more
            surplus = surplus - more
    return np.array([most] + holding)


def ragged(own_key, count, total, most, lean):
    if count == 2:
        one = jax.random.randint(own_key, (), max(1, total - most), min(most, total - 1) + 1)
        return jnp.stack([one, total - one])
    lengths = jnp.asarray(split_up(count, total, most, lean), jnp.int32)
    twos = (count - 1) // 2
    source_of, taker = lengths[1:1 + 2 * twos:2], lengths[2:2 + 2 * twos:2]
    room = jnp.minimum(source_of - 1, most - taker)
    passed = jax.random.randint(jax.random.fold_in(own_key, 1), (twos,), 0, 1 << 20) % (room + 1)
    lengths = lengths.at[1:1 + 2 * twos:2].set(source_of - passed).at[2:2 + 2 * twos:2].set(taker + passed)
    return lengths[jax.random.permutation(jax.random.fold_in(own_key, 2), count)]


def normal_values(own_key, dims, scale, reach, pieces=(), dtype=jnp.bfloat16):
    array = scale * jax.random.normal(own_key, dims, jnp.float32)
    if pieces:
        array = array * block_levels(own_key, dims, pieces, -0.22, 0.18)
    return jnp.clip(array, -reach, reach).astype(dtype)


def setup_inputs(seed: int = 0) -> dict:
    streams_of = jax.random.split(jax.random.key(seed), 13)
    return {
        "latents": normal_values(streams_of[0], (TIMES, LAT, TOKENS), 1.0, 6.0, ((0, 16), (2, 32)), jnp.float32),
        "time_terms": normal_values(streams_of[1], (TIMES, 4, D), 0.5, 4.0, (), jnp.float32),
        "step_sizes": jnp.clip(jnp.exp(jax.random.uniform(streams_of[2], (TIMES,), jnp.float32, math.log(0.05), math.log(0.25))), 0.05, 0.25),
        "doc_embed": normal_values(streams_of[3], (TOTAL_DOCS, D), 1.0, 6.0, ((0, 32), (1, 16))),
        "pack_docs": jax.random.permutation(streams_of[4], TOTAL_DOCS).astype(jnp.int32),
        "segment_ids": jax.vmap(lambda own: jnp.searchsorted(jnp.cumsum(ragged(own, DOCS_DEV, PACK, DOC_MOST, 2)), jnp.arange(PACK), side="right"))(jax.random.split(streams_of[5], N_REQ)).reshape((N_REQ, PACK)).astype(jnp.int32),
        "w_in": normal_values(streams_of[6], (LAT, D), LAT ** -0.5, 0.75),
        "w_qkv": draw_w_qkv(jax.random.fold_in(streams_of[12], 71), 0),
        "query_gain": draw_query_gain(jax.random.fold_in(streams_of[12], 71), 0),
        "key_gain": draw_key_gain(jax.random.fold_in(streams_of[12], 71), 0),
        "w_proj": normal_values(streams_of[10], (HH, HEAD, D), (HH * HEAD) ** -0.5, 0.125, ((0, 16),)),
        "w_final": normal_values(streams_of[11], (D, LAT), D ** -0.5, 0.109375),
    }


EPS = 1e-06
MASKED = -1e+30

def layer_norm(values):
    mean = lax.optimization_barrier(jnp.mean(values, axis=-1, keepdims=True))
    centred = values - mean
    spread = lax.optimization_barrier(jnp.mean(centred * centred, axis=-1, keepdims=True))
    return centred * lax.rsqrt(spread + EPS)

def rms_scale(values, gains):
    power = lax.optimization_barrier(jnp.mean(values * values, axis=-1, keepdims=True))
    return (values * lax.rsqrt(power + EPS) * gains).astype(jnp.bfloat16)

def hidden_state(latent_block, terms, token_vectors, w_in):
    lowered = latent_block.astype(jnp.bfloat16)
    hidden = lax.dot_general(lowered, w_in, (((0,), (0,)), ((), ())), preferred_element_type=jnp.float32)
    hidden = hidden + terms[0] + token_vectors
    modulated = layer_norm(hidden) * (1.0 + terms[2]) + terms[1]
    return (hidden, modulated.astype(jnp.bfloat16))

def reference(latents, time_terms, step_sizes, doc_embed, pack_docs, segment_ids, w_in, w_qkv, query_gain, key_gain, w_proj, w_final):
    pack_table = pack_docs.reshape(N_REQ, DOCS_DEV)
    token_docs = jnp.take_along_axis(pack_table, segment_ids, axis=1).reshape(-1).astype(jnp.int32)
    token_vectors = jnp.take(doc_embed, token_docs, axis=0).astype(jnp.float32)
    same_doc = segment_ids[:, :, None] == segment_ids[:, None, :]
    w_final_wide = w_final.astype(jnp.float32)
    qkv_matrix = w_qkv.reshape(D, 3 * HH * HEAD)
    scale = HEAD ** (-0.5)

    def one_step(pair):
        block, terms = pair
        hidden, normed = hidden_state(block, terms, token_vectors, w_in)
        projected = jnp.dot(normed, qkv_matrix, preferred_element_type=jnp.float32).reshape(N_REQ, PACK, 3, HH, HEAD)
        queries = lax.optimization_barrier(rms_scale(projected[:, :, 0], query_gain)).astype(jnp.float32)
        keys = lax.optimization_barrier(rms_scale(projected[:, :, 1], key_gain)).astype(jnp.float32)
        values = lax.optimization_barrier(projected[:, :, 2].astype(jnp.bfloat16)).astype(jnp.float32)
        scores = jnp.einsum('rqhe,rphe->rhqp', queries, keys) * scale
        scores = jnp.where(same_doc[:, None], scores, MASKED)
        top = lax.optimization_barrier(jnp.max(scores, axis=-1, keepdims=True))
        raised = jnp.exp(scores - top)
        weights = lax.optimization_barrier((raised / lax.optimization_barrier(jnp.sum(raised, axis=-1, keepdims=True))).astype(jnp.bfloat16))
        attended = jnp.einsum('rhqp,rphe->rqhe', weights.astype(jnp.float32), values).astype(jnp.bfloat16)
        attended = attended.reshape(TOKENS, HH, HEAD).transpose(1, 0, 2)

        def head_term(total, item):
            rows, proj_rows = item
            outer = (jnp.dot(rows, proj_rows, preferred_element_type=jnp.float32) * terms[3]).astype(jnp.bfloat16)
            term = lax.dot_general(w_final, outer, (((0,), (1,)), ((), ())), preferred_element_type=jnp.float32)
            return (total + term, None)
        start = lax.dot_general(w_final_wide, hidden, (((0,), (1,)), ((), ())), precision=lax.Precision.HIGHEST)
        total, unused = lax.scan(head_term, start, (attended, w_proj))
        return total
    drifts = lax.map(one_step, (latents, time_terms))
    scaled = step_sizes[:, None, None] * drifts
    before = jnp.cumsum(scaled, axis=0) - scaled
    return latents[0][None] + before
```

```python
import functools

import jax
import jax.numpy as jnp
from jax import lax
from jax.experimental import pallas as pl
from jax.experimental.pallas import tpu as pltpu
from jax.sharding import PartitionSpec as P

EPS = 1e-06
MASKED = -1e30
BF16, F32 = jnp.bfloat16, jnp.float32
HIGHEST = lax.Precision.HIGHEST
NN = (((1,), (0,)), ((), ()))
NT = (((1,), (1,)), ((), ()))
VMEM = pl.BlockSpec(memory_space=pltpu.VMEM)
SMEM = pl.BlockSpec(memory_space=pltpu.SMEM)
PARAMS = pltpu.CompilerParams(vmem_limit_bytes=48 * 2**20)


def dot(left, right, dims=NN, precision=None):
    return lax.dot_general(left, right, dims, precision=precision, preferred_element_type=F32)


def two_parts(values):
    high = values.astype(BF16)
    return high, (values - high.astype(F32)).astype(BF16)


def centre(values):
    return values - jnp.mean(values, axis=-1, keepdims=True)


def weights_kernel(
    steps, w_in, terms, w_qkv, w_final, w_proj, inward, shifts, outward, centred, rows, shift_rows
):
    times, chans = inward.shape[0], w_in.shape[0]
    wide, head = terms.shape[2], w_proj.shape[0]
    group = rows.shape[0] // chans
    centred[...] = centre(w_in[...].astype(F32))
    gram = dot(centred[...], centred[...], NT, HIGHEST)
    gram = jnp.concatenate(two_parts(gram), axis=0)
    gram = jnp.concatenate([gram, jnp.zeros_like(gram)], axis=1)

    def one(step, carry):
        for j in range(group):
            t = step * group + j
            scaled = centred[...] * (1.0 + terms[t, 2:3, :])
            rows[j * chans : (j + 1) * chans, :] = scaled.astype(BF16)
            shift_rows[pl.ds(t, 1), :] = terms[t, 1:2, :]
        for c in range(3):
            high, low = two_parts(dot(rows[...], w_qkv[c]))
            for j in range(group):
                t = step * group + j
                span = slice(j * chans, (j + 1) * chans)
                inward[t, :chans, c * head : (c + 1) * head] = high[span]
                inward[t, chans:, c * head : (c + 1) * head] = low[span]
        for j in range(group):
            t = step * group + j
            inward[t, :, 3 * head :] = gram
            gated = w_final[...].astype(F32) * terms[t, 3:4, :]
            rows[j * chans : (j + 1) * chans, :] = gated.astype(BF16)
        back = dot(rows[...], w_proj[...], NT)
        for j in range(group):
            t = step * group + j
            outward[t] = (back[j * chans : (j + 1) * chans] * steps[t]).astype(BF16)
        return carry

    lax.fori_loop(0, times // group, one, 0)
    high, low = two_parts(shift_rows[...])
    for c in range(3):
        shifts[:, c * head : (c + 1) * head] = dot(high, w_qkv[c]) + dot(low, w_qkv[c])


def heads_kernel(
    low,
    docs,
    terms,
    w_qkv,
    w_in,
    inward,
    outward,
    shifts,
    query_gain,
    key_gain,
    bias,
    member,
    start,
    sums,
    parts,
    scaled_rows,
    doc_terms,
):
    times, chans, tokens = low.shape
    wide, head = terms.shape[2], w_qkv.shape[2]
    count = docs.shape[1]
    documents = jnp.concatenate([docs[i].astype(F32) for i in range(docs.shape[0])], axis=1)

    def embed(pair, carry):
        whole, scaled = [], []
        for j in range(2):
            t = pair * 2 + j
            row = centre(documents + terms[t, 0:1, :])
            whole.append(row)
            scaled.append(row * (1.0 + terms[t, 2:3, :]))
        both = jnp.concatenate(whole, axis=0)
        at = pl.multiple_of(pair * 2 * count, 2 * count)
        scaled_rows[pl.ds(at, 2 * count), :] = jnp.concatenate(scaled, axis=0).astype(BF16)
        high, rest = two_parts(both)
        parts[0, pl.ds(at, 2 * count), :] = high
        parts[1, pl.ds(at, 2 * count), :] = rest
        power = jnp.sum(both * both, axis=-1, keepdims=True)
        lane = lax.broadcasted_iota(jnp.int32, (2 * count, head), 1)
        doc_terms[pl.ds(at, 2 * count), 3 * head :] = jnp.where(lane == chans, power, 0.0)
        return carry

    lax.fori_loop(0, times // 2, embed, 0, unroll=2)
    for c in range(3):
        doc_terms[:, c * head : (c + 1) * head] = dot(scaled_rows[...], w_qkv[c])
    cross = dot(parts[0], w_in[...], NT) + dot(parts[1], w_in[...], NT)
    doc_terms[:, 3 * head :] += jnp.concatenate([2.0 * cross, jnp.zeros_like(cross)], axis=1)

    lane = lax.broadcasted_iota(jnp.int32, (tokens, head - chans), 1)
    unit = jnp.where(lane == 0, 1.0, 0.0).astype(F32)
    scale = head**-0.5

    def one_time(t, total):
        sums[t] = total.astype(BF16)
        turned = low[t].astype(F32).T
        left = turned.astype(BF16)
        left = jnp.concatenate([left, left, member[...]], axis=1)
        at = pl.multiple_of(t * count, count)
        high, rest = two_parts(doc_terms[pl.ds(at, count), :])
        here = jnp.concatenate([high.astype(F32), rest.astype(F32)], axis=0).astype(BF16)
        right = jnp.concatenate([inward[t], here], axis=0)
        mixed = dot(left, right)
        spread = jnp.sum(
            mixed[:, 3 * head :] * jnp.concatenate([turned, unit], axis=1), axis=-1, keepdims=True
        )
        projected = mixed[:, : 3 * head] * lax.rsqrt(spread / wide + EPS) + shifts[pl.ds(t, 1), :]

        def normal(values, gains):
            power = jnp.mean(values * values, axis=-1, keepdims=True)
            return (values * lax.rsqrt(power + EPS) * gains).astype(BF16)

        queries = normal(projected[:, :head], query_gain[...])
        keys = normal(projected[:, head : 2 * head], key_gain[...])
        values = projected[:, 2 * head :].astype(BF16)
        scores = dot(queries, keys, NT) * scale + bias[...]
        raised = jnp.exp(scores - jnp.max(scores, axis=-1, keepdims=True))
        weights = (raised / jnp.sum(raised, axis=-1, keepdims=True)).astype(BF16)
        attended = dot(weights, values).astype(BF16)
        return total + dot(outward[t], attended, NT)

    def several(step, total):
        for j in range(4):
            total = one_time(step * 4 + j, total)
        return total

    lax.fori_loop(0, times // 4, several, start[...])


def residual_kernel(weights, low, docs, terms, w_in, w_final, member, out):
    times = low.shape[0]
    documents = jnp.concatenate([docs[i].astype(F32) for i in range(docs.shape[0])], axis=1)
    mixed = jnp.zeros(low.shape[1:], F32)
    embedded = jnp.zeros((1, terms.shape[2]), F32)
    whole = 0.0
    for t in range(times):
        mixed = mixed + weights[t] * low[t].astype(F32)
        embedded = embedded + weights[t] * terms[t, 0:1, :]
        whole = whole + weights[t]
    rows = embedded + whole * documents
    high = rows.astype(BF16)
    middle, rest = two_parts(rows - high.astype(F32))
    rows = jnp.concatenate(
        [high.astype(F32), middle.astype(F32), rest.astype(F32)], axis=0
    ).astype(BF16)
    narrow = dot(w_final[...], rows, NT)
    count = docs.shape[1]
    narrow = narrow[:, :count] + narrow[:, count : 2 * count] + narrow[:, 2 * count :]
    direct = dot(w_final[...], w_in[...], NT)
    chosen = dot(narrow, member[:, :count].astype(F32), NT, HIGHEST)
    out[...] = dot(direct, mixed, NN, HIGHEST) + chosen


def fold_weights(steps, w_in, terms, w_qkv, w_final, w_proj):
    times, wide, head, chans = terms.shape[0], terms.shape[2], w_proj.shape[0], w_in.shape[0]
    return pl.pallas_call(
        weights_kernel,
        out_shape=(
            jax.ShapeDtypeStruct((times, 2 * chans, 4 * head), BF16),
            jax.ShapeDtypeStruct((times, 3 * head), F32),
            jax.ShapeDtypeStruct((times, chans, head), BF16),
        ),
        in_specs=[SMEM] + [VMEM] * 5,
        out_specs=(VMEM, VMEM, VMEM),
        scratch_shapes=[
            pltpu.VMEM((chans, wide), F32),
            pltpu.VMEM((4 * chans, wide), BF16),
            pltpu.VMEM((times, wide), F32),
        ],
        compiler_params=PARAMS,
        name="fold_weights",
    )(steps, w_in, terms, w_qkv, w_final, w_proj)


def run_heads(low, docs, terms, w_qkv, *rest):
    rows = terms.shape[0] * docs.shape[1]
    wide, head = terms.shape[2], w_qkv.shape[2]
    return pl.pallas_call(
        heads_kernel,
        out_shape=jax.ShapeDtypeStruct(low.shape, BF16),
        in_specs=[VMEM] * 13,
        out_specs=VMEM,
        scratch_shapes=[
            pltpu.VMEM((2, rows, wide), BF16),
            pltpu.VMEM((rows, wide), BF16),
            pltpu.VMEM((rows, 4 * head), F32),
        ],
        compiler_params=PARAMS,
        name="run_heads",
    )(low, docs, terms, w_qkv, *rest)


def residual(weights, low, *rest):
    return pl.pallas_call(
        residual_kernel,
        out_shape=jax.ShapeDtypeStruct(low.shape[1:], F32),
        in_specs=[SMEM] + [VMEM] * 6,
        out_specs=VMEM,
        compiler_params=PARAMS,
        name="residual",
    )(weights, low, *rest)


def to_all(part, axis, size):
    copies = jnp.broadcast_to(part[None], (size,) + part.shape)
    return lax.all_to_all(copies, axis, 0, 0)


def local(
    latents,
    time_terms,
    step_sizes,
    doc_embed,
    pack_docs,
    segment_ids,
    w_in,
    w_qkv,
    query_gain,
    key_gain,
    w_proj,
    w_final,
):
    here = lax.axis_index("tm")
    times, owners = lax.axis_size("tm"), lax.axis_size("req")
    count, piece = doc_embed.shape
    lowered = latents[0].astype(BF16)
    w_heads = w_qkv[:, :, 0, :].transpose(1, 0, 2)
    w_last = w_final.T

    low = to_all(lowered, "tm", times)
    table = to_all(doc_embed, "req", owners).reshape(owners * count, piece)
    wanted = jnp.broadcast_to(pack_docs[None, :], (times, count)).reshape(-1)
    places = jnp.arange(owners * count, dtype=jnp.int32)
    pick = (wanted[:, None] == places[None, :]).astype(BF16)
    chosen = dot(pick, table).astype(BF16).reshape(times, count, piece)
    docs = lax.all_to_all(chosen, "tm", 0, 0)

    inward, shifts, outward = fold_weights(step_sizes, w_in, time_terms, w_heads, w_last, w_proj[0])
    segments = segment_ids[0]
    member = (segments[:, None] == jnp.arange(count, dtype=jnp.int32)[None, :]).astype(BF16)
    member = jnp.concatenate([member, member], axis=1)
    bias = jnp.where(segments[:, None] == segments[None, :], 0.0, MASKED).astype(F32)
    start = jnp.where(here == 0, latents[0] - lowered.astype(F32), 0.0)
    sums = run_heads(
        low,
        docs,
        time_terms,
        w_heads,
        w_in,
        inward,
        outward,
        shifts,
        query_gain,
        key_gain,
        bias,
        member,
        start,
    )
    arrived = lax.all_to_all(sums, "tm", 0, 0)
    weights = jnp.where(jnp.arange(times) < here, step_sizes, 0.0)
    direct = residual(weights, low, docs, time_terms, w_in, w_last, member)
    before = low[0].astype(F32) + direct + jnp.sum(arrived.astype(F32), axis=0)
    return jnp.where(here == 0, latents[0], before)[None]


def solution(mesh):
    in_specs = (
        P("tm", None, "req"),
        P(),
        P(),
        P("req", "tm"),
        P("req"),
        P("req", None),
        P(),
        P(None, None, "tm", None),
        P("tm", None),
        P("tm", None),
        P("tm", None, None),
        P(),
    )
    out_specs = P("tm", None, "req")
    return jax.shard_map(local, mesh=mesh, in_specs=in_specs, out_specs=out_specs, check_vma=False)
```

```python
import jax
import jax.numpy as jnp
from jax import lax
from jax.experimental import pallas as pl
from jax.experimental.pallas import tpu as pltpu
from jax.sharding import PartitionSpec as P

EPS = 1e-06
MASKED = -1e30
LOG2E = 1.4426950408889634
BF16, F32 = jnp.bfloat16, jnp.float32
NN = (((1,), (0,)), ((), ()))
NT = (((1,), (1,)), ((), ()))
VMEM = pl.BlockSpec(memory_space=pltpu.VMEM)
SMEM = pl.BlockSpec(memory_space=pltpu.SMEM)
HBM = pl.BlockSpec(memory_space=pltpu.HBM)
PARAMS = pltpu.CompilerParams(vmem_limit_bytes=24 * 2**20)


def dot(left, right, dims=NN, precision=None):
    return lax.dot_general(left, right, dims, precision=precision, preferred_element_type=F32)


def two_parts(values):
    high = values.astype(BF16)
    return high, (values - high.astype(F32)).astype(BF16)


def stack_rows(*parts):
    return jnp.concatenate([p.astype(F32) for p in parts], axis=0).astype(BF16)


def centre(values):
    return values - jnp.mean(values, axis=-1, keepdims=True)


def fetch(pairs, sems):
    copies = [pltpu.make_async_copy(a, b, sems.at[i]) for i, (a, b) in enumerate(pairs)]
    for copy in copies:
        copy.start()
    return copies


def inward_kernel(
    w_in, terms, latents, pack_docs, w_qkv,
    inward, pieces, pick, lowered, rest,
    w_in_v, terms_v, latents_v, packs_v, centred, rows, sems,
):
    chans, wide = w_in_v.shape
    times = terms_v.shape[0]
    head = w_qkv.shape[2]
    copies = fetch(
        [(w_in, w_in_v), (terms, terms_v), (latents, latents_v), (pack_docs, packs_v)], sems
    )
    copies[0].wait()
    centred[...] = centre(w_in_v[...].astype(F32))
    high, low = two_parts(centred[...])
    pieces[:chans, :] = high
    pieces[chans:, :] = low
    copies[1].wait()
    for step in range(times // 4):
        for j in range(4):
            scaled = centred[...] * (1.0 + terms_v[step * 4 + j, 2:3, :])
            rows[step % 2, j * chans : (j + 1) * chans, :] = scaled.astype(BF16)
        for c in range(3):
            turned = dot(rows[step % 2], w_qkv[c]).T.astype(BF16)
            span = slice(c * head, (c + 1) * head)
            inward[2 * step, span, :] = turned[:, : 2 * chans]
            inward[2 * step + 1, span, :] = turned[:, 2 * chans :]
    copies[2].wait()
    values = latents_v[0]
    lowered[...] = values.astype(BF16)
    rest[...] = values - values.astype(BF16).astype(F32)
    copies[3].wait()
    count = packs_v.shape[1]
    column = jnp.broadcast_to(packs_v[...].astype(F32), (count, count))
    eye = lax.broadcasted_iota(jnp.int32, (count, count), 0) == lax.broadcasted_iota(
        jnp.int32, (count, count), 1
    )
    column = jnp.sum(jnp.where(eye, column, 0.0), axis=1, keepdims=True)
    places = lax.broadcasted_iota(jnp.int32, (count, pick.shape[1]), 1).astype(F32)
    chosen = jnp.where(places == column, 1.0, 0.0)
    pick[...] = stack_rows(chosen, jnp.zeros_like(chosen))


def select_kernel(table, pick, lowered, out, staged, sems):
    size, rows, lanes = out.shape
    chans = lowered.shape[0]
    owners, count, piece = table.shape
    flat = table[...].reshape(owners * count, piece)
    chosen = dot(pick[...], flat)[:count]
    tail = jnp.concatenate(
        [chosen[:, lanes:], jnp.zeros((count, 2 * lanes - piece), F32)], axis=1
    )
    staged[:chans, :] = lowered[...]
    staged[chans:, :] = stack_rows(chosen[:, :lanes], tail)
    copies = fetch([(staged, out.at[i]) for i in range(size)], sems)
    for copy in copies:
        copy.wait()


def outward_kernel(
    steps, terms, w_final, w_proj, query_gain, key_gain, segments, sent, pieces, w_qkv,
    outward, shifts, gram, cross, embedded, scales, gains, bias, member,
    terms_v, w_final_v, w_proj_v, gains_v, segments_v, rows, sems,
):
    del sent
    times, chans, head = outward.shape
    copies = fetch(
        [
            (terms, terms_v), (w_final, w_final_v), (w_proj, w_proj_v),
            (query_gain, gains_v.at[0]), (key_gain, gains_v.at[1]), (segments, segments_v),
        ],
        sems,
    )
    both = pieces[...]
    square = dot(both, both, NT)
    square = square[:chans, :chans] + square[chans:, :chans] + square[:chans, chans:]
    high, low = two_parts(square)
    gram[:chans, :] = high
    gram[chans:, :] = low
    copies[0].wait()
    moved, means = [], []
    for t in range(times):
        moved.append(terms_v[t, 1:2, :])
        means.append(centre(terms_v[t, 0:1, :]))
        scales[t : t + 1, :] = 1.0 + terms_v[t, 2:3, :]
    moved, means = jnp.concatenate(moved, axis=0), jnp.concatenate(means, axis=0)
    embedded[...] = means
    high, low = two_parts(moved)
    split = stack_rows(high, low)
    for c in range(3):
        shift = dot(split, w_qkv[c])
        shifts[:, c * head : (c + 1) * head] = shift[:times] + shift[times:]
    high, low = two_parts(means)
    mixed = dot(stack_rows(high, low), both, NT)
    cross[...] = mixed[:times, :chans] + mixed[times:, :chans] + mixed[:times, chans:]
    copies[1].wait()
    copies[2].wait()
    for step in range(times // 4):
        for j in range(4):
            gated = w_final_v[...].astype(F32) * terms_v[step * 4 + j, 3:4, :]
            rows[step % 2, j * chans : (j + 1) * chans, :] = gated.astype(BF16)
        back = dot(rows[step % 2], w_proj_v[...], NT)
        for j in range(4):
            t = step * 4 + j
            outward[t] = (back[j * chans : (j + 1) * chans] * steps[t]).astype(BF16)
    copies[3].wait()
    copies[4].wait()
    copies[5].wait()
    tokens = segments_v.shape[1]
    gains[0] = jnp.broadcast_to(gains_v[0] * (head**-0.5 * LOG2E), (head, head)).T
    gains[1] = jnp.broadcast_to(gains_v[1], (head, head)).T
    ids = jnp.broadcast_to(segments_v[...].astype(F32), (tokens, tokens))
    bias[...] = jnp.where(ids == ids.T, 0.0, MASKED)
    count = member.shape[0]
    numbers = lax.broadcasted_iota(jnp.int32, (count, tokens), 0).astype(F32)
    member[...] = jnp.where(numbers == ids[:count], 1.0, 0.0)


def gather_documents(arrived, chans, count, piece):
    parts = []
    for i in range(arrived.shape[0]):
        block = arrived[i, chans:, :].astype(F32)
        parts.append(block[:count])
        parts.append(block[count:, : piece - block.shape[1]])
    return jnp.concatenate(parts, axis=1)


def heads_kernel(
    here, arrived, w_qkv, inward, outward, shifts, gram, cross, pieces, embedded, scales, gains,
    bias, member, rest,
    out,
    rows, staged, sems,
):
    times, chans, head = outward.shape
    count, tokens = member.shape
    wide = pieces.shape[1]
    documents = gather_documents(arrived, chans, count, wide // times)
    near = dot(documents.astype(BF16), pieces[:chans, :], NT) + dot(
        documents.astype(BF16), pieces[chans:, :], NT
    )
    documents = centre(documents)
    powers = []
    for t in range(0, times, 2):
        pair = []
        for j in range(2):
            row = documents + embedded[t + j : t + j + 1, :]
            powers.append(jnp.sum(row * row, axis=-1, keepdims=True))
            pair.append(row * scales[t + j : t + j + 1, :])
        rows[t * count : (t + 2) * count, :] = jnp.concatenate(pair, axis=0).astype(BF16)
    base = jnp.concatenate([dot(rows[...], w_qkv[c]) for c in range(3)], axis=1)
    turned = []
    for half in range(2):
        span = slice(half * 8 * count, (half + 1) * 8 * count)
        block = [base[span], shifts[half * 8 : (half + 1) * 8, :]]
        left = head - 8 * count - 8
        block.append(jnp.zeros((left, 3 * head), F32))
        turned.append(jnp.concatenate(block, axis=0).T.astype(BF16))

    belongs = member[...]
    scaled_low, rates = [], []
    for t in range(times):
        mixed = 2.0 * (near + cross[t : t + 1, :])
        high, low = two_parts(mixed)
        left = jnp.concatenate([gram[...], stack_rows(high, low)], axis=0)
        values = arrived[t, :chans, :]
        whole = dot(left, values)
        both = whole[:chans] + whole[chans : 2 * chans]
        values = values.astype(F32)
        other = whole[2 * chans : 2 * chans + count] + whole[2 * chans + count :]
        spread = jnp.sum(both * values, axis=0, keepdims=True) + jnp.sum(
            belongs * (other + powers[t]), axis=0, keepdims=True
        )
        rate = lax.rsqrt(spread / wide + EPS)
        rates.append(rate)
        scaled_low.append((values * rate).astype(BF16))

    def unit(values, gain):
        power = jnp.mean(values * values, axis=0, keepdims=True)
        return values * lax.rsqrt(power + EPS) * gain

    total = jnp.where(here[0] == 0, rest[...], 0.0)
    empty = jnp.zeros((chans, tokens), BF16)
    for t in range(times):
        staged[t] = total.astype(BF16)
        half, j = divmod(t, 8)
        left = jnp.concatenate([inward[t // 2], turned[half]], axis=1)
        first = [scaled_low[t], empty] if t % 2 == 0 else [empty, scaled_low[t]]
        ones = lax.broadcasted_iota(jnp.int32, (8, tokens), 0) == j
        second = [jnp.zeros((j * count, tokens), F32)] if j else []
        second.append(belongs * rates[t])
        if j < 7:
            second.append(jnp.zeros(((7 - j) * count, tokens), F32))
        second.append(jnp.where(ones, 1.0, 0.0))
        second.append(jnp.zeros((head - 8 * count - 8, tokens), F32))
        second = jnp.concatenate(second, axis=0).astype(BF16)
        projected = dot(left, jnp.concatenate(first + [second], axis=0))
        queries = unit(projected[:head], gains[0]).astype(BF16)
        keys = unit(projected[head : 2 * head], gains[1]).T.astype(BF16)
        values = projected[2 * head :].astype(BF16)
        scores = dot(keys, queries) + bias[...]
        raised = jnp.exp2(scores - jnp.max(scores, axis=0, keepdims=True))
        mass = jnp.sum(raised, axis=0, keepdims=True)
        attended = (dot(values, raised.astype(BF16)) * (1.0 / mass)).astype(BF16)
        total = total + dot(outward[t], attended)
    copies = fetch([(staged, out)], sems)
    copies[0].wait()


def residual_kernel(
    here, steps, arrived, terms, w_in, w_final, member, sums,
    out,
    terms_v, w_in_v, w_final_v, sems,
):
    del sums
    times = terms_v.shape[0]
    chans, wide = w_in_v.shape
    count = member.shape[0]
    copies = fetch([(terms, terms_v), (w_in, w_in_v), (w_final, w_final_v)], sems)
    documents = gather_documents(arrived, chans, count, wide // times)
    mixed = jnp.zeros(out.shape, F32)
    weights, whole = [], 0.0
    for t in range(times):
        weights.append(jnp.where(t < here[0], steps[t], 0.0))
        mixed = mixed + weights[t] * arrived[t, :chans, :].astype(F32)
        whole = whole + weights[t]
    copies[0].wait()
    embedded = jnp.zeros((1, wide), F32)
    for t in range(times):
        embedded = embedded + weights[t] * terms_v[t, 0:1, :]
    rows = embedded + whole * documents
    high = rows.astype(BF16)
    middle, low = two_parts(rows - high.astype(F32))
    copies[1].wait()
    copies[2].wait()
    final = w_final_v[...]
    narrow = dot(final, high, NT) + dot(final, middle, NT) + dot(final, low, NT)
    direct = dot(final, w_in_v[...], NT)
    highest = lax.Precision.HIGHEST
    near = dot(direct, mixed, NN, highest) + dot(narrow, member[...], NN, highest)
    out[...] = near + arrived[0, :chans, :].astype(F32)


def fold_inward(w_in, terms, latents, pack_docs, w_qkv, documents):
    times, (chans, wide), head = terms.shape[0], w_in.shape, w_qkv.shape[2]
    return pl.pallas_call(
        inward_kernel,
        out_shape=(
            jax.ShapeDtypeStruct((times // 2, 3 * head, 2 * chans), BF16),
            jax.ShapeDtypeStruct((2 * chans, wide), BF16),
            jax.ShapeDtypeStruct((2 * pack_docs.shape[1], documents), BF16),
            jax.ShapeDtypeStruct(latents.shape[1:], BF16),
            jax.ShapeDtypeStruct(latents.shape[1:], F32),
        ),
        in_specs=[HBM, HBM, HBM, HBM, VMEM],
        out_specs=(VMEM,) * 5,
        scratch_shapes=[
            pltpu.VMEM(w_in.shape, BF16),
            pltpu.VMEM(terms.shape, F32),
            pltpu.VMEM(latents.shape, F32),
            pltpu.VMEM(pack_docs.shape, jnp.int32),
            pltpu.VMEM(w_in.shape, F32),
            pltpu.VMEM((2, 4 * chans, wide), BF16),
            pltpu.SemaphoreType.DMA((4,)),
        ],
        compiler_params=PARAMS,
        name="fold_inward",
    )(w_in, terms, latents, pack_docs, w_qkv)


def select(table, pick, lowered, size):
    rows = lowered.shape[0] + pick.shape[0]
    block = (rows, lowered.shape[1])
    return pl.pallas_call(
        select_kernel,
        out_shape=jax.ShapeDtypeStruct((size,) + block, BF16),
        in_specs=[VMEM] * 3,
        out_specs=HBM,
        scratch_shapes=[pltpu.VMEM(block, BF16), pltpu.SemaphoreType.DMA((size,))],
        compiler_params=PARAMS,
        name="select",
    )(table, pick, lowered)


def fold_outward(
    steps, terms, w_final, w_proj, query_gain, key_gain, segments, sent, pieces, w_qkv, count
):
    times, wide = terms.shape[0], terms.shape[2]
    chans, head, tokens = w_final.shape[0], w_proj.shape[0], segments.shape[1]
    return pl.pallas_call(
        outward_kernel,
        out_shape=(
            jax.ShapeDtypeStruct((times, chans, head), BF16),
            jax.ShapeDtypeStruct((times, 3 * head), F32),
            jax.ShapeDtypeStruct((2 * chans, chans), BF16),
            jax.ShapeDtypeStruct((times, chans), F32),
            jax.ShapeDtypeStruct((times, wide), F32),
            jax.ShapeDtypeStruct((times, wide), F32),
            jax.ShapeDtypeStruct((2, head, head), F32),
            jax.ShapeDtypeStruct((tokens, tokens), F32),
            jax.ShapeDtypeStruct((count, tokens), F32),
        ),
        in_specs=[SMEM] + [HBM] * 7 + [VMEM] * 2,
        out_specs=(VMEM,) * 9,
        scratch_shapes=[
            pltpu.VMEM(terms.shape, F32),
            pltpu.VMEM(w_final.shape, BF16),
            pltpu.VMEM(w_proj.shape, BF16),
            pltpu.VMEM((2,) + query_gain.shape, F32),
            pltpu.VMEM(segments.shape, jnp.int32),
            pltpu.VMEM((2, 4 * chans, wide), BF16),
            pltpu.SemaphoreType.DMA((6,)),
        ],
        compiler_params=PARAMS,
        name="fold_outward",
    )(steps, terms, w_final, w_proj, query_gain, key_gain, segments, sent, pieces, w_qkv)


def run_heads(here, arrived, w_qkv, inward, outward, shifts, gram, cross, pieces, embedded, *rest):
    rows = arrived.shape[0] * (arrived.shape[1] - outward.shape[1]) // 2
    return pl.pallas_call(
        heads_kernel,
        out_shape=jax.ShapeDtypeStruct(outward.shape, BF16),
        in_specs=[SMEM] + [VMEM] * 14,
        out_specs=HBM,
        scratch_shapes=[
            pltpu.VMEM((rows, embedded.shape[1]), BF16),
            pltpu.VMEM(outward.shape, BF16),
            pltpu.SemaphoreType.DMA((1,)),
        ],
        compiler_params=PARAMS,
        name="run_heads",
    )(here, arrived, w_qkv, inward, outward, shifts, gram, cross, pieces, embedded, *rest)


def residual(here, steps, arrived, terms, w_in, w_final, member, sums):
    return pl.pallas_call(
        residual_kernel,
        out_shape=jax.ShapeDtypeStruct(sums.shape[1:], F32),
        in_specs=[SMEM] * 2 + [VMEM, HBM, HBM, HBM, VMEM, HBM],
        out_specs=VMEM,
        scratch_shapes=[
            pltpu.VMEM(terms.shape, F32),
            pltpu.VMEM(w_in.shape, BF16),
            pltpu.VMEM(w_final.shape, BF16),
            pltpu.SemaphoreType.DMA((3,)),
        ],
        compiler_params=PARAMS,
        name="residual",
    )(here, steps, arrived, terms, w_in, w_final, member, sums)


def local(
    latents,
    time_terms,
    step_sizes,
    doc_embed,
    pack_docs,
    segment_ids,
    w_in,
    w_qkv,
    query_gain,
    key_gain,
    w_proj,
    w_final,
):
    here = lax.axis_index("tm")
    place = here.astype(jnp.int32).reshape(1)
    times, owners = lax.axis_size("tm"), lax.axis_size("req")
    count, piece = doc_embed.shape
    w_heads = w_qkv[:, :, 0, :].transpose(1, 0, 2)
    w_last = w_final.T

    copies = jnp.broadcast_to(doc_embed[None], (owners, count, piece))
    table = lax.all_to_all(copies, "req", 0, 0)
    inward, pieces, pick, lowered, rest = fold_inward(
        w_in, time_terms, latents, pack_docs[None], w_heads, owners * count
    )
    sent = select(table, pick, lowered, times)
    arrived = lax.all_to_all(sent, "tm", 0, 0)
    outward, shifts, gram, cross, embedded, scales, gains, bias, member = fold_outward(
        step_sizes, time_terms, w_last, w_proj[0], query_gain, key_gain, segment_ids, sent,
        pieces, w_heads, count,
    )
    sums = run_heads(
        place, arrived, w_heads, inward, outward, shifts, gram, cross, pieces, embedded, scales,
        gains, bias, member, rest,
    )
    parts = lax.all_to_all(sums, "tm", 0, 0)
    direct = residual(place, step_sizes, arrived, time_terms, w_in, w_last, member, sums)
    before = direct + jnp.sum(parts.astype(F32), axis=0)
    return jnp.where(here == 0, latents[0], before)[None]


def solution(mesh):
    in_specs = (
        P("tm", None, "req"),
        P(),
        P(),
        P("req", "tm"),
        P("req"),
        P("req", None),
        P(),
        P(None, None, "tm", None),
        P("tm", None),
        P("tm", None),
        P("tm", None, None),
        P(),
    )
    out_specs = P("tm", None, "req")
    return jax.shard_map(local, mesh=mesh, in_specs=in_specs, out_specs=out_specs, check_vma=False)
```

```python
import jax
import jax.numpy as jnp
from jax import lax
from jax.experimental import pallas as pl
from jax.experimental.pallas import tpu as pltpu
from jax.sharding import PartitionSpec as P

EPS = 1e-06
MASKED = -1e30
LOG2E = 1.4426950408889634
BF16, F32 = jnp.bfloat16, jnp.float32
NN = (((1,), (0,)), ((), ()))
NT = (((1,), (1,)), ((), ()))
VMEM = pl.BlockSpec(memory_space=pltpu.VMEM)
SMEM = pl.BlockSpec(memory_space=pltpu.SMEM)
HBM = pl.BlockSpec(memory_space=pltpu.HBM)
PARAMS = pltpu.CompilerParams(vmem_limit_bytes=24 * 2**20)


def dot(left, right, dims=NN, precision=None):
    return lax.dot_general(left, right, dims, precision=precision, preferred_element_type=F32)


def two_parts(values):
    high = values.astype(BF16)
    return high, (values - high.astype(F32)).astype(BF16)


def stack_rows(*parts):
    return jnp.concatenate([p.astype(F32) for p in parts], axis=0).astype(BF16)


def centre(values):
    return values - jnp.mean(values, axis=-1, keepdims=True)


def pinned(*arrays):
    return tuple(pltpu.with_memory_space_constraint(a, pltpu.HBM) for a in arrays)


def fetch(pairs, sems):
    copies = [pltpu.make_async_copy(a, b, sems.at[i]) for i, (a, b) in enumerate(pairs)]
    for copy in copies:
        copy.start()
    return copies


def inward_kernel(
    w_in, terms, w_qkv, latents, pack_docs,
    inward, pieces, pick, rest, sent,
    w_in_v, terms_v, w_qkv_v, latents_v, packs_v, centred, rows, inward_v, pieces_v, pick_v, rest_v,
    lowered_v, sems, out_sems,
):
    chans, wide = w_in_v.shape
    times = terms_v.shape[0]
    head = w_qkv.shape[2]
    spans = [slice(c * head, (c + 1) * head) for c in range(3)]
    copies = fetch(
        [(w_in, w_in_v), (terms, terms_v)]
        + [(w_qkv.at[c], w_qkv_v.at[:, spans[c]]) for c in range(3)]
        + [(latents, latents_v), (pack_docs, packs_v)],
        sems,
    )
    copies[0].wait()
    centred[...] = centre(w_in_v[...].astype(F32))
    high, low = two_parts(centred[...])
    pieces_v[:chans, :] = high
    pieces_v[chans:, :] = low
    copies[5].wait()
    values = latents_v[0]
    high = values.astype(BF16)
    lowered_v[...] = high
    rest_v[...] = values - high.astype(F32)
    copies[6].wait()
    count = packs_v.shape[1]
    column = jnp.broadcast_to(packs_v[...].astype(F32), (count, count))
    eye = lax.broadcasted_iota(jnp.int32, (count, count), 0) == lax.broadcasted_iota(
        jnp.int32, (count, count), 1
    )
    column = jnp.sum(jnp.where(eye, column, 0.0), axis=1, keepdims=True)
    places = lax.broadcasted_iota(jnp.int32, (count, pick.shape[1]), 1).astype(F32)
    chosen = jnp.where(places == column, 1.0, 0.0)
    pick_v[...] = stack_rows(chosen, jnp.zeros_like(chosen))
    left = fetch(
        [(pieces_v, pieces), (rest_v, rest), (pick_v, pick)]
        + [(lowered_v, sent.at[i, pl.ds(0, chans)]) for i in range(times)],
        out_sems,
    )
    copies[1].wait()
    for step in range(times // 4):
        for j in range(4):
            scaled = centred[...] * (1.0 + terms_v[step * 4 + j, 2:3, :])
            rows[step % 2, j * chans : (j + 1) * chans, :] = scaled.astype(BF16)
        if step == 0:
            for c in range(3):
                copies[2 + c].wait()
        turned = dot(rows[step % 2], w_qkv_v[...]).T.astype(BF16)
        inward_v[2 * step] = turned[:, : 2 * chans]
        inward_v[2 * step + 1] = turned[:, 2 * chans :]
        copy = pltpu.make_async_copy(
            inward_v.at[pl.ds(2 * step, 2)],
            inward.at[pl.ds(2 * step, 2)],
            out_sems.at[3 + times + step],
        )
        copy.start()
        left.append(copy)
    for copy in left:
        copy.wait()


def select_kernel(table, pick, sent, out, pick_v, staged, sems):
    del sent
    size, rows, lanes = out.shape
    owners, count, piece = table.shape
    fetch([(pick, pick_v)], sems.at[pl.ds(size, 1)])[0].wait()
    chosen = dot(pick_v[...], table[...].reshape(owners * count, piece))[:count]
    tail = jnp.concatenate(
        [chosen[:, lanes:], jnp.zeros((count, 2 * lanes - piece), F32)], axis=1
    )
    staged[...] = stack_rows(chosen[:, :lanes], tail)
    head = rows - 2 * count
    copies = fetch([(staged, out.at[i, pl.ds(head, 2 * count)]) for i in range(size)], sems)
    for copy in copies:
        copy.wait()


def outward_kernel(
    steps, terms, w_final, w_proj, w_qkv, pieces, query_gain, key_gain, segments, sent,
    outward, shifts, gram, cross, embedded, scales, gains, bias, member,
    terms_v, w_final_v, w_proj_v, w_qkv_v, pieces_v, gains_v, segments_v, rows,
    outward_v, shifts_v, gram_v, cross_v, embedded_v, scales_v, gain_rows, bias_v, member_v,
    sems, out_sems,
):
    del sent
    times, chans, head = outward.shape
    spans = [slice(c * head, (c + 1) * head) for c in range(3)]
    copies = fetch(
        [
            (terms, terms_v), (w_final, w_final_v), (w_proj, w_proj_v), (pieces, pieces_v),
            (query_gain, gains_v.at[0]), (key_gain, gains_v.at[1]), (segments, segments_v),
        ]
        + [(w_qkv.at[c], w_qkv_v.at[:, spans[c]]) for c in range(3)],
        sems,
    )
    copies[0].wait()
    moved, means = [], []
    for t in range(times):
        moved.append(terms_v[t, 1:2, :])
        means.append(centre(terms_v[t, 0:1, :]))
        scales_v[t : t + 1, :] = 1.0 + terms_v[t, 2:3, :]
    moved, means = jnp.concatenate(moved, axis=0), jnp.concatenate(means, axis=0)
    embedded_v[...] = means
    copies[1].wait()
    copies[2].wait()
    for step in range(times // 4):
        for j in range(4):
            gated = w_final_v[...].astype(F32) * terms_v[step * 4 + j, 3:4, :]
            rows[step % 2, j * chans : (j + 1) * chans, :] = gated.astype(BF16)
        back = dot(rows[step % 2], w_proj_v[...], NT)
        for j in range(4):
            t = step * 4 + j
            outward_v[t] = (back[j * chans : (j + 1) * chans] * steps[t]).astype(BF16)
    copies[3].wait()
    both = pieces_v[...]
    square = dot(both, both, NT)
    square = square[:chans, :chans] + square[chans:, :chans] + square[:chans, chans:]
    high, low = two_parts(square)
    gram_v[:chans, :] = high
    gram_v[chans:, :] = low
    high, low = two_parts(means)
    mixed = dot(stack_rows(high, low), both, NT)
    cross_v[...] = mixed[:times, :chans] + mixed[times:, :chans] + mixed[:times, chans:]
    for copy in copies[4:]:
        copy.wait()
    high, low = two_parts(moved)
    shift = dot(stack_rows(high, low), w_qkv_v[...])
    shifts_v[...] = shift[:times] + shift[times:]
    tokens = segments_v.shape[1]
    gain_rows[0] = jnp.broadcast_to(gains_v[0] * (head**-0.5 * LOG2E), (head, head)).T
    gain_rows[1] = jnp.broadcast_to(gains_v[1], (head, head)).T
    ids = jnp.broadcast_to(segments_v[...].astype(F32), (tokens, tokens))
    bias_v[...] = jnp.where(ids == ids.T, 0.0, MASKED)
    count = member_v.shape[0]
    numbers = lax.broadcasted_iota(jnp.int32, (count, tokens), 0).astype(F32)
    member_v[...] = jnp.where(numbers == ids[:count], 1.0, 0.0)
    left = fetch(
        [
            (outward_v, outward), (shifts_v, shifts), (gram_v, gram), (cross_v, cross),
            (embedded_v, embedded), (scales_v, scales), (gain_rows, gains), (bias_v, bias),
            (member_v, member),
        ],
        out_sems,
    )
    for copy in left:
        copy.wait()


def gather_documents(arrived, chans, count, piece):
    parts = []
    for i in range(arrived.shape[0]):
        block = arrived[i, chans:, :].astype(F32)
        parts.append(block[:count])
        parts.append(block[count:, : piece - block.shape[1]])
    return jnp.concatenate(parts, axis=1)


def heads_kernel(
    here, arrived,
    embedded_h, scales_h, w_in_h, w_qkv_h, shifts_h, gram_h, cross_h, member_h, gains_h, bias_h,
    inward_h, outward_h, rest_h,
    out, kept,
    embedded, scales, w_in, w_qkv, shifts, gram, cross, member, gains, bias,
    inward, outward, rest,
    rows, staged, sems,
):
    times, chans, head = outward.shape
    count, tokens = member.shape
    wide = w_in.shape[1]
    spans = [slice(c * head, (c + 1) * head) for c in range(3)]
    copies = fetch(
        [(embedded_h, embedded), (scales_h, scales), (w_in_h, w_in)]
        + [(w_qkv_h.at[c], w_qkv.at[:, spans[c]]) for c in range(3)]
        + [
            (shifts_h, shifts), (gram_h, gram), (cross_h, cross), (member_h, member),
            (gains_h, gains), (bias_h, bias), (inward_h, inward), (outward_h, outward),
            (rest_h, rest), (arrived, kept),
        ],
        sems,
    )
    documents = centre(gather_documents(arrived, chans, count, wide // times))
    for copy in copies[:3]:
        copy.wait()
    high, low = two_parts(documents)
    near = dot(stack_rows(high, low), w_in[...], NT)
    near = near[:count] + near[count:]
    powers = []
    for t in range(0, times, 2):
        pair = []
        for j in range(2):
            row = documents + embedded[t + j : t + j + 1, :]
            powers.append(jnp.sum(row * row, axis=-1, keepdims=True))
            pair.append(row * scales[t + j : t + j + 1, :])
        rows[t * count : (t + 2) * count, :] = jnp.concatenate(pair, axis=0).astype(BF16)
    for copy in copies[3:7]:
        copy.wait()
    base = dot(rows[...], w_qkv[...])
    turned = []
    for half in range(2):
        span = slice(half * 8 * count, (half + 1) * 8 * count)
        block = [base[span], shifts[half * 8 : (half + 1) * 8, :]]
        left = head - 8 * count - 8
        block.append(jnp.zeros((left, 3 * head), F32))
        turned.append(jnp.concatenate(block, axis=0).T.astype(BF16))

    for copy in copies[7:-1]:
        copy.wait()
    belongs = member[...]
    scaled_low, rates = [], []
    for t in range(times):
        mixed = 2.0 * (near + cross[t : t + 1, :])
        high, low = two_parts(mixed)
        left = jnp.concatenate([gram[...], stack_rows(high, low)], axis=0)
        values = arrived[t, :chans, :]
        whole = dot(left, values)
        both = whole[:chans] + whole[chans : 2 * chans]
        values = values.astype(F32)
        other = whole[2 * chans : 2 * chans + count] + whole[2 * chans + count :]
        spread = jnp.sum(both * values, axis=0, keepdims=True) + jnp.sum(
            belongs * (other + powers[t]), axis=0, keepdims=True
        )
        rate = lax.rsqrt(spread / wide + EPS)
        rates.append(rate)
        scaled_low.append((values * rate).astype(BF16))

    def unit(values, gain):
        power = jnp.mean(values * values, axis=0, keepdims=True)
        return values * lax.rsqrt(power + EPS) * gain

    total = jnp.where(here[0] == 0, rest[...], 0.0)
    empty = jnp.zeros((chans, tokens), BF16)
    for t in range(times):
        staged[t] = total.astype(BF16)
        half, j = divmod(t, 8)
        left = jnp.concatenate([inward[t // 2], turned[half]], axis=1)
        first = [scaled_low[t], empty] if t % 2 == 0 else [empty, scaled_low[t]]
        ones = lax.broadcasted_iota(jnp.int32, (8, tokens), 0) == j
        second = [jnp.zeros((j * count, tokens), F32)] if j else []
        second.append(belongs * rates[t])
        if j < 7:
            second.append(jnp.zeros(((7 - j) * count, tokens), F32))
        second.append(jnp.where(ones, 1.0, 0.0))
        second.append(jnp.zeros((head - 8 * count - 8, tokens), F32))
        second = jnp.concatenate(second, axis=0).astype(BF16)
        projected = dot(left, jnp.concatenate(first + [second], axis=0))
        queries = unit(projected[:head], gains[0]).astype(BF16)
        keys = unit(projected[head : 2 * head], gains[1]).T.astype(BF16)
        values = projected[2 * head :].astype(BF16)
        scores = dot(keys, queries) + bias[...]
        raised = jnp.exp2(scores - jnp.max(scores, axis=0, keepdims=True))
        mass = jnp.sum(raised, axis=0, keepdims=True)
        attended = (dot(values, raised.astype(BF16)) * (1.0 / mass)).astype(BF16)
        total = total + dot(outward[t], attended)
    last = pltpu.make_async_copy(staged, out, sems.at[len(copies)])
    last.start()
    copies[-1].wait()
    last.wait()


def residual_kernel(
    here, steps, kept, terms, w_in, w_final, member_h,
    out,
    arrived, terms_v, w_in_v, w_final_v, member, sems,
):
    times = terms_v.shape[0]
    chans, wide = w_in_v.shape
    count = member.shape[0]
    copies = fetch(
        [
            (terms, terms_v), (w_in, w_in_v), (w_final, w_final_v), (kept, arrived),
            (member_h, member),
        ],
        sems,
    )
    copies[3].wait()
    copies[4].wait()
    documents = gather_documents(arrived, chans, count, wide // times)
    mixed = jnp.zeros(out.shape, F32)
    weights, whole = [], 0.0
    for t in range(times):
        weights.append(jnp.where(t < here[0], steps[t], 0.0))
        mixed = mixed + weights[t] * arrived[t, :chans, :].astype(F32)
        whole = whole + weights[t]
    copies[0].wait()
    embedded = jnp.zeros((1, wide), F32)
    for t in range(times):
        embedded = embedded + weights[t] * terms_v[t, 0:1, :]
    rows = embedded + whole * documents
    high = rows.astype(BF16)
    middle, low = two_parts(rows - high.astype(F32))
    copies[1].wait()
    copies[2].wait()
    final = w_final_v[...]
    narrow = dot(final, high, NT) + dot(final, middle, NT) + dot(final, low, NT)
    direct = dot(final, w_in_v[...], NT)
    highest = lax.Precision.HIGHEST
    near = dot(direct, mixed, NN, highest) + dot(narrow, member[...], NN, highest)
    out[...] = near + arrived[0, :chans, :].astype(F32)


def fold_inward(w_in, terms, w_qkv, latents, pack_docs, documents):
    times, (chans, wide), head = terms.shape[0], w_in.shape, w_qkv.shape[2]
    block, count = latents.shape[1:], pack_docs.shape[1]
    shapes = [
        ((times // 2, 3 * head, 2 * chans), BF16),
        ((2 * chans, wide), BF16),
        ((2 * count, documents), BF16),
        (block, F32),
    ]
    return pl.pallas_call(
        inward_kernel,
        out_shape=tuple(pltpu.HBM(*s) for s in shapes)
        + (pltpu.HBM((times, chans + 2 * count, block[1]), BF16),),
        in_specs=[HBM] * 5,
        out_specs=(HBM,) * 5,
        scratch_shapes=[
            pltpu.VMEM(w_in.shape, BF16),
            pltpu.VMEM(terms.shape, F32),
            pltpu.VMEM((wide, 3 * head), BF16),
            pltpu.VMEM(latents.shape, F32),
            pltpu.VMEM(pack_docs.shape, jnp.int32),
            pltpu.VMEM(w_in.shape, F32),
            pltpu.VMEM((2, 4 * chans, wide), BF16),
        ]
        + [pltpu.VMEM(*s) for s in shapes]
        + [
            pltpu.VMEM(block, BF16),
            pltpu.SemaphoreType.DMA((7,)),
            pltpu.SemaphoreType.DMA((3 + times + times // 4,)),
        ],
        compiler_params=PARAMS,
        name="fold_inward",
    )(*pinned(w_in, terms, w_qkv, latents, pack_docs))


def select(table, pick, sent):
    size = sent.shape[0]
    return pl.pallas_call(
        select_kernel,
        out_shape=pltpu.HBM(sent.shape, BF16),
        in_specs=[VMEM, HBM, HBM],
        out_specs=HBM,
        scratch_shapes=[
            pltpu.VMEM(pick.shape, BF16),
            pltpu.VMEM((pick.shape[0], sent.shape[2]), BF16),
            pltpu.SemaphoreType.DMA((size + 1,)),
        ],
        input_output_aliases={2: 0},
        compiler_params=PARAMS,
        name="select",
    )(table, *pinned(pick, sent))


def fold_outward(
    steps, terms, w_final, w_proj, w_qkv, pieces, query_gain, key_gain, segments, sent, count
):
    times, wide = terms.shape[0], terms.shape[2]
    chans, head, tokens = w_final.shape[0], w_proj.shape[0], segments.shape[1]
    shapes = [
        ((times, chans, head), BF16),
        ((times, 3 * head), F32),
        ((2 * chans, chans), BF16),
        ((times, chans), F32),
        ((times, wide), F32),
        ((times, wide), F32),
        ((2, head, head), F32),
        ((tokens, tokens), F32),
        ((count, tokens), F32),
    ]
    return pl.pallas_call(
        outward_kernel,
        out_shape=tuple(pltpu.HBM(*s) for s in shapes),
        in_specs=[SMEM] + [HBM] * 9,
        out_specs=(HBM,) * 9,
        scratch_shapes=[
            pltpu.VMEM(terms.shape, F32),
            pltpu.VMEM(w_final.shape, BF16),
            pltpu.VMEM(w_proj.shape, BF16),
            pltpu.VMEM((wide, 3 * head), BF16),
            pltpu.VMEM(pieces.shape, BF16),
            pltpu.VMEM((2,) + query_gain.shape, F32),
            pltpu.VMEM(segments.shape, jnp.int32),
            pltpu.VMEM((2, 4 * chans, wide), BF16),
        ]
        + [pltpu.VMEM(*s) for s in shapes]
        + [pltpu.SemaphoreType.DMA((10,)), pltpu.SemaphoreType.DMA((9,))],
        compiler_params=PARAMS,
        name="fold_outward",
    )(
        steps,
        *pinned(terms, w_final, w_proj, w_qkv, pieces, query_gain, key_gain, segments, sent),
    )


def run_heads(here, arrived, embedded, scales, w_in, w_qkv, *rest):
    outward = rest[-2]
    head = w_qkv.shape[2]
    rows = arrived.shape[0] * (arrived.shape[1] - outward.shape[1]) // 2
    held = [
        pltpu.VMEM(a.shape, a.dtype) for a in (embedded, scales, w_in)
    ] + [pltpu.VMEM((w_qkv.shape[1], 3 * head), BF16)]
    held += [pltpu.VMEM(a.shape, a.dtype) for a in rest]
    return pl.pallas_call(
        heads_kernel,
        out_shape=(pltpu.HBM(outward.shape, BF16), pltpu.HBM(arrived.shape, BF16)),
        in_specs=[SMEM, VMEM] + [HBM] * 13,
        out_specs=(HBM, HBM),
        scratch_shapes=held
        + [
            pltpu.VMEM((rows, embedded.shape[1]), BF16),
            pltpu.VMEM(outward.shape, BF16),
            pltpu.SemaphoreType.DMA((17,)),
        ],
        compiler_params=PARAMS,
        name="run_heads",
    )(here, arrived, *pinned(embedded, scales, w_in, w_qkv, *rest))


def residual(here, steps, kept, terms, w_in, w_final, member):
    return pl.pallas_call(
        residual_kernel,
        out_shape=jax.ShapeDtypeStruct((w_in.shape[0], kept.shape[2]), F32),
        in_specs=[SMEM] * 2 + [HBM] * 5,
        out_specs=VMEM,
        scratch_shapes=[
            pltpu.VMEM(kept.shape, BF16),
            pltpu.VMEM(terms.shape, F32),
            pltpu.VMEM(w_in.shape, BF16),
            pltpu.VMEM(w_final.shape, BF16),
            pltpu.VMEM(member.shape, F32),
            pltpu.SemaphoreType.DMA((5,)),
        ],
        compiler_params=PARAMS,
        name="residual",
    )(here, steps, *pinned(kept, terms, w_in, w_final, member))


def local(
    latents,
    time_terms,
    step_sizes,
    doc_embed,
    pack_docs,
    segment_ids,
    w_in,
    w_qkv,
    query_gain,
    key_gain,
    w_proj,
    w_final,
):
    here = lax.axis_index("tm")
    place = here.astype(jnp.int32).reshape(1)
    times, owners = lax.axis_size("tm"), lax.axis_size("req")
    count, piece = doc_embed.shape
    w_heads = w_qkv[:, :, 0, :].transpose(1, 0, 2)
    w_last = w_final.T

    copies = jnp.broadcast_to(doc_embed[None], (owners, count, piece))
    table = lax.all_to_all(copies, "req", 0, 0)
    inward, pieces, pick, rest, sent = fold_inward(
        w_in, time_terms, w_heads, latents, pack_docs[None], owners * count
    )
    sent = select(table, pick, sent)
    arrived = lax.all_to_all(sent, "tm", 0, 0)
    outward, shifts, gram, cross, embedded, scales, gains, bias, member = fold_outward(
        step_sizes, time_terms, w_last, w_proj[0], w_heads, pieces, query_gain, key_gain,
        segment_ids, sent, count,
    )
    sums, kept = run_heads(
        place, arrived, embedded, scales, w_in, w_heads, shifts, gram, cross, member, gains, bias,
        inward, outward, rest,
    )
    parts = lax.all_to_all(sums, "tm", 0, 0)
    direct = residual(place, step_sizes, kept, time_terms, w_in, w_last, member)
    before = direct + jnp.sum(parts.astype(F32), axis=0)
    return jnp.where(here == 0, latents[0], before)[None]


def solution(mesh):
    in_specs = (
        P("tm", None, "req"),
        P(),
        P(),
        P("req", "tm"),
        P("req"),
        P("req", None),
        P(),
        P(None, None, "tm", None),
        P("tm", None),
        P("tm", None),
        P("tm", None, None),
        P(),
    )
    out_specs = P("tm", None, "req")
    return jax.shard_map(local, mesh=mesh, in_specs=in_specs, out_specs=out_specs, check_vma=False)
```

```python
import jax
import jax.numpy as jnp
from jax import lax
from jax.experimental import pallas as pl
from jax.experimental.pallas import tpu as pltpu
from jax.sharding import PartitionSpec as P

EPS = 1e-06
MASKED = -1e30
LOG2E = 1.4426950408889634
BF16, F32 = jnp.bfloat16, jnp.float32
NN = (((1,), (0,)), ((), ()))
NT = (((1,), (1,)), ((), ()))
VMEM = pl.BlockSpec(memory_space=pltpu.VMEM)
SMEM = pl.BlockSpec(memory_space=pltpu.SMEM)
HBM = pl.BlockSpec(memory_space=pltpu.HBM)
PARAMS = pltpu.CompilerParams(vmem_limit_bytes=24 * 2**20)


def dot(left, right, dims=NN, precision=None):
    return lax.dot_general(left, right, dims, precision=precision, preferred_element_type=F32)


def two_parts(values):
    high = values.astype(BF16)
    return high, (values - high.astype(F32)).astype(BF16)


def stack_rows(*parts):
    return jnp.concatenate([p.astype(F32) for p in parts], axis=0).astype(BF16)


def centre(values):
    return values - jnp.mean(values, axis=-1, keepdims=True)


def pinned(*arrays):
    return tuple(pltpu.with_memory_space_constraint(a, pltpu.HBM) for a in arrays)


def fetch(pairs, sems):
    copies = [pltpu.make_async_copy(a, b, sems.at[i]) for i, (a, b) in enumerate(pairs)]
    for copy in copies:
        copy.start()
    return copies


def inward_kernel(
    w_in, terms, w_qkv, latents, pack_docs,
    inward, pieces, pick, rest, sent,
    w_in_v, terms_v, w_qkv_v, latents_v, packs_v, centred, rows, inward_v, pieces_v, pick_v, rest_v,
    lowered_v, sems, out_sems,
):
    chans, wide = w_in_v.shape
    times = terms_v.shape[0]
    head = w_qkv.shape[2]
    spans = [slice(c * head, (c + 1) * head) for c in range(3)]
    copies = fetch(
        [(w_in, w_in_v), (terms, terms_v)]
        + [(w_qkv.at[c], w_qkv_v.at[:, spans[c]]) for c in range(3)]
        + [(latents, latents_v), (pack_docs, packs_v)],
        sems,
    )
    copies[0].wait()
    centred[...] = centre(w_in_v[...].astype(F32))
    high, low = two_parts(centred[...])
    pieces_v[:chans, :] = high
    pieces_v[chans:, :] = low
    copies[5].wait()
    values = latents_v[0]
    high = values.astype(BF16)
    lowered_v[...] = high
    rest_v[...] = values - high.astype(F32)
    copies[6].wait()
    count = packs_v.shape[1]
    column = jnp.broadcast_to(packs_v[...].astype(F32), (count, count))
    eye = lax.broadcasted_iota(jnp.int32, (count, count), 0) == lax.broadcasted_iota(
        jnp.int32, (count, count), 1
    )
    column = jnp.sum(jnp.where(eye, column, 0.0), axis=1, keepdims=True)
    places = lax.broadcasted_iota(jnp.int32, (count, pick.shape[1]), 1).astype(F32)
    chosen = jnp.where(places == column, 1.0, 0.0)
    pick_v[...] = stack_rows(chosen, jnp.zeros_like(chosen))
    left = fetch(
        [(pieces_v, pieces), (rest_v, rest), (pick_v, pick)]
        + [(lowered_v, sent.at[i, pl.ds(0, chans)]) for i in range(times)],
        out_sems,
    )
    copies[1].wait()
    for step in range(times // 4):
        for j in range(4):
            scaled = centred[...] * (1.0 + terms_v[step * 4 + j, 2:3, :])
            rows[step % 2, j * chans : (j + 1) * chans, :] = scaled.astype(BF16)
        if step == 0:
            for c in range(3):
                copies[2 + c].wait()
        turned = dot(rows[step % 2], w_qkv_v[...]).T.astype(BF16)
        inward_v[2 * step] = turned[:, : 2 * chans]
        inward_v[2 * step + 1] = turned[:, 2 * chans :]
        copy = pltpu.make_async_copy(
            inward_v.at[pl.ds(2 * step, 2)],
            inward.at[pl.ds(2 * step, 2)],
            out_sems.at[3 + times + step],
        )
        copy.start()
        left.append(copy)
    for copy in left:
        copy.wait()


def select_kernel(table, pick, sent, out, pick_v, staged, sems):
    del sent
    size, rows, lanes = out.shape
    owners, count, piece = table.shape
    fetch([(pick, pick_v)], sems.at[pl.ds(size, 1)])[0].wait()
    chosen = dot(pick_v[...], table[...].reshape(owners * count, piece))[:count]
    tail = jnp.concatenate(
        [chosen[:, lanes:], jnp.zeros((count, 2 * lanes - piece), F32)], axis=1
    )
    staged[...] = stack_rows(chosen[:, :lanes], tail)
    head = rows - 2 * count
    copies = fetch([(staged, out.at[i, pl.ds(head, 2 * count)]) for i in range(size)], sems)
    for copy in copies:
        copy.wait()


def outward_kernel(
    here, steps, terms, w_final, w_proj, w_in, w_qkv, pieces, query_gain, key_gain, segments, sent,
    outward, shifts, gram, cross, embedded, scales, gains, bias, member, direct, earlier,
    terms_v, w_final_v, w_proj_v, w_in_v, w_qkv_v, pieces_v, gains_v, segments_v, rows,
    outward_v, shifts_v, gram_v, cross_v, embedded_v, scales_v, gain_rows, bias_v, member_v,
    direct_v, earlier_v,
    sems, out_sems,
):
    del sent
    times, chans, head = outward.shape
    spans = [slice(c * head, (c + 1) * head) for c in range(3)]
    copies = fetch(
        [
            (terms, terms_v), (w_final, w_final_v), (w_proj, w_proj_v), (pieces, pieces_v),
            (query_gain, gains_v.at[0]), (key_gain, gains_v.at[1]), (segments, segments_v),
            (w_in, w_in_v),
        ]
        + [(w_qkv.at[c], w_qkv_v.at[:, spans[c]]) for c in range(3)],
        sems,
    )
    copies[0].wait()
    moved, means = [], []
    for t in range(times):
        moved.append(terms_v[t, 1:2, :])
        means.append(centre(terms_v[t, 0:1, :]))
        scales_v[t : t + 1, :] = 1.0 + terms_v[t, 2:3, :]
    moved, means = jnp.concatenate(moved, axis=0), jnp.concatenate(means, axis=0)
    embedded_v[...] = means
    copies[1].wait()
    copies[2].wait()
    for step in range(times // 4):
        for j in range(4):
            gated = w_final_v[...].astype(F32) * terms_v[step * 4 + j, 3:4, :]
            rows[step % 2, j * chans : (j + 1) * chans, :] = gated.astype(BF16)
        back = dot(rows[step % 2], w_proj_v[...], NT)
        for j in range(4):
            t = step * 4 + j
            outward_v[t] = (back[j * chans : (j + 1) * chans] * steps[t]).astype(BF16)
    copies[3].wait()
    both = pieces_v[...]
    square = dot(both, both, NT)
    square = square[:chans, :chans] + square[chans:, :chans] + square[:chans, chans:]
    high, low = two_parts(square)
    gram_v[:chans, :] = high
    gram_v[chans:, :] = low
    high, low = two_parts(means)
    mixed = dot(stack_rows(high, low), both, NT)
    cross_v[...] = mixed[:times, :chans] + mixed[times:, :chans] + mixed[:times, chans:]
    for copy in copies[4:]:
        copy.wait()
    high, low = two_parts(moved)
    shift = dot(stack_rows(high, low), w_qkv_v[...])
    shifts_v[...] = shift[:times] + shift[times:]
    final = w_final_v[...]
    direct_v[...] = dot(final, w_in_v[...], NT)
    past = jnp.zeros((1, terms_v.shape[2]), F32)
    for t in range(times):
        past = past + jnp.where(t < here[0], steps[t], 0.0) * terms_v[t, 0:1, :]
    high = past.astype(BF16)
    middle, low = two_parts(past - high.astype(F32))
    parts = stack_rows(high, middle, low, jnp.zeros((5, terms_v.shape[2]), F32))
    earlier_v[...] = jnp.broadcast_to(
        jnp.sum(dot(final, parts, NT), axis=-1, keepdims=True), earlier_v.shape
    )
    tokens = segments_v.shape[1]
    gain_rows[0] = jnp.broadcast_to(gains_v[0] * (head**-0.5 * LOG2E), (head, head)).T
    gain_rows[1] = jnp.broadcast_to(gains_v[1], (head, head)).T
    ids = jnp.broadcast_to(segments_v[...].astype(F32), (tokens, tokens))
    bias_v[...] = jnp.where(ids == ids.T, 0.0, MASKED)
    count = member_v.shape[0]
    numbers = lax.broadcasted_iota(jnp.int32, (count, tokens), 0).astype(F32)
    member_v[...] = jnp.where(numbers == ids[:count], 1.0, 0.0)
    left = fetch(
        [
            (outward_v, outward), (shifts_v, shifts), (gram_v, gram), (cross_v, cross),
            (embedded_v, embedded), (scales_v, scales), (gain_rows, gains), (bias_v, bias),
            (member_v, member), (direct_v, direct), (earlier_v, earlier),
        ],
        out_sems,
    )
    for copy in left:
        copy.wait()


def gather_documents(arrived, chans, count, piece):
    parts = []
    for i in range(arrived.shape[0]):
        block = arrived[i, chans:, :].astype(F32)
        parts.append(block[:count])
        parts.append(block[count:, : piece - block.shape[1]])
    return jnp.concatenate(parts, axis=1)


def heads_kernel(
    here, steps, arrived,
    embedded_h, scales_h, w_in_h, w_final_h, w_qkv_h, shifts_h, gram_h, cross_h, member_h, gains_h,
    bias_h, direct_h, earlier_h, inward_h, outward_h, rest_h,
    out, residual,
    embedded, scales, w_in, w_final, w_qkv, shifts, gram, cross, member, gains,
    bias, direct, earlier, inward, outward, rest,
    rows, residual_v, sems,
):
    times, chans, head = outward.shape
    count, tokens = member.shape
    wide = w_in.shape[1]
    spans = [slice(c * head, (c + 1) * head) for c in range(3)]
    copies = fetch(
        [(embedded_h, embedded), (scales_h, scales), (w_in_h, w_in), (w_final_h, w_final)]
        + [(w_qkv_h.at[c], w_qkv.at[:, spans[c]]) for c in range(3)]
        + [
            (shifts_h, shifts), (gram_h, gram), (cross_h, cross), (member_h, member),
            (gains_h, gains), (bias_h, bias), (direct_h, direct), (earlier_h, earlier),
            (inward_h, inward), (outward_h, outward), (rest_h, rest),
        ],
        sems,
    )
    documents = gather_documents(arrived, chans, count, wide // times)
    exact = stack_rows(documents, jnp.zeros_like(documents))
    documents = centre(documents)
    for copy in copies[:4]:
        copy.wait()
    narrow = dot(w_final[...], exact, NT)[:, :count]
    high, low = two_parts(documents)
    near = dot(stack_rows(high, low), w_in[...], NT)
    near = near[:count] + near[count:]
    powers = []
    for t in range(0, times, 2):
        pair = []
        for j in range(2):
            row = documents + embedded[t + j : t + j + 1, :]
            powers.append(jnp.sum(row * row, axis=-1, keepdims=True))
            pair.append(row * scales[t + j : t + j + 1, :])
        rows[t * count : (t + 2) * count, :] = jnp.concatenate(pair, axis=0).astype(BF16)
    for copy in copies[4:8]:
        copy.wait()
    base = dot(rows[...], w_qkv[...])
    turned = []
    for half in range(2):
        span = slice(half * 8 * count, (half + 1) * 8 * count)
        block = [base[span], shifts[half * 8 : (half + 1) * 8, :]]
        left = head - 8 * count - 8
        block.append(jnp.zeros((left, 3 * head), F32))
        turned.append(jnp.concatenate(block, axis=0).T.astype(BF16))

    for copy in copies[8:]:
        copy.wait()
    belongs = member[...]
    past, whole = jnp.zeros((chans, tokens), F32), 0.0
    for t in range(times):
        weight = jnp.where(t < here[0], steps[t], 0.0)
        past = past + weight * arrived[t, :chans, :].astype(F32)
        whole = whole + weight
    highest = lax.Precision.HIGHEST
    near_docs = dot(whole * narrow + earlier[...], belongs, NN, highest)
    residual_v[...] = (
        dot(direct[...], past, NN, highest) + near_docs + arrived[0, :chans, :].astype(F32)
    )
    last = pltpu.make_async_copy(residual_v, residual, sems.at[len(copies)])
    last.start()
    scaled_low, rates = [], []
    for t in range(times):
        mixed = 2.0 * (near + cross[t : t + 1, :])
        high, low = two_parts(mixed)
        left = jnp.concatenate([gram[...], stack_rows(high, low)], axis=0)
        values = arrived[t, :chans, :]
        whole = dot(left, values)
        both = whole[:chans] + whole[chans : 2 * chans]
        values = values.astype(F32)
        other = whole[2 * chans : 2 * chans + count] + whole[2 * chans + count :]
        spread = jnp.sum(both * values, axis=0, keepdims=True) + jnp.sum(
            belongs * (other + powers[t]), axis=0, keepdims=True
        )
        rate = lax.rsqrt(spread / wide + EPS)
        rates.append(rate)
        scaled_low.append((values * rate).astype(BF16))

    def unit(values, gain):
        power = jnp.mean(values * values, axis=0, keepdims=True)
        return values * lax.rsqrt(power + EPS) * gain

    total = jnp.where(here[0] == 0, rest[...], 0.0)
    empty = jnp.zeros((chans, tokens), BF16)
    for t in range(times):
        out[t] = total.astype(BF16)
        half, j = divmod(t, 8)
        left = jnp.concatenate([inward[t // 2], turned[half]], axis=1)
        first = [scaled_low[t], empty] if t % 2 == 0 else [empty, scaled_low[t]]
        ones = lax.broadcasted_iota(jnp.int32, (8, tokens), 0) == j
        second = [jnp.zeros((j * count, tokens), F32)] if j else []
        second.append(belongs * rates[t])
        if j < 7:
            second.append(jnp.zeros(((7 - j) * count, tokens), F32))
        second.append(jnp.where(ones, 1.0, 0.0))
        second.append(jnp.zeros((head - 8 * count - 8, tokens), F32))
        second = jnp.concatenate(second, axis=0).astype(BF16)
        projected = dot(left, jnp.concatenate(first + [second], axis=0))
        queries = unit(projected[:head], gains[0]).astype(BF16)
        keys = unit(projected[head : 2 * head], gains[1]).T.astype(BF16)
        values = projected[2 * head :].astype(BF16)
        scores = dot(keys, queries) + bias[...]
        raised = jnp.exp2(scores - jnp.max(scores, axis=0, keepdims=True))
        mass = jnp.sum(raised, axis=0, keepdims=True)
        attended = (dot(values, raised.astype(BF16)) * (1.0 / mass)).astype(BF16)
        total = total + dot(outward[t], attended)
    last.wait()


def fold_inward(w_in, terms, w_qkv, latents, pack_docs, documents):
    times, (chans, wide), head = terms.shape[0], w_in.shape, w_qkv.shape[2]
    block, count = latents.shape[1:], pack_docs.shape[1]
    shapes = [
        ((times // 2, 3 * head, 2 * chans), BF16),
        ((2 * chans, wide), BF16),
        ((2 * count, documents), BF16),
        (block, F32),
    ]
    return pl.pallas_call(
        inward_kernel,
        out_shape=tuple(pltpu.HBM(*s) for s in shapes)
        + (pltpu.HBM((times, chans + 2 * count, block[1]), BF16),),
        in_specs=[HBM] * 5,
        out_specs=(HBM,) * 5,
        scratch_shapes=[
            pltpu.VMEM(w_in.shape, BF16),
            pltpu.VMEM(terms.shape, F32),
            pltpu.VMEM((wide, 3 * head), BF16),
            pltpu.VMEM(latents.shape, F32),
            pltpu.VMEM(pack_docs.shape, jnp.int32),
            pltpu.VMEM(w_in.shape, F32),
            pltpu.VMEM((2, 4 * chans, wide), BF16),
        ]
        + [pltpu.VMEM(*s) for s in shapes]
        + [
            pltpu.VMEM(block, BF16),
            pltpu.SemaphoreType.DMA((7,)),
            pltpu.SemaphoreType.DMA((3 + times + times // 4,)),
        ],
        compiler_params=PARAMS,
        name="fold_inward",
    )(*pinned(w_in, terms, w_qkv, latents, pack_docs))


def select(table, pick, sent):
    size = sent.shape[0]
    return pl.pallas_call(
        select_kernel,
        out_shape=pltpu.HBM(sent.shape, BF16),
        in_specs=[VMEM, HBM, HBM],
        out_specs=HBM,
        scratch_shapes=[
            pltpu.VMEM(pick.shape, BF16),
            pltpu.VMEM((pick.shape[0], sent.shape[2]), BF16),
            pltpu.SemaphoreType.DMA((size + 1,)),
        ],
        input_output_aliases={2: 0},
        compiler_params=PARAMS,
        name="select",
    )(table, *pinned(pick, sent))


def fold_outward(
    here, steps, terms, w_final, w_proj, w_in, w_qkv, pieces, query_gain, key_gain, segments, sent,
    count,
):
    times, wide = terms.shape[0], terms.shape[2]
    chans, head, tokens = w_final.shape[0], w_proj.shape[0], segments.shape[1]
    shapes = [
        ((times, chans, head), BF16),
        ((times, 3 * head), F32),
        ((2 * chans, chans), BF16),
        ((times, chans), F32),
        ((times, wide), F32),
        ((times, wide), F32),
        ((2, head, head), F32),
        ((tokens, tokens), F32),
        ((count, tokens), F32),
        ((chans, chans), F32),
        ((chans, count), F32),
    ]
    return pl.pallas_call(
        outward_kernel,
        out_shape=tuple(pltpu.HBM(*s) for s in shapes),
        in_specs=[SMEM] * 2 + [HBM] * 10,
        out_specs=(HBM,) * 11,
        scratch_shapes=[
            pltpu.VMEM(terms.shape, F32),
            pltpu.VMEM(w_final.shape, BF16),
            pltpu.VMEM(w_proj.shape, BF16),
            pltpu.VMEM(w_in.shape, BF16),
            pltpu.VMEM((wide, 3 * head), BF16),
            pltpu.VMEM(pieces.shape, BF16),
            pltpu.VMEM((2,) + query_gain.shape, F32),
            pltpu.VMEM(segments.shape, jnp.int32),
            pltpu.VMEM((2, 4 * chans, wide), BF16),
        ]
        + [pltpu.VMEM(*s) for s in shapes]
        + [pltpu.SemaphoreType.DMA((11,)), pltpu.SemaphoreType.DMA((11,))],
        compiler_params=PARAMS,
        name="fold_outward",
    )(
        here,
        steps,
        *pinned(terms, w_final, w_proj, w_in, w_qkv, pieces, query_gain, key_gain, segments, sent),
    )


def run_heads(here, steps, arrived, embedded, scales, w_in, w_final, w_qkv, *rest):
    outward = rest[-2]
    wide, head = w_qkv.shape[1:]
    rows = arrived.shape[0] * (arrived.shape[1] - outward.shape[1]) // 2
    held = [pltpu.VMEM(a.shape, a.dtype) for a in (embedded, scales, w_in, w_final)]
    held += [pltpu.VMEM((wide, 3 * head), BF16)]
    held += [pltpu.VMEM(a.shape, a.dtype) for a in rest]
    block = rest[-1].shape
    return pl.pallas_call(
        heads_kernel,
        out_shape=(jax.ShapeDtypeStruct(outward.shape, BF16), pltpu.HBM(block, F32)),
        in_specs=[SMEM, SMEM, VMEM] + [HBM] * (5 + len(rest)),
        out_specs=(VMEM, HBM),
        scratch_shapes=held
        + [
            pltpu.VMEM((rows, wide), BF16),
            pltpu.VMEM(block, F32),
            pltpu.SemaphoreType.DMA((8 + len(rest),)),
        ],
        compiler_params=PARAMS,
        name="run_heads",
    )(here, steps, arrived, *pinned(embedded, scales, w_in, w_final, w_qkv, *rest))


def local(
    latents,
    time_terms,
    step_sizes,
    doc_embed,
    pack_docs,
    segment_ids,
    w_in,
    w_qkv,
    query_gain,
    key_gain,
    w_proj,
    w_final,
):
    here = lax.axis_index("tm")
    place = here.astype(jnp.int32).reshape(1)
    times, owners = lax.axis_size("tm"), lax.axis_size("req")
    count, piece = doc_embed.shape
    w_heads = w_qkv[:, :, 0, :].transpose(1, 0, 2)
    w_last = w_final.T

    copies = jnp.broadcast_to(doc_embed[None], (owners, count, piece))
    table = lax.all_to_all(copies, "req", 0, 0)
    inward, pieces, pick, rest, sent = fold_inward(
        w_in, time_terms, w_heads, latents, pack_docs[None], owners * count
    )
    sent = select(table, pick, sent)
    arrived = lax.all_to_all(sent, "tm", 0, 0)
    outward, shifts, gram, cross, embedded, scales, gains, bias, member, direct, earlier = (
        fold_outward(
            place, step_sizes, time_terms, w_last, w_proj[0], w_in, w_heads, pieces, query_gain,
            key_gain, segment_ids, sent, count,
        )
    )
    sums, residual = run_heads(
        place, step_sizes, arrived, embedded, scales, w_in, w_last, w_heads, shifts, gram, cross,
        member, gains, bias, direct, earlier, inward, outward, rest,
    )
    parts = lax.all_to_all(sums, "tm", 0, 0)
    before = residual + jnp.sum(parts.astype(F32), axis=0)
    return jnp.where(here == 0, latents[0], before)[None]


def solution(mesh):
    in_specs = (
        P("tm", None, "req"),
        P(),
        P(),
        P("req", "tm"),
        P("req"),
        P("req", None),
        P(),
        P(None, None, "tm", None),
        P("tm", None),
        P("tm", None),
        P("tm", None, None),
        P(),
    )
    out_specs = P("tm", None, "req")
    return jax.shard_map(local, mesh=mesh, in_specs=in_specs, out_specs=out_specs, check_vma=False)
```

```python
import jax
import jax.numpy as jnp
from jax import lax
from jax.experimental import pallas as pl
from jax.experimental.pallas import tpu as pltpu
from jax.sharding import PartitionSpec as P

EPS = 1e-06
MASKED = -1e30
LOG2E = 1.4426950408889634
BF16, F32 = jnp.bfloat16, jnp.float32
NN = (((1,), (0,)), ((), ()))
NT = (((1,), (1,)), ((), ()))
VMEM = pl.BlockSpec(memory_space=pltpu.VMEM)
SMEM = pl.BlockSpec(memory_space=pltpu.SMEM)
HBM = pl.BlockSpec(memory_space=pltpu.HBM)
PARAMS = pltpu.CompilerParams(vmem_limit_bytes=24 * 2**20)


def dot(left, right, dims=NN, precision=None):
    return lax.dot_general(left, right, dims, precision=precision, preferred_element_type=F32)


def two_parts(values):
    high = values.astype(BF16)
    return high, (values - high.astype(F32)).astype(BF16)


def stack_rows(*parts):
    return jnp.concatenate([p.astype(F32) for p in parts], axis=0).astype(BF16)


def centre(values):
    return values - jnp.mean(values, axis=-1, keepdims=True)


def pinned(*arrays):
    return tuple(pltpu.with_memory_space_constraint(a, pltpu.HBM) for a in arrays)


def fetch(pairs, sems):
    copies = [pltpu.make_async_copy(a, b, sems.at[i]) for i, (a, b) in enumerate(pairs)]
    for copy in copies:
        copy.start()
    return copies


def pack_kernel(
    latents, pack_docs,
    pick, rest, sent,
    latents_v, packs_v, pick_v, rest_v, lowered_v, sems, out_sems,
):
    times, chans = sent.shape[0], latents_v.shape[1]
    copies = fetch([(latents, latents_v), (pack_docs, packs_v)], sems)
    copies[0].wait()
    values = latents_v[0]
    high = values.astype(BF16)
    lowered_v[...] = high
    rest_v[...] = values - high.astype(F32)
    copies[1].wait()
    count = packs_v.shape[1]
    column = jnp.broadcast_to(packs_v[...].astype(F32), (count, count))
    eye = lax.broadcasted_iota(jnp.int32, (count, count), 0) == lax.broadcasted_iota(
        jnp.int32, (count, count), 1
    )
    column = jnp.sum(jnp.where(eye, column, 0.0), axis=1, keepdims=True)
    places = lax.broadcasted_iota(jnp.int32, (count, pick.shape[1]), 1).astype(F32)
    chosen = jnp.where(places == column, 1.0, 0.0)
    pick_v[...] = stack_rows(chosen, jnp.zeros_like(chosen))
    left = fetch(
        [(rest_v, rest), (pick_v, pick)]
        + [(lowered_v, sent.at[i, pl.ds(0, chans)]) for i in range(times)],
        out_sems,
    )
    for copy in left:
        copy.wait()


def select_kernel(table, pick, sent, out, pick_v, staged, sems):
    del sent
    size, rows, lanes = out.shape
    owners, count, piece = table.shape
    fetch([(pick, pick_v)], sems.at[pl.ds(size, 1)])[0].wait()
    chosen = dot(pick_v[...], table[...].reshape(owners * count, piece))[:count]
    tail = jnp.concatenate(
        [chosen[:, lanes:], jnp.zeros((count, 2 * lanes - piece), F32)], axis=1
    )
    staged[...] = stack_rows(chosen[:, :lanes], tail)
    head = rows - 2 * count
    copies = fetch([(staged, out.at[i, pl.ds(head, 2 * count)]) for i in range(size)], sems)
    for copy in copies:
        copy.wait()


def small_rows(times, chans, head, tokens, count):
    sizes = [
        ("query_gain", head), ("key_gain", head), ("bias", tokens), ("member", count),
        ("direct", chans), ("earlier", chans), ("cross", times), ("shifts", 3 * times),
    ]
    places, at = {}, 0
    for name, rows in sizes:
        places[name] = (at, at + rows)
        at += rows
    return places, at


def weights_kernel(
    here, steps, terms, w_in, w_qkv, w_final, w_proj, query_gain, key_gain, segments, sent,
    inward, outward, lines, gram, small,
    terms_v, w_in_v, w_qkv_v, w_final_v, w_proj_v, gains_v, segments_v,
    centred, pieces, rows, inward_v, outward_v, lines_v, gram_v, small_v, sems, out_sems,
):
    del sent
    times, chans, head = outward.shape
    tokens, count = segments_v.shape[1], 8
    wide = w_in_v.shape[1]
    places, _ = small_rows(times, chans, head, tokens, count)
    copies = fetch(
        [
            (w_in, w_in_v), (terms, terms_v), (w_qkv, w_qkv_v), (w_final, w_final_v),
            (w_proj, w_proj_v), (query_gain, gains_v.at[0]), (key_gain, gains_v.at[1]),
            (segments, segments_v),
        ],
        sems,
    )
    copies[0].wait()
    centred[...] = centre(w_in_v[...].astype(F32))
    high, low = two_parts(centred[...])
    pieces[:chans, :] = high
    pieces[chans:, :] = low
    copies[1].wait()
    left = []
    for step in range(times // 4):
        for j in range(4):
            scaled = centred[...] * (1.0 + terms_v[step * 4 + j, 2:3, :])
            rows[step % 2, j * chans : (j + 1) * chans, :] = scaled.astype(BF16)
        if step == 0:
            copies[2].wait()
        for c in range(3):
            turned = dot(rows[step % 2], w_qkv_v[c]).T.astype(BF16)
            inward_v[2 * step, c * head : (c + 1) * head, :] = turned[:, : 2 * chans]
            inward_v[2 * step + 1, c * head : (c + 1) * head, :] = turned[:, 2 * chans :]
    left += fetch([(inward_v, inward)], out_sems)
    copies[3].wait()
    copies[4].wait()
    for step in range(times // 4):
        for j in range(4):
            gated = w_final_v[...].astype(F32) * terms_v[step * 4 + j, 3:4, :]
            rows[step % 2, j * chans : (j + 1) * chans, :] = gated.astype(BF16)
        back = dot(rows[step % 2], w_proj_v[...], NT)
        for j in range(4):
            t = step * 4 + j
            outward_v[t] = (back[j * chans : (j + 1) * chans] * steps[t]).astype(BF16)
    left += fetch([(outward_v, outward)], out_sems.at[pl.ds(1, 1)])
    moved, means = [], []
    past = jnp.zeros((1, wide), F32)
    for t in range(times):
        moved.append(terms_v[t, 1:2, :])
        means.append(centre(terms_v[t, 0:1, :]))
        lines_v[times + t : times + t + 1, :] = 1.0 + terms_v[t, 2:3, :]
        past = past + jnp.where(t < here[0], steps[t], 0.0) * terms_v[t, 0:1, :]
    moved, means = jnp.concatenate(moved, axis=0), jnp.concatenate(means, axis=0)
    lines_v[:times, :] = means
    left += fetch([(lines_v, lines)], out_sems.at[pl.ds(2, 1)])

    def put(name, values):
        first, last = places[name]
        small_v[first:last, :] = jnp.concatenate(
            [values, jnp.zeros((values.shape[0], small_v.shape[1] - values.shape[1]), F32)], axis=1
        ) if values.shape[1] < small_v.shape[1] else values

    both = pieces[...]
    square = dot(both, both, NT)
    square = square[:chans, :chans] + square[chans:, :chans] + square[:chans, chans:]
    high, low = two_parts(square)
    gram_v[:chans, :] = high
    gram_v[chans:, :] = low
    left += fetch([(gram_v, gram)], out_sems.at[pl.ds(3, 1)])
    high, low = two_parts(means)
    mixed = dot(stack_rows(high, low), both, NT)
    put("cross", mixed[:times, :chans] + mixed[times:, :chans] + mixed[:times, chans:])
    high, low = two_parts(moved)
    split = stack_rows(high, low)
    shifts = []
    for c in range(3):
        shift = dot(split, w_qkv_v[c])
        shifts.append(shift[:times] + shift[times:])
    put("shifts", jnp.concatenate(shifts, axis=0))
    final = w_final_v[...]
    put("direct", dot(final, w_in_v[...], NT))
    high = past.astype(BF16)
    middle, low = two_parts(past - high.astype(F32))
    parts = stack_rows(high, middle, low, jnp.zeros((5, wide), F32))
    earlier = jnp.sum(dot(final, parts, NT), axis=-1, keepdims=True)
    put("earlier", jnp.broadcast_to(earlier, (chans, small_v.shape[1])))
    for copy in copies[5:]:
        copy.wait()
    put("query_gain", jnp.broadcast_to(gains_v[0] * (head**-0.5 * LOG2E), (head, head)).T)
    put("key_gain", jnp.broadcast_to(gains_v[1], (head, head)).T)
    ids = jnp.broadcast_to(segments_v[...].astype(F32), (tokens, tokens))
    put("bias", jnp.where(ids == ids.T, 0.0, MASKED))
    numbers = lax.broadcasted_iota(jnp.int32, (count, tokens), 0).astype(F32)
    put("member", jnp.where(numbers == ids[:count], 1.0, 0.0))
    left += fetch([(small_v, small)], out_sems.at[pl.ds(4, 1)])
    for copy in left:
        copy.wait()


def gather_documents(arrived, chans, count, piece):
    parts = []
    for i in range(arrived.shape[0]):
        block = arrived[i, chans:, :].astype(F32)
        parts.append(block[:count])
        parts.append(block[count:, : piece - block.shape[1]])
    return jnp.concatenate(parts, axis=1)


def heads_kernel(
    here, steps, arrived,
    lines_h, w_in_h, w_final_h, w_qkv_h, gram_h, small_h, inward_h, outward_h, rest_h,
    out, residual,
    lines, w_in, w_final, w_qkv, gram, small, inward, outward, rest,
    rows, residual_v, queries, keys, values, raised, mass, attended, sems,
):
    times, chans, head = outward.shape
    tokens = arrived.shape[2]
    count = (arrived.shape[1] - chans) // 2
    wide = w_in.shape[1]
    places, _ = small_rows(times, chans, head, tokens, count)
    copies = fetch(
        [
            (lines_h, lines), (w_in_h, w_in), (w_final_h, w_final), (w_qkv_h, w_qkv),
            (gram_h, gram), (small_h, small), (inward_h, inward), (outward_h, outward),
            (rest_h, rest),
        ],
        sems,
    )

    def table(name, lanes=None):
        first, last = places[name]
        return small[first:last, :lanes]

    documents = gather_documents(arrived, chans, count, wide // times)
    exact = stack_rows(documents, jnp.zeros_like(documents))
    documents = centre(documents)
    copies[0].wait()
    powers = []
    for t in range(0, times, 2):
        pair = []
        for j in range(2):
            row = documents + lines[t + j : t + j + 1, :]
            powers.append(jnp.sum(row * row, axis=-1, keepdims=True))
            pair.append(row * lines[times + t + j : times + t + j + 1, :])
        rows[t * count : (t + 2) * count, :] = jnp.concatenate(pair, axis=0).astype(BF16)
    copies[1].wait()
    copies[2].wait()
    narrow = dot(w_final[...], exact, NT)[:, :count]
    high, low = two_parts(documents)
    near = dot(stack_rows(high, low), w_in[...], NT)
    near = near[:count] + near[count:]
    copies[3].wait()
    base = jnp.concatenate([dot(rows[...], w_qkv[c]) for c in range(3)], axis=1)
    for copy in copies[4:]:
        copy.wait()
    shifts = table("shifts")
    shifts = jnp.concatenate([shifts[c * times : (c + 1) * times] for c in range(3)], axis=1)
    turned = []
    for half in range(2):
        span = slice(half * 8 * count, (half + 1) * 8 * count)
        block = [base[span], shifts[half * 8 : (half + 1) * 8, :]]
        left = head - 8 * count - 8
        block.append(jnp.zeros((left, 3 * head), F32))
        turned.append(jnp.concatenate(block, axis=0).T.astype(BF16))

    belongs = table("member")
    cross = table("cross", chans)
    past, whole = jnp.zeros((chans, tokens), F32), 0.0
    for t in range(times):
        weight = jnp.where(t < here[0], steps[t], 0.0)
        past = past + weight * arrived[t, :chans, :].astype(F32)
        whole = whole + weight
    highest = lax.Precision.HIGHEST
    near_docs = dot(whole * narrow + table("earlier", count), belongs, NN, highest)
    first_rest = jnp.where(here[0] == 0, rest[...], 0.0)
    residual_v[...] = (
        dot(table("direct", chans), past, NN, highest)
        + near_docs
        + arrived[0, :chans, :].astype(F32)
        + first_rest
    )
    last = pltpu.make_async_copy(residual_v, residual, sems.at[len(copies)])
    last.start()

    scaled_low, rates = [], []
    for t in range(times):
        mixed = 2.0 * (near + cross[t : t + 1, :])
        high, low = two_parts(mixed)
        left = jnp.concatenate([gram[...], stack_rows(high, low)], axis=0)
        block = arrived[t, :chans, :]
        product = dot(left, block)
        both = product[:chans] + product[chans : 2 * chans]
        block = block.astype(F32)
        other = product[2 * chans : 2 * chans + count] + product[2 * chans + count :]
        spread = jnp.sum(both * block, axis=0, keepdims=True) + jnp.sum(
            belongs * (other + powers[t]), axis=0, keepdims=True
        )
        rate = lax.rsqrt(spread / wide + EPS)
        rates.append(rate)
        scaled_low.append((block * rate).astype(BF16))

    def unit(block, gain):
        power = jnp.mean(block * block, axis=0, keepdims=True)
        return block * (lax.rsqrt(power + EPS) * gain)

    empty = jnp.zeros((chans, tokens), BF16)
    for t in range(times):
        half, j = divmod(t, 8)
        left = jnp.concatenate([inward[t // 2], turned[half]], axis=1)
        first = [scaled_low[t], empty] if t % 2 == 0 else [empty, scaled_low[t]]
        ones = lax.broadcasted_iota(jnp.int32, (8, tokens), 0) == j
        second = [jnp.zeros((j * count, tokens), F32)] if j else []
        second.append(belongs * rates[t])
        if j < 7:
            second.append(jnp.zeros(((7 - j) * count, tokens), F32))
        second.append(jnp.where(ones, 1.0, 0.0))
        second.append(jnp.zeros((head - 8 * count - 8, tokens), F32))
        second = jnp.concatenate(second, axis=0).astype(BF16)
        right = jnp.concatenate(first + [second], axis=0)
        queries[t] = unit(dot(left[:head], right), table("query_gain")).astype(BF16)
        keys[t] = unit(dot(left[head : 2 * head], right), table("key_gain")).T.astype(BF16)
        values[t] = dot(left[2 * head :], right).astype(BF16)
    for t in range(times):
        scores = dot(keys[t], queries[t]) + table("bias")
        powered = jnp.exp2(scores - jnp.max(scores, axis=0, keepdims=True))
        mass[t : t + 1, :] = 1.0 / jnp.sum(powered, axis=0, keepdims=True)
        raised[t] = powered.astype(BF16)
    for t in range(times):
        attended[t] = (dot(values[t], raised[t]) * mass[t : t + 1, :]).astype(BF16)
    out[0] = jnp.zeros((chans, tokens), BF16)
    total = first_rest
    for t in range(times - 1):
        total = total + dot(outward[t], attended[t])
        out[t + 1] = total.astype(BF16)
    last.wait()


def pack(latents, pack_docs, documents, times):
    block, count = latents.shape[1:], pack_docs.shape[1]
    return pl.pallas_call(
        pack_kernel,
        out_shape=(
            pltpu.HBM((2 * count, documents), BF16),
            pltpu.HBM(block, F32),
            pltpu.HBM((times, block[0] + 2 * count, block[1]), BF16),
        ),
        in_specs=[HBM] * 2,
        out_specs=(HBM,) * 3,
        scratch_shapes=[
            pltpu.VMEM(latents.shape, F32),
            pltpu.VMEM(pack_docs.shape, jnp.int32),
            pltpu.VMEM((2 * count, documents), BF16),
            pltpu.VMEM(block, F32),
            pltpu.VMEM(block, BF16),
            pltpu.SemaphoreType.DMA((2,)),
            pltpu.SemaphoreType.DMA((2 + times,)),
        ],
        compiler_params=PARAMS,
        name="pack",
    )(*pinned(latents, pack_docs))


def select(table, pick, sent):
    size = sent.shape[0]
    return pl.pallas_call(
        select_kernel,
        out_shape=pltpu.HBM(sent.shape, BF16),
        in_specs=[VMEM, HBM, HBM],
        out_specs=HBM,
        scratch_shapes=[
            pltpu.VMEM(pick.shape, BF16),
            pltpu.VMEM((pick.shape[0], sent.shape[2]), BF16),
            pltpu.SemaphoreType.DMA((size + 1,)),
        ],
        input_output_aliases={2: 0},
        compiler_params=PARAMS,
        name="select",
    )(table, *pinned(pick, sent))


def fold_weights(
    here, steps, terms, w_in, w_qkv, w_final, w_proj, query_gain, key_gain, segments, sent
):
    times, wide = terms.shape[0], terms.shape[2]
    chans, head, tokens = w_final.shape[0], w_proj.shape[0], segments.shape[1]
    count = (sent.shape[1] - chans) // 2
    shapes = [
        ((times // 2, 3 * head, 2 * chans), BF16),
        ((times, chans, head), BF16),
        ((2 * times, wide), F32),
        ((2 * chans, chans), BF16),
        ((small_rows(times, chans, head, tokens, count)[1], tokens), F32),
    ]
    return pl.pallas_call(
        weights_kernel,
        out_shape=tuple(pltpu.HBM(*s) for s in shapes),
        in_specs=[SMEM] * 2 + [HBM] * 9,
        out_specs=(HBM,) * 5,
        scratch_shapes=[
            pltpu.VMEM(a.shape, a.dtype) for a in (terms, w_in, w_qkv, w_final, w_proj)
        ]
        + [
            pltpu.VMEM((2,) + query_gain.shape, F32),
            pltpu.VMEM(segments.shape, jnp.int32),
            pltpu.VMEM((chans, wide), F32),
            pltpu.VMEM((2 * chans, wide), BF16),
            pltpu.VMEM((2, 4 * chans, wide), BF16),
        ]
        + [pltpu.VMEM(*s) for s in shapes]
        + [pltpu.SemaphoreType.DMA((8,)), pltpu.SemaphoreType.DMA((5,))],
        compiler_params=PARAMS,
        name="fold_weights",
    )(
        here,
        steps,
        *pinned(terms, w_in, w_qkv, w_final, w_proj, query_gain, key_gain, segments, sent),
    )


def run_heads(here, steps, arrived, *operands):
    outward, rest = operands[-2:]
    times, chans, head = outward.shape
    tokens = arrived.shape[2]
    rows = times * (arrived.shape[1] - chans) // 2
    wide = operands[0].shape[1]
    square = pltpu.VMEM((times, head, tokens), BF16)
    return pl.pallas_call(
        heads_kernel,
        out_shape=(jax.ShapeDtypeStruct(outward.shape, BF16), pltpu.HBM(rest.shape, F32)),
        in_specs=[SMEM, SMEM, VMEM] + [HBM] * len(operands),
        out_specs=(VMEM, HBM),
        scratch_shapes=[pltpu.VMEM(a.shape, a.dtype) for a in operands]
        + [
            pltpu.VMEM((rows, wide), BF16),
            pltpu.VMEM(rest.shape, F32),
            square, square, square, square,
            pltpu.VMEM((times, tokens), F32),
            square,
            pltpu.SemaphoreType.DMA((1 + len(operands),)),
        ],
        compiler_params=PARAMS,
        name="run_heads",
    )(here, steps, arrived, *pinned(*operands))


def local(
    latents,
    time_terms,
    step_sizes,
    doc_embed,
    pack_docs,
    segment_ids,
    w_in,
    w_qkv,
    query_gain,
    key_gain,
    w_proj,
    w_final,
):
    here = lax.axis_index("tm")
    place = here.astype(jnp.int32).reshape(1)
    times, owners = lax.axis_size("tm"), lax.axis_size("req")
    count, piece = doc_embed.shape
    w_heads = w_qkv[:, :, 0, :].transpose(1, 0, 2)
    w_last = w_final.T

    copies = jnp.broadcast_to(doc_embed[None], (owners, count, piece))
    table = lax.all_to_all(copies, "req", 0, 0)
    pick, rest, sent = pack(latents, pack_docs[None], owners * count, times)
    sent = select(table, pick, sent)
    arrived = lax.all_to_all(sent, "tm", 0, 0)
    inward, outward, lines, gram, small = fold_weights(
        place, step_sizes, time_terms, w_in, w_heads, w_last, w_proj[0], query_gain, key_gain,
        segment_ids, sent,
    )
    sums, residual = run_heads(
        place, step_sizes, arrived, lines, w_in, w_last, w_heads, gram, small, inward, outward,
        rest,
    )
    parts = lax.all_to_all(sums, "tm", 0, 0)
    return (residual + jnp.sum(parts.astype(F32), axis=0))[None]


def solution(mesh):
    in_specs = (
        P("tm", None, "req"),
        P(),
        P(),
        P("req", "tm"),
        P("req"),
        P("req", None),
        P(),
        P(None, None, "tm", None),
        P("tm", None),
        P("tm", None),
        P("tm", None, None),
        P(),
    )
    out_specs = P("tm", None, "req")
    return jax.shard_map(local, mesh=mesh, in_specs=in_specs, out_specs=out_specs, check_vma=False)
```

```python
import jax
import jax.numpy as jnp
from jax import lax
from jax.experimental import pallas as pl
from jax.experimental.pallas import tpu as pltpu
from jax.sharding import PartitionSpec as P

EPS = 1e-06
MASKED = -1e30
LOG2E = 1.4426950408889634
BF16, F32 = jnp.bfloat16, jnp.float32
NN = (((1,), (0,)), ((), ()))
NT = (((1,), (1,)), ((), ()))
VMEM = pl.BlockSpec(memory_space=pltpu.VMEM)
SMEM = pl.BlockSpec(memory_space=pltpu.SMEM)
HBM = pl.BlockSpec(memory_space=pltpu.HBM)
PARAMS = pltpu.CompilerParams(vmem_limit_bytes=24 * 2**20)


def dot(left, right, dims=NN, precision=None):
    return lax.dot_general(left, right, dims, precision=precision, preferred_element_type=F32)


def two_parts(values):
    high = values.astype(BF16)
    return high, (values - high.astype(F32)).astype(BF16)


def stack_rows(*parts):
    return jnp.concatenate([p.astype(F32) for p in parts], axis=0).astype(BF16)


def centre(values):
    return values - jnp.mean(values, axis=-1, keepdims=True)


def pinned(*arrays):
    return tuple(pltpu.with_memory_space_constraint(a, pltpu.HBM) for a in arrays)


def fetch(pairs, sems):
    copies = [pltpu.make_async_copy(a, b, sems.at[i]) for i, (a, b) in enumerate(pairs)]
    for copy in copies:
        copy.start()
    return copies


def select_kernel(
    table, latents, pack_docs,
    sent, rest,
    latents_v, packs_v, rest_v, lowered_v, chosen_v, sems, out_sems,
):
    times, rows, lanes = sent.shape
    chans = latents_v.shape[1]
    owners, count, piece = table.shape
    copies = fetch([(latents, latents_v), (pack_docs, packs_v)], sems)
    copies[0].wait()
    values = latents_v[0]
    high = values.astype(BF16)
    lowered_v[...] = high
    rest_v[...] = values - high.astype(F32)
    left = fetch(
        [(rest_v, rest)] + [(lowered_v, sent.at[i, pl.ds(0, chans)]) for i in range(times)],
        out_sems,
    )
    copies[1].wait()
    column = jnp.broadcast_to(packs_v[...].astype(F32), (count, count))
    eye = lax.broadcasted_iota(jnp.int32, (count, count), 0) == lax.broadcasted_iota(
        jnp.int32, (count, count), 1
    )
    column = jnp.sum(jnp.where(eye, column, 0.0), axis=1, keepdims=True)
    places = lax.broadcasted_iota(jnp.int32, (count, owners * count), 1).astype(F32)
    pick = jnp.where(places == column, 1.0, 0.0)
    pick = stack_rows(pick, jnp.zeros_like(pick))
    chosen = dot(pick, table[...].reshape(owners * count, piece))[:count]
    tail = jnp.concatenate(
        [chosen[:, lanes:], jnp.zeros((count, 2 * lanes - piece), F32)], axis=1
    )
    chosen_v[...] = stack_rows(chosen[:, :lanes], tail)
    left += fetch(
        [(chosen_v, sent.at[i, pl.ds(chans, 2 * count)]) for i in range(times)],
        out_sems.at[pl.ds(1 + times, times)],
    )
    for copy in left:
        copy.wait()


def small_rows(times, chans, head, tokens, count):
    sizes = [
        ("query_gain", head), ("key_gain", head), ("bias", tokens), ("member", count),
        ("direct", chans), ("earlier", chans), ("cross", times), ("shifts", 3 * times),
        ("rest", chans), ("weights", times),
    ]
    places, at = {}, 0
    for name, rows in sizes:
        places[name] = (at, at + rows)
        at += rows
    return places, at


def weights_kernel(
    here, steps, terms, w_in, w_qkv, w_final, w_proj, query_gain, key_gain, segments, rest,
    inward, outward, lines, gram, small,
    terms_v, w_in_v, w_qkv_v, w_final_v, w_proj_v, gains_v, segments_v, rest_v,
    centred, pieces, rows, inward_v, outward_v, lines_v, gram_v, small_v, sems, out_sems,
):
    times, chans, head = outward.shape
    tokens, count = segments_v.shape[1], 8
    wide = w_in_v.shape[1]
    places, _ = small_rows(times, chans, head, tokens, count)
    copies = fetch(
        [
            (w_in, w_in_v), (terms, terms_v), (w_qkv, w_qkv_v), (w_final, w_final_v),
            (w_proj, w_proj_v), (query_gain, gains_v.at[0]), (key_gain, gains_v.at[1]),
            (segments, segments_v), (rest, rest_v),
        ],
        sems,
    )
    copies[0].wait()
    centred[...] = centre(w_in_v[...].astype(F32))
    high, low = two_parts(centred[...])
    pieces[:chans, :] = high
    pieces[chans:, :] = low
    copies[1].wait()
    left = []
    for step in range(times // 4):
        for j in range(4):
            scaled = centred[...] * (1.0 + terms_v[step * 4 + j, 2:3, :])
            rows[step % 2, j * chans : (j + 1) * chans, :] = scaled.astype(BF16)
        if step == 0:
            copies[2].wait()
        for c in range(3):
            turned = dot(rows[step % 2], w_qkv_v[c]).T.astype(BF16)
            inward_v[2 * step, c * head : (c + 1) * head, :] = turned[:, : 2 * chans]
            inward_v[2 * step + 1, c * head : (c + 1) * head, :] = turned[:, 2 * chans :]
    left += fetch([(inward_v, inward)], out_sems)
    copies[3].wait()
    copies[4].wait()
    for step in range(times // 4):
        for j in range(4):
            gated = w_final_v[...].astype(F32) * terms_v[step * 4 + j, 3:4, :]
            rows[step % 2, j * chans : (j + 1) * chans, :] = gated.astype(BF16)
        back = dot(rows[step % 2], w_proj_v[...], NT)
        for j in range(4):
            t = step * 4 + j
            outward_v[t] = (back[j * chans : (j + 1) * chans] * steps[t]).astype(BF16)
    left += fetch([(outward_v, outward)], out_sems.at[pl.ds(1, 1)])
    moved, means = [], []
    past = jnp.zeros((1, wide), F32)
    for t in range(times):
        moved.append(terms_v[t, 1:2, :])
        means.append(centre(terms_v[t, 0:1, :]))
        lines_v[times + t : times + t + 1, :] = 1.0 + terms_v[t, 2:3, :]
        past = past + jnp.where(t < here[0], steps[t], 0.0) * terms_v[t, 0:1, :]
    moved, means = jnp.concatenate(moved, axis=0), jnp.concatenate(means, axis=0)
    lines_v[:times, :] = means
    left += fetch([(lines_v, lines)], out_sems.at[pl.ds(2, 1)])

    def put(name, values):
        first, last = places[name]
        small_v[first:last, :] = jnp.concatenate(
            [values, jnp.zeros((values.shape[0], small_v.shape[1] - values.shape[1]), F32)], axis=1
        ) if values.shape[1] < small_v.shape[1] else values

    both = pieces[...]
    square = dot(both, both, NT)
    square = square[:chans, :chans] + square[chans:, :chans] + square[:chans, chans:]
    high, low = two_parts(square)
    gram_v[:chans, :] = high
    gram_v[chans:, :] = low
    left += fetch([(gram_v, gram)], out_sems.at[pl.ds(3, 1)])
    high, low = two_parts(means)
    mixed = dot(stack_rows(high, low), both, NT)
    put("cross", mixed[:times, :chans] + mixed[times:, :chans] + mixed[:times, chans:])
    high, low = two_parts(moved)
    split = stack_rows(high, low)
    shifts = []
    for c in range(3):
        shift = dot(split, w_qkv_v[c])
        shifts.append(shift[:times] + shift[times:])
    put("shifts", jnp.concatenate(shifts, axis=0))
    final = w_final_v[...]
    put("direct", dot(final, w_in_v[...], NT))
    high = past.astype(BF16)
    middle, low = two_parts(past - high.astype(F32))
    parts = stack_rows(high, middle, low, jnp.zeros((5, wide), F32))
    earlier = jnp.sum(dot(final, parts, NT), axis=-1, keepdims=True)
    put("earlier", jnp.broadcast_to(earlier, (chans, small_v.shape[1])))
    for copy in copies[5:]:
        copy.wait()
    put("query_gain", jnp.broadcast_to(gains_v[0] * (head**-0.5 * LOG2E), (head, head)).T)
    put("key_gain", jnp.broadcast_to(gains_v[1], (head, head)).T)
    ids = jnp.broadcast_to(segments_v[...].astype(F32), (tokens, tokens))
    put("bias", jnp.where(ids == ids.T, 0.0, MASKED))
    numbers = lax.broadcasted_iota(jnp.int32, (count, tokens), 0).astype(F32)
    put("rest", jnp.where(here[0] == 0, rest_v[...], 0.0))
    ones = jnp.ones((1, tokens), F32)
    passed = [ones * jnp.where(t < here[0], steps[t], 0.0) for t in range(times)]
    put("weights", jnp.concatenate(passed, axis=0))
    put("member", jnp.where(numbers == ids[:count], 1.0, 0.0))
    left += fetch([(small_v, small)], out_sems.at[pl.ds(4, 1)])
    for copy in left:
        copy.wait()


def gather_documents(arrived, chans, count, piece):
    parts = []
    for i in range(arrived.shape[0]):
        block = arrived[i, chans:, :].astype(F32)
        parts.append(block[:count])
        parts.append(block[count:, : piece - block.shape[1]])
    return jnp.concatenate(parts, axis=1)


def heads_kernel(
    arrived,
    lines_h, w_in_h, w_final_h, w_qkv_h, gram_h, small_h, inward_h, outward_h,
    out, residual,
    lines, w_in, w_final, w_qkv, gram, small, inward, outward,
    rows, residual_v, queries, keys, values, raised, mass, attended, sems,
):
    times, chans, head = outward.shape
    tokens = arrived.shape[2]
    count = (arrived.shape[1] - chans) // 2
    wide = w_in.shape[1]
    places, _ = small_rows(times, chans, head, tokens, count)
    copies = fetch(
        [
            (lines_h, lines), (w_in_h, w_in), (w_final_h, w_final), (w_qkv_h, w_qkv),
            (gram_h, gram), (small_h, small), (inward_h, inward), (outward_h, outward),
        ],
        sems,
    )

    def table(name, lanes=None):
        first, last = places[name]
        return small[first:last, :lanes]

    documents = gather_documents(arrived, chans, count, wide // times)
    exact = stack_rows(documents, jnp.zeros_like(documents))
    documents = centre(documents)
    copies[0].wait()
    powers = []
    for t in range(0, times, 2):
        pair = []
        for j in range(2):
            row = documents + lines[t + j : t + j + 1, :]
            powers.append(jnp.sum(row * row, axis=-1, keepdims=True))
            pair.append(row * lines[times + t + j : times + t + j + 1, :])
        rows[t * count : (t + 2) * count, :] = jnp.concatenate(pair, axis=0).astype(BF16)
    copies[1].wait()
    copies[2].wait()
    narrow = dot(w_final[...], exact, NT)[:, :count]
    high, low = two_parts(documents)
    near = dot(stack_rows(high, low), w_in[...], NT)
    near = near[:count] + near[count:]
    copies[3].wait()
    base = jnp.concatenate([dot(rows[...], w_qkv[c]) for c in range(3)], axis=1)
    for copy in copies[4:]:
        copy.wait()
    shifts = table("shifts")
    shifts = jnp.concatenate([shifts[c * times : (c + 1) * times] for c in range(3)], axis=1)
    turned = []
    for half in range(2):
        span = slice(half * 8 * count, (half + 1) * 8 * count)
        block = [base[span], shifts[half * 8 : (half + 1) * 8, :]]
        left = head - 8 * count - 8
        block.append(jnp.zeros((left, 3 * head), F32))
        turned.append(jnp.concatenate(block, axis=0).T.astype(BF16))

    belongs = table("member")
    cross = table("cross", chans)
    weights = table("weights")
    past = jnp.zeros((chans, tokens), F32)
    for t in range(times):
        past = past + weights[t : t + 1, :] * arrived[t, :chans, :].astype(F32)
    whole = jnp.sum(weights[:, :count], axis=0, keepdims=True)
    highest = lax.Precision.HIGHEST
    near_docs = dot(whole * narrow + table("earlier", count), belongs, NN, highest)
    first_rest = table("rest")
    residual_v[...] = (
        dot(table("direct", chans), past, NN, highest)
        + near_docs
        + arrived[0, :chans, :].astype(F32)
        + first_rest
    )
    last = pltpu.make_async_copy(residual_v, residual, sems.at[len(copies)])
    last.start()

    scaled_low, rates = [], []
    for t in range(times):
        mixed = 2.0 * (near + cross[t : t + 1, :])
        high, low = two_parts(mixed)
        left = jnp.concatenate([gram[...], stack_rows(high, low)], axis=0)
        block = arrived[t, :chans, :]
        product = dot(left, block)
        both = product[:chans] + product[chans : 2 * chans]
        block = block.astype(F32)
        other = product[2 * chans : 2 * chans + count] + product[2 * chans + count :]
        spread = jnp.sum(both * block, axis=0, keepdims=True) + jnp.sum(
            belongs * (other + powers[t]), axis=0, keepdims=True
        )
        rate = lax.rsqrt(spread / wide + EPS)
        rates.append(rate)
        scaled_low.append((block * rate).astype(BF16))

    def unit(block, gain):
        power = jnp.mean(block * block, axis=0, keepdims=True)
        return block * (lax.rsqrt(power + EPS) * gain)

    empty = jnp.zeros((chans, tokens), BF16)
    for t in range(times):
        half, j = divmod(t, 8)
        left = jnp.concatenate([inward[t // 2], turned[half]], axis=1)
        first = [scaled_low[t], empty] if t % 2 == 0 else [empty, scaled_low[t]]
        ones = lax.broadcasted_iota(jnp.int32, (8, tokens), 0) == j
        second = [jnp.zeros((j * count, tokens), F32)] if j else []
        second.append(belongs * rates[t])
        if j < 7:
            second.append(jnp.zeros(((7 - j) * count, tokens), F32))
        second.append(jnp.where(ones, 1.0, 0.0))
        second.append(jnp.zeros((head - 8 * count - 8, tokens), F32))
        second = jnp.concatenate(second, axis=0).astype(BF16)
        right = jnp.concatenate(first + [second], axis=0)
        queries[t] = unit(dot(left[:head], right), table("query_gain")).astype(BF16)
        keys[t] = unit(dot(left[head : 2 * head], right), table("key_gain")).T.astype(BF16)
        values[t] = dot(left[2 * head :], right).astype(BF16)
    for t in range(times):
        scores = dot(keys[t], queries[t]) + table("bias")
        powered = jnp.exp2(scores - jnp.max(scores, axis=0, keepdims=True))
        mass[t : t + 1, :] = 1.0 / jnp.sum(powered, axis=0, keepdims=True)
        raised[t] = powered.astype(BF16)
    for t in range(times):
        attended[t] = (dot(values[t], raised[t]) * mass[t : t + 1, :]).astype(BF16)
    out[0] = jnp.zeros((chans, tokens), BF16)
    total = first_rest
    for t in range(times - 1):
        total = total + dot(outward[t], attended[t])
        out[t + 1] = total.astype(BF16)
    last.wait()


def select(table, latents, pack_docs, times):
    block, count = latents.shape[1:], pack_docs.shape[1]
    return pl.pallas_call(
        select_kernel,
        out_shape=(
            pltpu.HBM((times, block[0] + 2 * count, block[1]), BF16),
            pltpu.HBM(block, F32),
        ),
        in_specs=[VMEM, HBM, HBM],
        out_specs=(HBM, HBM),
        scratch_shapes=[
            pltpu.VMEM(latents.shape, F32),
            pltpu.VMEM(pack_docs.shape, jnp.int32),
            pltpu.VMEM(block, F32),
            pltpu.VMEM(block, BF16),
            pltpu.VMEM((2 * count, block[1]), BF16),
            pltpu.SemaphoreType.DMA((2,)),
            pltpu.SemaphoreType.DMA((1 + 2 * times,)),
        ],
        compiler_params=PARAMS,
        name="select",
    )(table, *pinned(latents, pack_docs))


def fold_weights(
    here, steps, terms, w_in, w_qkv, w_final, w_proj, query_gain, key_gain, segments, rest
):
    times, wide = terms.shape[0], terms.shape[2]
    chans, head, tokens = w_final.shape[0], w_proj.shape[0], segments.shape[1]
    count = 8
    shapes = [
        ((times // 2, 3 * head, 2 * chans), BF16),
        ((times, chans, head), BF16),
        ((2 * times, wide), F32),
        ((2 * chans, chans), BF16),
        ((small_rows(times, chans, head, tokens, count)[1], tokens), F32),
    ]
    return pl.pallas_call(
        weights_kernel,
        out_shape=tuple(pltpu.HBM(*s) for s in shapes),
        in_specs=[SMEM] * 2 + [HBM] * 9,
        out_specs=(HBM,) * 5,
        scratch_shapes=[
            pltpu.VMEM(a.shape, a.dtype) for a in (terms, w_in, w_qkv, w_final, w_proj)
        ]
        + [
            pltpu.VMEM((2,) + query_gain.shape, F32),
            pltpu.VMEM(segments.shape, jnp.int32),
            pltpu.VMEM(rest.shape, F32),
            pltpu.VMEM((chans, wide), F32),
            pltpu.VMEM((2 * chans, wide), BF16),
            pltpu.VMEM((2, 4 * chans, wide), BF16),
        ]
        + [pltpu.VMEM(*s) for s in shapes]
        + [pltpu.SemaphoreType.DMA((9,)), pltpu.SemaphoreType.DMA((5,))],
        compiler_params=PARAMS,
        name="fold_weights",
    )(
        here,
        steps,
        *pinned(terms, w_in, w_qkv, w_final, w_proj, query_gain, key_gain, segments, rest),
    )


def run_heads(arrived, *operands):
    outward = operands[-1]
    times, chans, head = outward.shape
    tokens = arrived.shape[2]
    rows = times * (arrived.shape[1] - chans) // 2
    wide = operands[0].shape[1]
    square = pltpu.VMEM((times, head, tokens), BF16)
    return pl.pallas_call(
        heads_kernel,
        out_shape=(
            jax.ShapeDtypeStruct((times, chans, tokens), BF16),
            pltpu.HBM((chans, tokens), F32),
        ),
        in_specs=[VMEM] + [HBM] * len(operands),
        out_specs=(VMEM, HBM),
        scratch_shapes=[pltpu.VMEM(a.shape, a.dtype) for a in operands]
        + [
            pltpu.VMEM((rows, wide), BF16),
            pltpu.VMEM((chans, tokens), F32),
            square, square, square, square,
            pltpu.VMEM((times, tokens), F32),
            square,
            pltpu.SemaphoreType.DMA((1 + len(operands),)),
        ],
        compiler_params=PARAMS,
        name="run_heads",
    )(arrived, *pinned(*operands))


def local(
    latents,
    time_terms,
    step_sizes,
    doc_embed,
    pack_docs,
    segment_ids,
    w_in,
    w_qkv,
    query_gain,
    key_gain,
    w_proj,
    w_final,
):
    here = lax.axis_index("tm")
    place = here.astype(jnp.int32).reshape(1)
    times, owners = lax.axis_size("tm"), lax.axis_size("req")
    count, piece = doc_embed.shape
    w_heads = w_qkv[:, :, 0, :].transpose(1, 0, 2)
    w_last = w_final.T

    copies = jnp.broadcast_to(doc_embed[None], (owners, count, piece))
    table = lax.all_to_all(copies, "req", 0, 0)
    sent, rest = select(table, latents, pack_docs[None], times)
    arrived = lax.all_to_all(sent, "tm", 0, 0)
    inward, outward, lines, gram, small = fold_weights(
        place, step_sizes, time_terms, w_in, w_heads, w_last, w_proj[0], query_gain, key_gain,
        segment_ids, rest,
    )
    sums, residual = run_heads(
        arrived, lines, w_in, w_last, w_heads, gram, small, inward, outward
    )
    parts = lax.all_to_all(sums, "tm", 0, 0)
    return (residual + jnp.sum(parts.astype(F32), axis=0))[None]


def solution(mesh):
    in_specs = (
        P("tm", None, "req"),
        P(),
        P(),
        P("req", "tm"),
        P("req"),
        P("req", None),
        P(),
        P(None, None, "tm", None),
        P("tm", None),
        P("tm", None),
        P("tm", None, None),
        P(),
    )
    out_specs = P("tm", None, "req")
    return jax.shard_map(local, mesh=mesh, in_specs=in_specs, out_specs=out_specs, check_vma=False)
```

```python
import jax
import jax.numpy as jnp
from jax import lax
from jax.experimental import pallas as pl
from jax.experimental.pallas import tpu as pltpu
from jax.sharding import PartitionSpec as P

EPS = 1e-06
MASKED = -1e30
LOG2E = 1.4426950408889634
BF16, F32 = jnp.bfloat16, jnp.float32
NN = (((1,), (0,)), ((), ()))
NT = (((1,), (1,)), ((), ()))
VMEM = pl.BlockSpec(memory_space=pltpu.VMEM)
SMEM = pl.BlockSpec(memory_space=pltpu.SMEM)
HBM = pl.BlockSpec(memory_space=pltpu.HBM)
PARAMS = pltpu.CompilerParams(vmem_limit_bytes=24 * 2**20)


def dot(left, right, dims=NN, precision=None):
    return lax.dot_general(left, right, dims, precision=precision, preferred_element_type=F32)


def two_parts(values):
    high = values.astype(BF16)
    return high, (values - high.astype(F32)).astype(BF16)


def stack_rows(*parts):
    return jnp.concatenate([p.astype(F32) for p in parts], axis=0).astype(BF16)


def centre(values):
    return values - jnp.mean(values, axis=-1, keepdims=True)


def pinned(*arrays):
    return tuple(pltpu.with_memory_space_constraint(a, pltpu.HBM) for a in arrays)


def fetch(pairs, sems):
    copies = [pltpu.make_async_copy(a, b, sems.at[i]) for i, (a, b) in enumerate(pairs)]
    for copy in copies:
        copy.start()
    return copies


def first_core():
    return lax.rem(lax.axis_index("req"), 2) == 0


def fold_inward(centred, terms, w_qkv, rows, inward):
    chans, head = centred.shape[0], w_qkv.shape[2]
    for step in range(terms.shape[0] // 4):
        for j in range(4):
            scaled = centred[...] * (1.0 + terms[step * 4 + j, 2:3, :])
            rows[step % 2, j * chans : (j + 1) * chans, :] = scaled.astype(BF16)
        for c in range(3):
            turned = dot(rows[step % 2], w_qkv[c]).T.astype(BF16)
            inward[2 * step, c * head : (c + 1) * head, :] = turned[:, : 2 * chans]
            inward[2 * step + 1, c * head : (c + 1) * head, :] = turned[:, 2 * chans :]


def select_kernel(
    table, latents, pack_docs, w_in, terms, w_qkv,
    sent, rest, inward,
    latents_v, packs_v, rest_v, lowered_v, chosen_v, sems, out_sems,
    w_in_v, terms_v, w_qkv_v, centred, line_rows, inward_v, fold_sems,
):
    early = first_core()
    folds = [(w_in, w_in_v), (terms, terms_v), (w_qkv, w_qkv_v)]
    times, rows, lanes = sent.shape
    chans = latents_v.shape[1]
    owners, count, piece = table.shape
    copies = fetch([(latents, latents_v), (pack_docs, packs_v)], sems)

    @pl.when(early)
    def _():
        fetch(folds, fold_sems)

    copies[0].wait()
    values = latents_v[0]
    high = values.astype(BF16)
    lowered_v[...] = high
    rest_v[...] = values - high.astype(F32)
    left = fetch(
        [(rest_v, rest)] + [(lowered_v, sent.at[i, pl.ds(0, chans)]) for i in range(times)],
        out_sems,
    )
    copies[1].wait()
    column = jnp.broadcast_to(packs_v[...].astype(F32), (count, count))
    eye = lax.broadcasted_iota(jnp.int32, (count, count), 0) == lax.broadcasted_iota(
        jnp.int32, (count, count), 1
    )
    column = jnp.sum(jnp.where(eye, column, 0.0), axis=1, keepdims=True)
    places = lax.broadcasted_iota(jnp.int32, (count, owners * count), 1).astype(F32)
    pick = jnp.where(places == column, 1.0, 0.0)
    pick = stack_rows(pick, jnp.zeros_like(pick))
    chosen = dot(pick, table[...].reshape(owners * count, piece))[:count]
    tail = jnp.concatenate(
        [chosen[:, lanes:], jnp.zeros((count, 2 * lanes - piece), F32)], axis=1
    )
    chosen_v[...] = stack_rows(chosen[:, :lanes], tail)
    left += fetch(
        [(chosen_v, sent.at[i, pl.ds(chans, 2 * count)]) for i in range(times)],
        out_sems.at[pl.ds(1 + times, times)],
    )

    @pl.when(early)
    def _():
        for i, (source, target) in enumerate(folds):
            pltpu.make_async_copy(source, target, fold_sems.at[i]).wait()
        centred[...] = centre(w_in_v[...].astype(F32))
        fold_inward(centred, terms_v, w_qkv_v, line_rows, inward_v)
        fetch([(inward_v, inward)], fold_sems)[0].wait()

    for copy in left:
        copy.wait()


def small_rows(times, chans, head, tokens, count):
    sizes = [
        ("query_gain", head), ("key_gain", head), ("bias", tokens), ("member", count),
        ("direct", chans), ("earlier", chans), ("cross", times), ("shifts", 3 * times),
        ("rest", chans), ("weights", times),
    ]
    places, at = {}, 0
    for name, rows in sizes:
        places[name] = (at, at + rows)
        at += rows
    return places, at


def weights_kernel(
    here, steps, terms, w_in, w_qkv, w_final, w_proj, query_gain, key_gain, segments, rest,
    begun, inward, outward, lines, gram, small,
    terms_v, w_in_v, w_qkv_v, w_final_v, w_proj_v, gains_v, segments_v, rest_v,
    centred, pieces, rows, inward_v, outward_v, lines_v, gram_v, small_v, sems, out_sems,
):
    del begun
    times, chans, head = outward.shape
    tokens, count = segments_v.shape[1], 8
    wide = w_in_v.shape[1]
    places, _ = small_rows(times, chans, head, tokens, count)
    copies = fetch(
        [
            (w_in, w_in_v), (terms, terms_v), (w_qkv, w_qkv_v), (w_final, w_final_v),
            (w_proj, w_proj_v), (query_gain, gains_v.at[0]), (key_gain, gains_v.at[1]),
            (segments, segments_v), (rest, rest_v),
        ],
        sems,
    )
    copies[0].wait()
    centred[...] = centre(w_in_v[...].astype(F32))
    high, low = two_parts(centred[...])
    pieces[:chans, :] = high
    pieces[chans:, :] = low
    copies[1].wait()
    copies[2].wait()
    left = []

    @pl.when(jnp.logical_not(first_core()))
    def _():
        fold_inward(centred, terms_v, w_qkv_v, rows, inward_v)
        fetch([(inward_v, inward)], out_sems)[0].wait()

    copies[3].wait()
    copies[4].wait()
    for step in range(times // 4):
        for j in range(4):
            gated = w_final_v[...].astype(F32) * terms_v[step * 4 + j, 3:4, :]
            rows[step % 2, j * chans : (j + 1) * chans, :] = gated.astype(BF16)
        back = dot(rows[step % 2], w_proj_v[...], NT)
        for j in range(4):
            t = step * 4 + j
            outward_v[t] = (back[j * chans : (j + 1) * chans] * steps[t]).astype(BF16)
    left += fetch([(outward_v, outward)], out_sems.at[pl.ds(1, 1)])
    moved, means = [], []
    past = jnp.zeros((1, wide), F32)
    for t in range(times):
        moved.append(terms_v[t, 1:2, :])
        means.append(centre(terms_v[t, 0:1, :]))
        lines_v[times + t : times + t + 1, :] = 1.0 + terms_v[t, 2:3, :]
        past = past + jnp.where(t < here[0], steps[t], 0.0) * terms_v[t, 0:1, :]
    moved, means = jnp.concatenate(moved, axis=0), jnp.concatenate(means, axis=0)
    lines_v[:times, :] = means
    left += fetch([(lines_v, lines)], out_sems.at[pl.ds(2, 1)])

    def put(name, values):
        first, last = places[name]
        small_v[first:last, :] = jnp.concatenate(
            [values, jnp.zeros((values.shape[0], small_v.shape[1] - values.shape[1]), F32)], axis=1
        ) if values.shape[1] < small_v.shape[1] else values

    both = pieces[...]
    square = dot(both, both, NT)
    square = square[:chans, :chans] + square[chans:, :chans] + square[:chans, chans:]
    high, low = two_parts(square)
    gram_v[:chans, :] = high
    gram_v[chans:, :] = low
    left += fetch([(gram_v, gram)], out_sems.at[pl.ds(3, 1)])
    high, low = two_parts(means)
    mixed = dot(stack_rows(high, low), both, NT)
    put("cross", mixed[:times, :chans] + mixed[times:, :chans] + mixed[:times, chans:])
    high, low = two_parts(moved)
    split = stack_rows(high, low)
    shifts = []
    for c in range(3):
        shift = dot(split, w_qkv_v[c])
        shifts.append(shift[:times] + shift[times:])
    put("shifts", jnp.concatenate(shifts, axis=0))
    final = w_final_v[...]
    put("direct", dot(final, w_in_v[...], NT))
    high = past.astype(BF16)
    middle, low = two_parts(past - high.astype(F32))
    parts = stack_rows(high, middle, low, jnp.zeros((5, wide), F32))
    earlier = jnp.sum(dot(final, parts, NT), axis=-1, keepdims=True)
    put("earlier", jnp.broadcast_to(earlier, (chans, small_v.shape[1])))
    for copy in copies[5:]:
        copy.wait()
    put("query_gain", jnp.broadcast_to(gains_v[0] * (head**-0.5 * LOG2E), (head, head)).T)
    put("key_gain", jnp.broadcast_to(gains_v[1], (head, head)).T)
    ids = jnp.broadcast_to(segments_v[...].astype(F32), (tokens, tokens))
    put("bias", jnp.where(ids == ids.T, 0.0, MASKED))
    numbers = lax.broadcasted_iota(jnp.int32, (count, tokens), 0).astype(F32)
    put("rest", jnp.where(here[0] == 0, rest_v[...], 0.0))
    ones = jnp.ones((1, tokens), F32)
    passed = [ones * jnp.where(t < here[0], steps[t], 0.0) for t in range(times)]
    put("weights", jnp.concatenate(passed, axis=0))
    put("member", jnp.where(numbers == ids[:count], 1.0, 0.0))
    left += fetch([(small_v, small)], out_sems.at[pl.ds(4, 1)])
    for copy in left:
        copy.wait()


def gather_documents(arrived, chans, count, piece):
    parts = []
    for i in range(arrived.shape[0]):
        block = arrived[i, chans:, :].astype(F32)
        parts.append(block[:count])
        parts.append(block[count:, : piece - block.shape[1]])
    return jnp.concatenate(parts, axis=1)


def heads_kernel(
    arrived,
    lines_h, w_in_h, w_final_h, w_qkv_h, gram_h, small_h, inward_h, outward_h,
    out, residual,
    lines, w_in, w_final, w_qkv, gram, small, inward, outward,
    rows, queries, keys, values, raised, mass, attended, sems,
):
    times, chans, head = outward.shape
    tokens = arrived.shape[2]
    count = (arrived.shape[1] - chans) // 2
    wide = w_in.shape[1]
    places, _ = small_rows(times, chans, head, tokens, count)
    copies = fetch(
        [
            (lines_h, lines), (w_in_h, w_in), (w_final_h, w_final), (w_qkv_h, w_qkv),
            (gram_h, gram), (small_h, small), (inward_h, inward), (outward_h, outward),
        ],
        sems,
    )

    def table(name, lanes=None):
        first, last = places[name]
        return small[first:last, :lanes]

    documents = gather_documents(arrived, chans, count, wide // times)
    exact = stack_rows(documents, jnp.zeros_like(documents))
    documents = centre(documents)
    copies[0].wait()
    powers = []
    for t in range(0, times, 2):
        pair = []
        for j in range(2):
            row = documents + lines[t + j : t + j + 1, :]
            powers.append(jnp.sum(row * row, axis=-1, keepdims=True))
            pair.append(row * lines[times + t + j : times + t + j + 1, :])
        rows[t * count : (t + 2) * count, :] = jnp.concatenate(pair, axis=0).astype(BF16)
    copies[1].wait()
    copies[2].wait()
    narrow = dot(w_final[...], exact, NT)[:, :count]
    high, low = two_parts(documents)
    near = dot(stack_rows(high, low), w_in[...], NT)
    near = near[:count] + near[count:]
    copies[3].wait()
    base = jnp.concatenate([dot(rows[...], w_qkv[c]) for c in range(3)], axis=1)
    for copy in copies[4:]:
        copy.wait()
    shifts = table("shifts")
    shifts = jnp.concatenate([shifts[c * times : (c + 1) * times] for c in range(3)], axis=1)
    turned = []
    for half in range(2):
        span = slice(half * 8 * count, (half + 1) * 8 * count)
        block = [base[span], shifts[half * 8 : (half + 1) * 8, :]]
        left = head - 8 * count - 8
        block.append(jnp.zeros((left, 3 * head), F32))
        turned.append(jnp.concatenate(block, axis=0).T.astype(BF16))

    belongs = table("member")
    cross = table("cross", chans)
    weights = table("weights")
    past = jnp.zeros((chans, tokens), F32)
    for t in range(times):
        past = past + weights[t : t + 1, :] * arrived[t, :chans, :].astype(F32)
    whole = jnp.sum(weights[:, :count], axis=0, keepdims=True)
    highest = lax.Precision.HIGHEST
    near_docs = dot(whole * narrow + table("earlier", count), belongs, NN, highest)
    first_rest = table("rest")
    residual[...] = (
        dot(table("direct", chans), past, NN, highest)
        + near_docs
        + arrived[0, :chans, :].astype(F32)
        + first_rest
    )

    scaled_low, rates = [], []
    for t in range(times):
        mixed = 2.0 * (near + cross[t : t + 1, :])
        high, low = two_parts(mixed)
        left = jnp.concatenate([gram[...], stack_rows(high, low)], axis=0)
        block = arrived[t, :chans, :]
        product = dot(left, block)
        both = product[:chans] + product[chans : 2 * chans]
        block = block.astype(F32)
        other = product[2 * chans : 2 * chans + count] + product[2 * chans + count :]
        spread = jnp.sum(both * block, axis=0, keepdims=True) + jnp.sum(
            belongs * (other + powers[t]), axis=0, keepdims=True
        )
        rate = lax.rsqrt(spread / wide + EPS)
        rates.append(rate)
        scaled_low.append((block * rate).astype(BF16))

    def unit(block, gain):
        power = jnp.mean(block * block, axis=0, keepdims=True)
        return block * (lax.rsqrt(power + EPS) * gain)

    empty = jnp.zeros((chans, tokens), BF16)
    for t in range(times):
        half, j = divmod(t, 8)
        left = jnp.concatenate([inward[t // 2], turned[half]], axis=1)
        first = [scaled_low[t], empty] if t % 2 == 0 else [empty, scaled_low[t]]
        ones = lax.broadcasted_iota(jnp.int32, (8, tokens), 0) == j
        second = [jnp.zeros((j * count, tokens), F32)] if j else []
        second.append(belongs * rates[t])
        if j < 7:
            second.append(jnp.zeros(((7 - j) * count, tokens), F32))
        second.append(jnp.where(ones, 1.0, 0.0))
        second.append(jnp.zeros((head - 8 * count - 8, tokens), F32))
        second = jnp.concatenate(second, axis=0).astype(BF16)
        right = jnp.concatenate(first + [second], axis=0)
        mixed = dot(left, right)
        queries[t] = unit(mixed[:head], table("query_gain")).astype(BF16)
        keys[t] = unit(mixed[head : 2 * head], table("key_gain")).astype(BF16).T
        values[t] = mixed[2 * head :].astype(BF16)
    for t in range(times):
        scores = dot(keys[t], queries[t]) + table("bias")
        powered = jnp.exp2(scores - jnp.max(scores, axis=0, keepdims=True))
        mass[t : t + 1, :] = 1.0 / jnp.sum(powered, axis=0, keepdims=True)
        raised[t] = powered.astype(BF16)
    for t in range(times):
        attended[t] = (dot(values[t], raised[t]) * mass[t : t + 1, :]).astype(BF16)
    out[0] = jnp.zeros((chans, tokens), BF16)
    total = first_rest
    for t in range(times - 1):
        total = total + dot(outward[t], attended[t])
        out[t + 1] = total.astype(BF16)


def select(table, latents, pack_docs, w_in, terms, w_qkv):
    block, count = latents.shape[1:], pack_docs.shape[1]
    times, (chans, wide), head = terms.shape[0], w_in.shape, w_qkv.shape[2]
    folded = ((times // 2, 3 * head, 2 * chans), BF16)
    return pl.pallas_call(
        select_kernel,
        out_shape=(
            pltpu.HBM((times, block[0] + 2 * count, block[1]), BF16),
            pltpu.HBM(block, F32),
            pltpu.HBM(*folded),
        ),
        in_specs=[VMEM] + [HBM] * 5,
        out_specs=(HBM,) * 3,
        scratch_shapes=[
            pltpu.VMEM(latents.shape, F32),
            pltpu.VMEM(pack_docs.shape, jnp.int32),
            pltpu.VMEM(block, F32),
            pltpu.VMEM(block, BF16),
            pltpu.VMEM((2 * count, block[1]), BF16),
            pltpu.SemaphoreType.DMA((2,)),
            pltpu.SemaphoreType.DMA((1 + 2 * times,)),
            pltpu.VMEM(w_in.shape, BF16),
            pltpu.VMEM(terms.shape, F32),
            pltpu.VMEM(w_qkv.shape, BF16),
            pltpu.VMEM(w_in.shape, F32),
            pltpu.VMEM((2, 4 * chans, wide), BF16),
            pltpu.VMEM(*folded),
            pltpu.SemaphoreType.DMA((3,)),
        ],
        compiler_params=PARAMS,
        name="select",
    )(table, *pinned(latents, pack_docs, w_in, terms, w_qkv))


def fold_weights(
    here, steps, terms, w_in, w_qkv, w_final, w_proj, query_gain, key_gain, segments, rest, inward
):
    times, wide = terms.shape[0], terms.shape[2]
    chans, head, tokens = w_final.shape[0], w_proj.shape[0], segments.shape[1]
    count = 8
    shapes = [
        ((times // 2, 3 * head, 2 * chans), BF16),
        ((times, chans, head), BF16),
        ((2 * times, wide), F32),
        ((2 * chans, chans), BF16),
        ((small_rows(times, chans, head, tokens, count)[1], tokens), F32),
    ]
    return pl.pallas_call(
        weights_kernel,
        out_shape=tuple(pltpu.HBM(*s) for s in shapes),
        in_specs=[SMEM] * 2 + [HBM] * 10,
        out_specs=(HBM,) * 5,
        input_output_aliases={11: 0},
        scratch_shapes=[
            pltpu.VMEM(a.shape, a.dtype) for a in (terms, w_in, w_qkv, w_final, w_proj)
        ]
        + [
            pltpu.VMEM((2,) + query_gain.shape, F32),
            pltpu.VMEM(segments.shape, jnp.int32),
            pltpu.VMEM(rest.shape, F32),
            pltpu.VMEM((chans, wide), F32),
            pltpu.VMEM((2 * chans, wide), BF16),
            pltpu.VMEM((2, 4 * chans, wide), BF16),
        ]
        + [pltpu.VMEM(*s) for s in shapes]
        + [pltpu.SemaphoreType.DMA((9,)), pltpu.SemaphoreType.DMA((5,))],
        compiler_params=PARAMS,
        name="fold_weights",
    )(
        here,
        steps,
        *pinned(terms, w_in, w_qkv, w_final, w_proj, query_gain, key_gain, segments, rest, inward),
    )


def run_heads(arrived, *operands):
    outward = operands[-1]
    times, chans, head = outward.shape
    tokens = arrived.shape[2]
    rows = times * (arrived.shape[1] - chans) // 2
    wide = operands[0].shape[1]
    square = pltpu.VMEM((times, head, tokens), BF16)
    return pl.pallas_call(
        heads_kernel,
        out_shape=(
            jax.ShapeDtypeStruct((times, chans, tokens), BF16),
            jax.ShapeDtypeStruct((chans, tokens), F32),
        ),
        in_specs=[VMEM] + [HBM] * len(operands),
        out_specs=(VMEM, VMEM),
        scratch_shapes=[pltpu.VMEM(a.shape, a.dtype) for a in operands]
        + [
            pltpu.VMEM((rows, wide), BF16),
            square, square, square, square,
            pltpu.VMEM((times, tokens), F32),
            square,
            pltpu.SemaphoreType.DMA((len(operands),)),
        ],
        compiler_params=PARAMS,
        name="run_heads",
    )(arrived, *pinned(*operands))


def local(
    latents,
    time_terms,
    step_sizes,
    doc_embed,
    pack_docs,
    segment_ids,
    w_in,
    w_qkv,
    query_gain,
    key_gain,
    w_proj,
    w_final,
):
    here = lax.axis_index("tm")
    place = here.astype(jnp.int32).reshape(1)
    owners = lax.axis_size("req")
    count, piece = doc_embed.shape
    w_heads = w_qkv[:, :, 0, :].transpose(1, 0, 2)
    w_last = w_final.T

    copies = jnp.broadcast_to(doc_embed[None], (owners, count, piece))
    table = lax.all_to_all(copies, "req", 0, 0)
    sent, rest, inward = select(
        table, latents, pack_docs[None], w_in, time_terms, w_heads
    )
    arrived = lax.all_to_all(sent, "tm", 0, 0)
    inward, outward, lines, gram, small = fold_weights(
        place, step_sizes, time_terms, w_in, w_heads, w_last, w_proj[0], query_gain, key_gain,
        segment_ids, rest, inward,
    )
    sums, residual = run_heads(
        arrived, lines, w_in, w_last, w_heads, gram, small, inward, outward
    )
    parts = lax.all_to_all(sums, "tm", 0, 0)
    return (residual + jnp.sum(parts.astype(F32), axis=0))[None]


def solution(mesh):
    in_specs = (
        P("tm", None, "req"),
        P(),
        P(),
        P("req", "tm"),
        P("req"),
        P("req", None),
        P(),
        P(None, None, "tm", None),
        P("tm", None),
        P("tm", None),
        P("tm", None, None),
        P(),
    )
    out_specs = P("tm", None, "req")
    return jax.shard_map(local, mesh=mesh, in_specs=in_specs, out_specs=out_specs, check_vma=False)
```

```python
import jax
import jax.numpy as jnp
from jax import lax
from jax.experimental import pallas as pl
from jax.experimental.pallas import tpu as pltpu
from jax.sharding import PartitionSpec as P

EPS = 1e-06
EARLY = 3
MASKED = -1e30
LOG2E = 1.4426950408889634
BF16, F32 = jnp.bfloat16, jnp.float32
NN = (((1,), (0,)), ((), ()))
NT = (((1,), (1,)), ((), ()))
VMEM = pl.BlockSpec(memory_space=pltpu.VMEM)
SMEM = pl.BlockSpec(memory_space=pltpu.SMEM)
HBM = pl.BlockSpec(memory_space=pltpu.HBM)
PARAMS = pltpu.CompilerParams(vmem_limit_bytes=24 * 2**20)


def dot(left, right, dims=NN, precision=None):
    return lax.dot_general(left, right, dims, precision=precision, preferred_element_type=F32)


def two_parts(values):
    high = values.astype(BF16)
    return high, (values - high.astype(F32)).astype(BF16)


def stack_rows(*parts):
    return jnp.concatenate([p.astype(F32) for p in parts], axis=0).astype(BF16)


def centre(values):
    return values - jnp.mean(values, axis=-1, keepdims=True)


def pinned(*arrays):
    return tuple(pltpu.with_memory_space_constraint(a, pltpu.HBM) for a in arrays)


def fetch(pairs, sems):
    copies = [pltpu.make_async_copy(a, b, sems.at[i]) for i, (a, b) in enumerate(pairs)]
    for copy in copies:
        copy.start()
    return copies


def first_core():
    return lax.rem(lax.axis_index("req"), 2) == 0


def fold_inward(steps, centred, terms, w_qkv, rows, inward):
    chans, head = centred.shape[0], w_qkv.shape[2]
    for step in steps:
        for j in range(4):
            scaled = centred[...] * (1.0 + terms[step * 4 + j, 2:3, :])
            rows[step % 2, j * chans : (j + 1) * chans, :] = scaled.astype(BF16)
        for c in range(3):
            turned = dot(rows[step % 2], w_qkv[c]).T.astype(BF16)
            inward[2 * step, c * head : (c + 1) * head, :] = turned[:, : 2 * chans]
            inward[2 * step + 1, c * head : (c + 1) * head, :] = turned[:, 2 * chans :]


def select_kernel(
    table, latents, pack_docs, w_in, terms, w_qkv,
    sent, rest, inward,
    latents_v, packs_v, rest_v, lowered_v, chosen_v, sems, out_sems,
    w_in_v, terms_v, w_qkv_v, centred, line_rows, inward_v, fold_sems,
):
    early = first_core()
    folds = [(w_in, w_in_v), (terms, terms_v), (w_qkv, w_qkv_v)]
    times, rows, lanes = sent.shape
    chans = latents_v.shape[1]
    owners, count, piece = table.shape
    copies = fetch([(latents, latents_v), (pack_docs, packs_v)], sems)

    @pl.when(early)
    def _():
        fetch(folds, fold_sems)

    copies[0].wait()
    values = latents_v[0]
    high = values.astype(BF16)
    lowered_v[...] = high
    rest_v[...] = values - high.astype(F32)
    left = fetch(
        [(rest_v, rest)] + [(lowered_v, sent.at[i, pl.ds(0, chans)]) for i in range(times)],
        out_sems,
    )
    copies[1].wait()
    column = jnp.broadcast_to(packs_v[...].astype(F32), (count, count))
    eye = lax.broadcasted_iota(jnp.int32, (count, count), 0) == lax.broadcasted_iota(
        jnp.int32, (count, count), 1
    )
    column = jnp.sum(jnp.where(eye, column, 0.0), axis=1, keepdims=True)
    places = lax.broadcasted_iota(jnp.int32, (count, owners * count), 1).astype(F32)
    pick = jnp.where(places == column, 1.0, 0.0)
    pick = stack_rows(pick, jnp.zeros_like(pick))
    chosen = dot(pick, table[...].reshape(owners * count, piece))[:count]
    tail = jnp.concatenate(
        [chosen[:, lanes:], jnp.zeros((count, 2 * lanes - piece), F32)], axis=1
    )
    chosen_v[...] = stack_rows(chosen[:, :lanes], tail)
    left += fetch(
        [(chosen_v, sent.at[i, pl.ds(chans, 2 * count)]) for i in range(times)],
        out_sems.at[pl.ds(1 + times, times)],
    )

    @pl.when(early)
    def _():
        for i, (source, target) in enumerate(folds):
            pltpu.make_async_copy(source, target, fold_sems.at[i]).wait()
        centred[...] = centre(w_in_v[...].astype(F32))
        fold_inward(range(EARLY), centred, terms_v, w_qkv_v, line_rows, inward_v)
        done = pl.ds(0, 2 * EARLY)
        fetch([(inward_v.at[done], inward.at[done])], fold_sems)[0].wait()

    for copy in left:
        copy.wait()


def small_rows(times, chans, head, tokens, count):
    sizes = [
        ("query_gain", head), ("key_gain", head), ("bias", tokens), ("member", count),
        ("direct", chans), ("earlier", chans), ("cross", times), ("shifts", 3 * times),
        ("rest", chans), ("weights", times),
    ]
    places, at = {}, 0
    for name, rows in sizes:
        places[name] = (at, at + rows)
        at += rows
    return places, at


def weights_kernel(
    here, steps, terms, w_in, w_qkv, w_final, w_proj, query_gain, key_gain, segments, rest,
    begun, inward, outward, lines, gram, small,
    terms_v, w_in_v, w_qkv_v, w_final_v, w_proj_v, gains_v, segments_v, rest_v,
    centred, pieces, rows, inward_v, outward_v, lines_v, gram_v, small_v, sems, out_sems,
):
    del begun
    times, chans, head = outward.shape
    tokens, count = segments_v.shape[1], 8
    wide = w_in_v.shape[1]
    places, _ = small_rows(times, chans, head, tokens, count)
    copies = fetch(
        [
            (w_in, w_in_v), (terms, terms_v), (w_qkv, w_qkv_v), (w_final, w_final_v),
            (w_proj, w_proj_v), (query_gain, gains_v.at[0]), (key_gain, gains_v.at[1]),
            (segments, segments_v), (rest, rest_v),
        ],
        sems,
    )
    copies[0].wait()
    centred[...] = centre(w_in_v[...].astype(F32))
    high, low = two_parts(centred[...])
    pieces[:chans, :] = high
    pieces[chans:, :] = low
    copies[1].wait()
    copies[2].wait()
    left = []

    @pl.when(first_core())
    def _():
        fold_inward(range(EARLY, times // 4), centred, terms_v, w_qkv_v, rows, inward_v)
        done = pl.ds(2 * EARLY, times // 2 - 2 * EARLY)
        fetch([(inward_v.at[done], inward.at[done])], out_sems)[0].wait()

    @pl.when(jnp.logical_not(first_core()))
    def _():
        fold_inward(range(times // 4), centred, terms_v, w_qkv_v, rows, inward_v)
        fetch([(inward_v, inward)], out_sems)[0].wait()

    copies[3].wait()
    copies[4].wait()
    for step in range(times // 4):
        for j in range(4):
            gated = w_final_v[...].astype(F32) * terms_v[step * 4 + j, 3:4, :]
            rows[step % 2, j * chans : (j + 1) * chans, :] = gated.astype(BF16)
        back = dot(rows[step % 2], w_proj_v[...], NT)
        for j in range(4):
            t = step * 4 + j
            outward_v[t] = (back[j * chans : (j + 1) * chans] * steps[t]).astype(BF16)
    left += fetch([(outward_v, outward)], out_sems.at[pl.ds(1, 1)])
    moved, means = [], []
    past = jnp.zeros((1, wide), F32)
    for t in range(times):
        moved.append(terms_v[t, 1:2, :])
        means.append(centre(terms_v[t, 0:1, :]))
        lines_v[times + t : times + t + 1, :] = 1.0 + terms_v[t, 2:3, :]
        past = past + jnp.where(t < here[0], steps[t], 0.0) * terms_v[t, 0:1, :]
    moved, means = jnp.concatenate(moved, axis=0), jnp.concatenate(means, axis=0)
    lines_v[:times, :] = means
    left += fetch([(lines_v, lines)], out_sems.at[pl.ds(2, 1)])

    def put(name, values):
        first, last = places[name]
        small_v[first:last, :] = jnp.concatenate(
            [values, jnp.zeros((values.shape[0], small_v.shape[1] - values.shape[1]), F32)], axis=1
        ) if values.shape[1] < small_v.shape[1] else values

    both = pieces[...]
    square = dot(both, both, NT)
    square = square[:chans, :chans] + square[chans:, :chans] + square[:chans, chans:]
    high, low = two_parts(square)
    gram_v[:chans, :] = high
    gram_v[chans:, :] = low
    left += fetch([(gram_v, gram)], out_sems.at[pl.ds(3, 1)])
    high, low = two_parts(means)
    mixed = dot(stack_rows(high, low), both, NT)
    put("cross", mixed[:times, :chans] + mixed[times:, :chans] + mixed[:times, chans:])
    high, low = two_parts(moved)
    split = stack_rows(high, low)
    shifts = []
    for c in range(3):
        shift = dot(split, w_qkv_v[c])
        shifts.append(shift[:times] + shift[times:])
    put("shifts", jnp.concatenate(shifts, axis=0))
    final = w_final_v[...]
    put("direct", dot(final, w_in_v[...], NT))
    high = past.astype(BF16)
    middle, low = two_parts(past - high.astype(F32))
    parts = stack_rows(high, middle, low, jnp.zeros((5, wide), F32))
    earlier = jnp.sum(dot(final, parts, NT), axis=-1, keepdims=True)
    put("earlier", jnp.broadcast_to(earlier, (chans, small_v.shape[1])))
    for copy in copies[5:]:
        copy.wait()
    put("query_gain", jnp.broadcast_to(gains_v[0] * (head**-0.5 * LOG2E), (head, head)).T)
    put("key_gain", jnp.broadcast_to(gains_v[1], (head, head)).T)
    ids = jnp.broadcast_to(segments_v[...].astype(F32), (tokens, tokens))
    put("bias", jnp.where(ids == ids.T, 0.0, MASKED))
    numbers = lax.broadcasted_iota(jnp.int32, (count, tokens), 0).astype(F32)
    put("rest", jnp.where(here[0] == 0, rest_v[...], 0.0))
    ones = jnp.ones((1, tokens), F32)
    passed = [ones * jnp.where(t < here[0], steps[t], 0.0) for t in range(times)]
    put("weights", jnp.concatenate(passed, axis=0))
    put("member", jnp.where(numbers == ids[:count], 1.0, 0.0))
    left += fetch([(small_v, small)], out_sems.at[pl.ds(4, 1)])
    for copy in left:
        copy.wait()


def gather_documents(arrived, chans, count, piece):
    parts = []
    for i in range(arrived.shape[0]):
        block = arrived[i, chans:, :].astype(F32)
        parts.append(block[:count])
        parts.append(block[count:, : piece - block.shape[1]])
    return jnp.concatenate(parts, axis=1)


def heads_kernel(
    arrived,
    lines_h, w_in_h, w_final_h, w_qkv_h, gram_h, small_h, inward_h, outward_h,
    out, residual,
    lines, w_in, w_final, w_qkv, gram, small, inward, outward,
    rows, queries, keys, values, raised, mass, attended, sems,
):
    times, chans, head = outward.shape
    tokens = arrived.shape[2]
    count = (arrived.shape[1] - chans) // 2
    wide = w_in.shape[1]
    places, _ = small_rows(times, chans, head, tokens, count)
    copies = fetch(
        [
            (lines_h, lines), (w_in_h, w_in), (w_final_h, w_final), (w_qkv_h, w_qkv),
            (gram_h, gram), (small_h, small), (inward_h, inward), (outward_h, outward),
        ],
        sems,
    )

    def table(name, lanes=None):
        first, last = places[name]
        return small[first:last, :lanes]

    documents = gather_documents(arrived, chans, count, wide // times)
    exact = stack_rows(documents, jnp.zeros_like(documents))
    documents = centre(documents)
    copies[0].wait()
    powers = []
    for t in range(0, times, 2):
        pair = []
        for j in range(2):
            row = documents + lines[t + j : t + j + 1, :]
            powers.append(jnp.sum(row * row, axis=-1, keepdims=True))
            pair.append(row * lines[times + t + j : times + t + j + 1, :])
        rows[t * count : (t + 2) * count, :] = jnp.concatenate(pair, axis=0).astype(BF16)
    copies[1].wait()
    copies[2].wait()
    narrow = dot(w_final[...], exact, NT)[:, :count]
    high, low = two_parts(documents)
    near = dot(stack_rows(high, low), w_in[...], NT)
    near = near[:count] + near[count:]
    copies[3].wait()
    base = jnp.concatenate([dot(rows[...], w_qkv[c]) for c in range(3)], axis=1)
    for copy in copies[4:]:
        copy.wait()
    shifts = table("shifts")
    shifts = jnp.concatenate([shifts[c * times : (c + 1) * times] for c in range(3)], axis=1)
    turned = []
    for half in range(2):
        span = slice(half * 8 * count, (half + 1) * 8 * count)
        block = [base[span], shifts[half * 8 : (half + 1) * 8, :]]
        left = head - 8 * count - 8
        block.append(jnp.zeros((left, 3 * head), F32))
        turned.append(jnp.concatenate(block, axis=0).T.astype(BF16))

    belongs = table("member")
    cross = table("cross", chans)
    weights = table("weights")
    past = jnp.zeros((chans, tokens), F32)
    for t in range(times):
        past = past + weights[t : t + 1, :] * arrived[t, :chans, :].astype(F32)
    whole = jnp.sum(weights[:, :count], axis=0, keepdims=True)
    highest = lax.Precision.HIGHEST
    near_docs = dot(whole * narrow + table("earlier", count), belongs, NN, highest)
    first_rest = table("rest")
    residual[...] = (
        dot(table("direct", chans), past, NN, highest)
        + near_docs
        + arrived[0, :chans, :].astype(F32)
        + first_rest
    )

    scaled_low, rates = [], []
    for t in range(times):
        mixed = 2.0 * (near + cross[t : t + 1, :])
        high, low = two_parts(mixed)
        left = jnp.concatenate([gram[...], stack_rows(high, low)], axis=0)
        block = arrived[t, :chans, :]
        product = dot(left, block)
        both = product[:chans] + product[chans : 2 * chans]
        block = block.astype(F32)
        other = product[2 * chans : 2 * chans + count] + product[2 * chans + count :]
        spread = jnp.sum(both * block, axis=0, keepdims=True) + jnp.sum(
            belongs * (other + powers[t]), axis=0, keepdims=True
        )
        rate = lax.rsqrt(spread / wide + EPS)
        rates.append(rate)
        scaled_low.append((block * rate).astype(BF16))

    def unit(block, gain):
        power = jnp.mean(block * block, axis=0, keepdims=True)
        return block * (lax.rsqrt(power + EPS) * gain)

    empty = jnp.zeros((chans, tokens), BF16)
    for t in range(times):
        half, j = divmod(t, 8)
        left = jnp.concatenate([inward[t // 2], turned[half]], axis=1)
        first = [scaled_low[t], empty] if t % 2 == 0 else [empty, scaled_low[t]]
        ones = lax.broadcasted_iota(jnp.int32, (8, tokens), 0) == j
        second = [jnp.zeros((j * count, tokens), F32)] if j else []
        second.append(belongs * rates[t])
        if j < 7:
            second.append(jnp.zeros(((7 - j) * count, tokens), F32))
        second.append(jnp.where(ones, 1.0, 0.0))
        second.append(jnp.zeros((head - 8 * count - 8, tokens), F32))
        second = jnp.concatenate(second, axis=0).astype(BF16)
        right = jnp.concatenate(first + [second], axis=0)
        mixed = dot(left, right)
        queries[t] = unit(mixed[:head], table("query_gain")).astype(BF16)
        keys[t] = unit(mixed[head : 2 * head], table("key_gain")).astype(BF16).T
        values[t] = mixed[2 * head :].astype(BF16)
    for t in range(times):
        scores = dot(keys[t], queries[t]) + table("bias")
        powered = jnp.exp2(scores - jnp.max(scores, axis=0, keepdims=True))
        mass[t : t + 1, :] = 1.0 / jnp.sum(powered, axis=0, keepdims=True)
        raised[t] = powered.astype(BF16)
    for t in range(times):
        attended[t] = (dot(values[t], raised[t]) * mass[t : t + 1, :]).astype(BF16)
    out[0] = jnp.zeros((chans, tokens), BF16)
    total = first_rest
    for t in range(times - 1):
        total = total + dot(outward[t], attended[t])
        out[t + 1] = total.astype(BF16)


def select(table, latents, pack_docs, w_in, terms, w_qkv):
    block, count = latents.shape[1:], pack_docs.shape[1]
    times, (chans, wide), head = terms.shape[0], w_in.shape, w_qkv.shape[2]
    folded = ((times // 2, 3 * head, 2 * chans), BF16)
    return pl.pallas_call(
        select_kernel,
        out_shape=(
            pltpu.HBM((times, block[0] + 2 * count, block[1]), BF16),
            pltpu.HBM(block, F32),
            pltpu.HBM(*folded),
        ),
        in_specs=[VMEM] + [HBM] * 5,
        out_specs=(HBM,) * 3,
        scratch_shapes=[
            pltpu.VMEM(latents.shape, F32),
            pltpu.VMEM(pack_docs.shape, jnp.int32),
            pltpu.VMEM(block, F32),
            pltpu.VMEM(block, BF16),
            pltpu.VMEM((2 * count, block[1]), BF16),
            pltpu.SemaphoreType.DMA((2,)),
            pltpu.SemaphoreType.DMA((1 + 2 * times,)),
            pltpu.VMEM(w_in.shape, BF16),
            pltpu.VMEM(terms.shape, F32),
            pltpu.VMEM(w_qkv.shape, BF16),
            pltpu.VMEM(w_in.shape, F32),
            pltpu.VMEM((2, 4 * chans, wide), BF16),
            pltpu.VMEM(*folded),
            pltpu.SemaphoreType.DMA((3,)),
        ],
        compiler_params=PARAMS,
        name="select",
    )(table, *pinned(latents, pack_docs, w_in, terms, w_qkv))


def fold_weights(
    here, steps, terms, w_in, w_qkv, w_final, w_proj, query_gain, key_gain, segments, rest, inward
):
    times, wide = terms.shape[0], terms.shape[2]
    chans, head, tokens = w_final.shape[0], w_proj.shape[0], segments.shape[1]
    count = 8
    shapes = [
        ((times // 2, 3 * head, 2 * chans), BF16),
        ((times, chans, head), BF16),
        ((2 * times, wide), F32),
        ((2 * chans, chans), BF16),
        ((small_rows(times, chans, head, tokens, count)[1], tokens), F32),
    ]
    return pl.pallas_call(
        weights_kernel,
        out_shape=tuple(pltpu.HBM(*s) for s in shapes),
        in_specs=[SMEM] * 2 + [HBM] * 10,
        out_specs=(HBM,) * 5,
        input_output_aliases={11: 0},
        scratch_shapes=[
            pltpu.VMEM(a.shape, a.dtype) for a in (terms, w_in, w_qkv, w_final, w_proj)
        ]
        + [
            pltpu.VMEM((2,) + query_gain.shape, F32),
            pltpu.VMEM(segments.shape, jnp.int32),
            pltpu.VMEM(rest.shape, F32),
            pltpu.VMEM((chans, wide), F32),
            pltpu.VMEM((2 * chans, wide), BF16),
            pltpu.VMEM((2, 4 * chans, wide), BF16),
        ]
        + [pltpu.VMEM(*s) for s in shapes]
        + [pltpu.SemaphoreType.DMA((9,)), pltpu.SemaphoreType.DMA((5,))],
        compiler_params=PARAMS,
        name="fold_weights",
    )(
        here,
        steps,
        *pinned(terms, w_in, w_qkv, w_final, w_proj, query_gain, key_gain, segments, rest, inward),
    )


def run_heads(arrived, *operands):
    outward = operands[-1]
    times, chans, head = outward.shape
    tokens = arrived.shape[2]
    rows = times * (arrived.shape[1] - chans) // 2
    wide = operands[0].shape[1]
    square = pltpu.VMEM((times, head, tokens), BF16)
    return pl.pallas_call(
        heads_kernel,
        out_shape=(
            jax.ShapeDtypeStruct((times, chans, tokens), BF16),
            jax.ShapeDtypeStruct((chans, tokens), F32),
        ),
        in_specs=[VMEM] + [HBM] * len(operands),
        out_specs=(VMEM, VMEM),
        scratch_shapes=[pltpu.VMEM(a.shape, a.dtype) for a in operands]
        + [
            pltpu.VMEM((rows, wide), BF16),
            square, square, square, square,
            pltpu.VMEM((times, tokens), F32),
            square,
            pltpu.SemaphoreType.DMA((len(operands),)),
        ],
        compiler_params=PARAMS,
        name="run_heads",
    )(arrived, *pinned(*operands))


def local(
    latents,
    time_terms,
    step_sizes,
    doc_embed,
    pack_docs,
    segment_ids,
    w_in,
    w_qkv,
    query_gain,
    key_gain,
    w_proj,
    w_final,
):
    here = lax.axis_index("tm")
    place = here.astype(jnp.int32).reshape(1)
    owners = lax.axis_size("req")
    count, piece = doc_embed.shape
    w_heads = w_qkv[:, :, 0, :].transpose(1, 0, 2)
    w_last = w_final.T

    copies = jnp.broadcast_to(doc_embed[None], (owners, count, piece))
    table = lax.all_to_all(copies, "req", 0, 0)
    sent, rest, inward = select(
        table, latents, pack_docs[None], w_in, time_terms, w_heads
    )
    arrived = lax.all_to_all(sent, "tm", 0, 0)
    inward, outward, lines, gram, small = fold_weights(
        place, step_sizes, time_terms, w_in, w_heads, w_last, w_proj[0], query_gain, key_gain,
        segment_ids, rest, inward,
    )
    sums, residual = run_heads(
        arrived, lines, w_in, w_last, w_heads, gram, small, inward, outward
    )
    parts = lax.all_to_all(sums, "tm", 0, 0)
    return (residual + jnp.sum(parts.astype(F32), axis=0))[None]


def solution(mesh):
    in_specs = (
        P("tm", None, "req"),
        P(),
        P(),
        P("req", "tm"),
        P("req"),
        P("req", None),
        P(),
        P(None, None, "tm", None),
        P("tm", None),
        P("tm", None),
        P("tm", None, None),
        P(),
    )
    out_specs = P("tm", None, "req")
    return jax.shard_map(local, mesh=mesh, in_specs=in_specs, out_specs=out_specs, check_vma=False)
```

```python
import jax
import jax.numpy as jnp
from jax import lax
from jax.experimental import pallas as pl
from jax.experimental.pallas import tpu as pltpu
from jax.sharding import PartitionSpec as P

EPS = 1e-06
EARLY = 3
MASKED = -1e30
LOG2E = 1.4426950408889634
BF16, F32 = jnp.bfloat16, jnp.float32
NN = (((1,), (0,)), ((), ()))
NT = (((1,), (1,)), ((), ()))
VMEM = pl.BlockSpec(memory_space=pltpu.VMEM)
SMEM = pl.BlockSpec(memory_space=pltpu.SMEM)
HBM = pl.BlockSpec(memory_space=pltpu.HBM)
PARAMS = pltpu.CompilerParams(vmem_limit_bytes=24 * 2**20)


def dot(left, right, dims=NN, precision=None):
    return lax.dot_general(left, right, dims, precision=precision, preferred_element_type=F32)


def two_parts(values):
    high = values.astype(BF16)
    return high, (values - high.astype(F32)).astype(BF16)


def stack_rows(*parts):
    return jnp.concatenate([p.astype(F32) for p in parts], axis=0).astype(BF16)


def centre(values):
    return values - jnp.mean(values, axis=-1, keepdims=True)


def pinned(*arrays):
    return tuple(pltpu.with_memory_space_constraint(a, pltpu.HBM) for a in arrays)


def fetch(pairs, sems):
    copies = [pltpu.make_async_copy(a, b, sems.at[i]) for i, (a, b) in enumerate(pairs)]
    for copy in copies:
        copy.start()
    return copies


def first_core():
    return lax.rem(lax.axis_index("req"), 2) == 0


def fold_inward(steps, centred, terms, w_qkv, rows, inward):
    chans, head = centred.shape[0], w_qkv.shape[2]
    for step in steps:
        for j in range(4):
            scaled = centred[...] * (1.0 + terms[step * 4 + j, 2:3, :])
            rows[step % 2, j * chans : (j + 1) * chans, :] = scaled.astype(BF16)
        for c in range(3):
            turned = dot(rows[step % 2], w_qkv[c]).T.astype(BF16)
            inward[2 * step, c * head : (c + 1) * head, :] = turned[:, : 2 * chans]
            inward[2 * step + 1, c * head : (c + 1) * head, :] = turned[:, 2 * chans :]


def select_kernel(
    table, latents, pack_docs, w_in, terms, w_qkv,
    sent, rest, inward,
    latents_v, packs_v, rest_v, lowered_v, chosen_v, sems, out_sems,
    w_in_v, terms_v, w_qkv_v, centred, line_rows, inward_v, fold_sems,
):
    early = first_core()
    folds = [(w_in, w_in_v), (terms, terms_v), (w_qkv, w_qkv_v)]
    times, rows, lanes = sent.shape
    chans = latents_v.shape[1]
    owners, count, piece = table.shape
    copies = fetch([(latents, latents_v), (pack_docs, packs_v)], sems)

    @pl.when(early)
    def _():
        fetch(folds, fold_sems)

    copies[0].wait()
    values = latents_v[0]
    high = values.astype(BF16)
    lowered_v[...] = high
    rest_v[...] = values - high.astype(F32)
    left = fetch(
        [(rest_v, rest)] + [(lowered_v, sent.at[i, pl.ds(0, chans)]) for i in range(times)],
        out_sems,
    )
    copies[1].wait()
    column = jnp.broadcast_to(packs_v[...].astype(F32), (count, count))
    eye = lax.broadcasted_iota(jnp.int32, (count, count), 0) == lax.broadcasted_iota(
        jnp.int32, (count, count), 1
    )
    column = jnp.sum(jnp.where(eye, column, 0.0), axis=1, keepdims=True)
    places = lax.broadcasted_iota(jnp.int32, (count, owners * count), 1).astype(F32)
    pick = jnp.where(places == column, 1.0, 0.0)
    pick = stack_rows(pick, jnp.zeros_like(pick))
    chosen = dot(pick, table[...].reshape(owners * count, piece))[:count]
    tail = jnp.concatenate(
        [chosen[:, lanes:], jnp.zeros((count, 2 * lanes - piece), F32)], axis=1
    )
    chosen_v[...] = stack_rows(chosen[:, :lanes], tail)
    left += fetch(
        [(chosen_v, sent.at[i, pl.ds(chans, 2 * count)]) for i in range(times)],
        out_sems.at[pl.ds(1 + times, times)],
    )

    @pl.when(early)
    def _():
        for i, (source, target) in enumerate(folds):
            pltpu.make_async_copy(source, target, fold_sems.at[i]).wait()
        centred[...] = centre(w_in_v[...].astype(F32))
        fold_inward(range(EARLY), centred, terms_v, w_qkv_v, line_rows, inward_v)
        done = pl.ds(0, 2 * EARLY)
        fetch([(inward_v.at[done], inward.at[done])], fold_sems)[0].wait()

    for copy in left:
        copy.wait()


def small_rows(times, chans, head, tokens, count):
    sizes = [
        ("query_gain", head), ("key_gain", head), ("bias", tokens), ("member", count),
        ("direct", chans), ("earlier", chans), ("cross", times), ("shifts", 3 * times),
        ("rest", chans), ("weights", times),
    ]
    places, at = {}, 0
    for name, rows in sizes:
        places[name] = (at, at + rows)
        at += rows
    return places, at


def weights_kernel(
    here, steps, terms, w_in, w_qkv, w_final, w_proj, query_gain, key_gain, segments, rest,
    begun, inward, outward, lines, gram, small,
    terms_v, w_in_v, w_qkv_v, w_final_v, w_proj_v, gains_v, segments_v, rest_v,
    centred, pieces, rows, inward_v, outward_v, lines_v, gram_v, small_v, sems, out_sems,
):
    del begun
    times, chans, head = outward.shape
    tokens, count = segments_v.shape[1], 8
    wide = w_in_v.shape[1]
    places, _ = small_rows(times, chans, head, tokens, count)
    copies = fetch(
        [
            (w_in, w_in_v), (terms, terms_v), (w_qkv, w_qkv_v), (w_final, w_final_v),
            (w_proj, w_proj_v), (query_gain, gains_v.at[0]), (key_gain, gains_v.at[1]),
            (segments, segments_v), (rest, rest_v),
        ],
        sems,
    )
    copies[0].wait()
    centred[...] = centre(w_in_v[...].astype(F32))
    high, low = two_parts(centred[...])
    pieces[:chans, :] = high
    pieces[chans:, :] = low
    copies[1].wait()
    copies[2].wait()
    left = []

    @pl.when(first_core())
    def _():
        fold_inward(range(EARLY, times // 4), centred, terms_v, w_qkv_v, rows, inward_v)
        done = pl.ds(2 * EARLY, times // 2 - 2 * EARLY)
        fetch([(inward_v.at[done], inward.at[done])], out_sems)[0].wait()

    @pl.when(jnp.logical_not(first_core()))
    def _():
        fold_inward(range(times // 4), centred, terms_v, w_qkv_v, rows, inward_v)
        fetch([(inward_v, inward)], out_sems)[0].wait()

    copies[3].wait()
    copies[4].wait()
    for step in range(times // 4):
        for j in range(4):
            gated = w_final_v[...].astype(F32) * terms_v[step * 4 + j, 3:4, :]
            rows[step % 2, j * chans : (j + 1) * chans, :] = gated.astype(BF16)
        back = dot(rows[step % 2], w_proj_v[...], NT)
        for j in range(4):
            t = step * 4 + j
            outward_v[t] = (back[j * chans : (j + 1) * chans] * steps[t]).astype(BF16)
    left += fetch([(outward_v, outward)], out_sems.at[pl.ds(1, 1)])
    moved, means = [], []
    past = jnp.zeros((1, wide), F32)
    for t in range(times):
        moved.append(terms_v[t, 1:2, :])
        means.append(centre(terms_v[t, 0:1, :]))
        lines_v[times + t : times + t + 1, :] = 1.0 + terms_v[t, 2:3, :]
        past = past + jnp.where(t < here[0], steps[t], 0.0) * terms_v[t, 0:1, :]
    moved, means = jnp.concatenate(moved, axis=0), jnp.concatenate(means, axis=0)
    lines_v[:times, :] = means
    left += fetch([(lines_v, lines)], out_sems.at[pl.ds(2, 1)])

    def put(name, values):
        first, last = places[name]
        small_v[first:last, :] = jnp.concatenate(
            [values, jnp.zeros((values.shape[0], small_v.shape[1] - values.shape[1]), F32)], axis=1
        ) if values.shape[1] < small_v.shape[1] else values

    both = pieces[...]
    square = dot(both, both, NT)
    square = square[:chans, :chans] + square[chans:, :chans] + square[:chans, chans:]
    high, low = two_parts(square)
    gram_v[:chans, :] = high
    gram_v[chans:, :] = low
    left += fetch([(gram_v, gram)], out_sems.at[pl.ds(3, 1)])
    high, low = two_parts(means)
    mixed = dot(stack_rows(high, low), both, NT)
    put("cross", mixed[:times, :chans] + mixed[times:, :chans] + mixed[:times, chans:])
    high, low = two_parts(moved)
    split = stack_rows(high, low)
    shifts = []
    for c in range(3):
        shift = dot(split, w_qkv_v[c])
        shifts.append(shift[:times] + shift[times:])
    put("shifts", jnp.concatenate(shifts, axis=0))
    final = w_final_v[...]
    put("direct", dot(final, w_in_v[...], NT))
    high = past.astype(BF16)
    middle, low = two_parts(past - high.astype(F32))
    parts = stack_rows(high, middle, low, jnp.zeros((5, wide), F32))
    earlier = jnp.sum(dot(final, parts, NT), axis=-1, keepdims=True)
    put("earlier", jnp.broadcast_to(earlier, (chans, small_v.shape[1])))
    for copy in copies[5:]:
        copy.wait()
    put("query_gain", jnp.broadcast_to(gains_v[0] * (head**-0.5 * LOG2E), (head, head)).T)
    put("key_gain", jnp.broadcast_to(gains_v[1], (head, head)).T)
    ids = jnp.broadcast_to(segments_v[...].astype(F32), (tokens, tokens))
    put("bias", jnp.where(ids == ids.T, 0.0, MASKED))
    numbers = lax.broadcasted_iota(jnp.int32, (count, tokens), 0).astype(F32)
    put("rest", jnp.where(here[0] == 0, rest_v[...], 0.0))
    ones = jnp.ones((1, tokens), F32)
    passed = [ones * jnp.where(t < here[0], steps[t], 0.0) for t in range(times)]
    put("weights", jnp.concatenate(passed, axis=0))
    put("member", jnp.where(numbers == ids[:count], 1.0, 0.0))
    left += fetch([(small_v, small)], out_sems.at[pl.ds(4, 1)])
    for copy in left:
        copy.wait()


def gather_documents(arrived, chans, count, piece):
    parts = []
    for i in range(arrived.shape[0]):
        block = arrived[i, chans:, :].astype(F32)
        parts.append(block[:count])
        parts.append(block[count:, : piece - block.shape[1]])
    return jnp.concatenate(parts, axis=1)


def heads_kernel(
    arrived,
    lines_h, w_in_h, w_final_h, w_qkv_h, gram_h, small_h, inward_h, outward_h,
    out, residual,
    lines, w_in, w_final, w_qkv, gram, small, inward, outward,
    rows, queries, keys, values, raised, mass, attended, sems,
):
    times, chans, head = outward.shape
    tokens = arrived.shape[2]
    count = (arrived.shape[1] - chans) // 2
    wide = w_in.shape[1]
    places, _ = small_rows(times, chans, head, tokens, count)
    copies = fetch(
        [
            (lines_h, lines), (w_in_h, w_in), (w_final_h, w_final), (w_qkv_h, w_qkv),
            (gram_h, gram), (small_h, small), (inward_h, inward), (outward_h, outward),
        ],
        sems,
    )

    def table(name, lanes=None):
        first, last = places[name]
        return small[first:last, :lanes]

    documents = gather_documents(arrived, chans, count, wide // times)
    exact = stack_rows(documents, jnp.zeros_like(documents))
    documents = centre(documents)
    copies[0].wait()
    powers = []
    for t in range(0, times, 2):
        pair = []
        for j in range(2):
            row = documents + lines[t + j : t + j + 1, :]
            powers.append(jnp.sum(row * row, axis=-1, keepdims=True))
            pair.append(row * lines[times + t + j : times + t + j + 1, :])
        rows[t * count : (t + 2) * count, :] = jnp.concatenate(pair, axis=0).astype(BF16)
    copies[1].wait()
    copies[2].wait()
    narrow = dot(w_final[...], exact, NT)[:, :count]
    high, low = two_parts(documents)
    near = dot(stack_rows(high, low), w_in[...], NT)
    near = near[:count] + near[count:]
    copies[3].wait()
    base = dot(rows[...], jnp.concatenate([w_qkv[c] for c in range(3)], axis=1))
    for copy in copies[4:]:
        copy.wait()
    shifts = table("shifts")
    shifts = jnp.concatenate([shifts[c * times : (c + 1) * times] for c in range(3)], axis=1)
    turned = []
    for half in range(2):
        span = slice(half * 8 * count, (half + 1) * 8 * count)
        block = [base[span], shifts[half * 8 : (half + 1) * 8, :]]
        left = head - 8 * count - 8
        block.append(jnp.zeros((left, 3 * head), F32))
        turned.append(jnp.concatenate(block, axis=0).T.astype(BF16))

    belongs = table("member")
    cross = table("cross", chans)
    weights = table("weights")
    past = jnp.zeros((chans, tokens), F32)
    for t in range(times):
        past = past + weights[t : t + 1, :] * arrived[t, :chans, :].astype(F32)
    whole = jnp.sum(weights[:, :count], axis=0, keepdims=True)
    highest = lax.Precision.HIGHEST
    near_docs = dot(whole * narrow + table("earlier", count), belongs, NN, highest)
    first_rest = table("rest")
    residual[...] = (
        dot(table("direct", chans), past, NN, highest)
        + near_docs
        + arrived[0, :chans, :].astype(F32)
        + first_rest
    )

    scaled_low, rates = [], []
    for pair in range(0, times, 2):
        left = [gram[...]]
        for t in (pair, pair + 1):
            high, low = two_parts(2.0 * (near + cross[t : t + 1, :]))
            left.append(stack_rows(high, low))
        blocks = [arrived[t, :chans, :] for t in (pair, pair + 1)]
        products = dot(jnp.concatenate(left, axis=0), jnp.concatenate(blocks, axis=1))
        for k in range(2):
            product = products[:, k * tokens : (k + 1) * tokens]
            both = product[:chans] + product[chans : 2 * chans]
            block = blocks[k].astype(F32)
            at = 2 * chans + 2 * k * count
            other = product[at : at + count] + product[at + count : at + 2 * count]
            spread = jnp.sum(both * block, axis=0, keepdims=True) + jnp.sum(
                belongs * (other + powers[pair + k]), axis=0, keepdims=True
            )
            rate = lax.rsqrt(spread / wide + EPS)
            rates.append(rate)
            scaled_low.append((block * rate).astype(BF16))

    def unit(block, gain):
        power = jnp.mean(block * block, axis=0, keepdims=True)
        return block * (lax.rsqrt(power + EPS) * gain)

    empty = jnp.zeros((chans, tokens), BF16)
    for pair in range(0, times, 2):
        left = jnp.concatenate([inward[pair // 2], turned[pair // 8]], axis=1)
        columns = []
        for t in (pair, pair + 1):
            j = t % 8
            first = [scaled_low[t], empty] if t == pair else [empty, scaled_low[t]]
            ones = lax.broadcasted_iota(jnp.int32, (8, tokens), 0) == j
            second = [jnp.zeros((j * count, tokens), F32)] if j else []
            second.append(belongs * rates[t])
            if j < 7:
                second.append(jnp.zeros(((7 - j) * count, tokens), F32))
            second.append(jnp.where(ones, 1.0, 0.0))
            second.append(jnp.zeros((head - 8 * count - 8, tokens), F32))
            second = jnp.concatenate(second, axis=0).astype(BF16)
            columns.append(jnp.concatenate(first + [second], axis=0))
        right = jnp.concatenate(columns, axis=1)
        for c in range(3):
            products = dot(left[c * head : (c + 1) * head], right)
            for k in range(2):
                block = products[:, k * tokens : (k + 1) * tokens]
                if c == 0:
                    queries[pair + k] = unit(block, table("query_gain")).astype(BF16)
                elif c == 1:
                    keys[pair + k] = unit(block, table("key_gain")).astype(BF16).T
                else:
                    values[pair + k] = block.astype(BF16)
    for t in range(times):
        scores = dot(keys[t], queries[t]) + table("bias")
        powered = jnp.exp2(scores - jnp.max(scores, axis=0, keepdims=True))
        mass[t : t + 1, :] = 1.0 / jnp.sum(powered, axis=0, keepdims=True)
        raised[t] = powered.astype(BF16)
    for t in range(times):
        attended[t] = (dot(values[t], raised[t]) * mass[t : t + 1, :]).astype(BF16)
    out[0] = jnp.zeros((chans, tokens), BF16)
    total = first_rest
    for t in range(times - 1):
        total = total + dot(outward[t], attended[t])
        out[t + 1] = total.astype(BF16)


def select(table, latents, pack_docs, w_in, terms, w_qkv):
    block, count = latents.shape[1:], pack_docs.shape[1]
    times, (chans, wide), head = terms.shape[0], w_in.shape, w_qkv.shape[2]
    folded = ((times // 2, 3 * head, 2 * chans), BF16)
    return pl.pallas_call(
        select_kernel,
        out_shape=(
            pltpu.HBM((times, block[0] + 2 * count, block[1]), BF16),
            pltpu.HBM(block, F32),
            pltpu.HBM(*folded),
        ),
        in_specs=[VMEM] + [HBM] * 5,
        out_specs=(HBM,) * 3,
        scratch_shapes=[
            pltpu.VMEM(latents.shape, F32),
            pltpu.VMEM(pack_docs.shape, jnp.int32),
            pltpu.VMEM(block, F32),
            pltpu.VMEM(block, BF16),
            pltpu.VMEM((2 * count, block[1]), BF16),
            pltpu.SemaphoreType.DMA((2,)),
            pltpu.SemaphoreType.DMA((1 + 2 * times,)),
            pltpu.VMEM(w_in.shape, BF16),
            pltpu.VMEM(terms.shape, F32),
            pltpu.VMEM(w_qkv.shape, BF16),
            pltpu.VMEM(w_in.shape, F32),
            pltpu.VMEM((2, 4 * chans, wide), BF16),
            pltpu.VMEM(*folded),
            pltpu.SemaphoreType.DMA((3,)),
        ],
        compiler_params=PARAMS,
        name="select",
    )(table, *pinned(latents, pack_docs, w_in, terms, w_qkv))


def fold_weights(
    here, steps, terms, w_in, w_qkv, w_final, w_proj, query_gain, key_gain, segments, rest, inward
):
    times, wide = terms.shape[0], terms.shape[2]
    chans, head, tokens = w_final.shape[0], w_proj.shape[0], segments.shape[1]
    count = 8
    shapes = [
        ((times // 2, 3 * head, 2 * chans), BF16),
        ((times, chans, head), BF16),
        ((2 * times, wide), F32),
        ((2 * chans, chans), BF16),
        ((small_rows(times, chans, head, tokens, count)[1], tokens), F32),
    ]
    return pl.pallas_call(
        weights_kernel,
        out_shape=tuple(pltpu.HBM(*s) for s in shapes),
        in_specs=[SMEM] * 2 + [HBM] * 10,
        out_specs=(HBM,) * 5,
        input_output_aliases={11: 0},
        scratch_shapes=[
            pltpu.VMEM(a.shape, a.dtype) for a in (terms, w_in, w_qkv, w_final, w_proj)
        ]
        + [
            pltpu.VMEM((2,) + query_gain.shape, F32),
            pltpu.VMEM(segments.shape, jnp.int32),
            pltpu.VMEM(rest.shape, F32),
            pltpu.VMEM((chans, wide), F32),
            pltpu.VMEM((2 * chans, wide), BF16),
            pltpu.VMEM((2, 4 * chans, wide), BF16),
        ]
        + [pltpu.VMEM(*s) for s in shapes]
        + [pltpu.SemaphoreType.DMA((9,)), pltpu.SemaphoreType.DMA((5,))],
        compiler_params=PARAMS,
        name="fold_weights",
    )(
        here,
        steps,
        *pinned(terms, w_in, w_qkv, w_final, w_proj, query_gain, key_gain, segments, rest, inward),
    )


def run_heads(arrived, *operands):
    outward = operands[-1]
    times, chans, head = outward.shape
    tokens = arrived.shape[2]
    rows = times * (arrived.shape[1] - chans) // 2
    wide = operands[0].shape[1]
    square = pltpu.VMEM((times, head, tokens), BF16)
    return pl.pallas_call(
        heads_kernel,
        out_shape=(
            jax.ShapeDtypeStruct((times, chans, tokens), BF16),
            jax.ShapeDtypeStruct((chans, tokens), F32),
        ),
        in_specs=[VMEM] + [HBM] * len(operands),
        out_specs=(VMEM, VMEM),
        scratch_shapes=[pltpu.VMEM(a.shape, a.dtype) for a in operands]
        + [
            pltpu.VMEM((rows, wide), BF16),
            square, square, square, square,
            pltpu.VMEM((times, tokens), F32),
            square,
            pltpu.SemaphoreType.DMA((len(operands),)),
        ],
        compiler_params=PARAMS,
        name="run_heads",
    )(arrived, *pinned(*operands))


def local(
    latents,
    time_terms,
    step_sizes,
    doc_embed,
    pack_docs,
    segment_ids,
    w_in,
    w_qkv,
    query_gain,
    key_gain,
    w_proj,
    w_final,
):
    here = lax.axis_index("tm")
    place = here.astype(jnp.int32).reshape(1)
    owners = lax.axis_size("req")
    count, piece = doc_embed.shape
    w_heads = w_qkv[:, :, 0, :].transpose(1, 0, 2)
    w_last = w_final.T

    copies = jnp.broadcast_to(doc_embed[None], (owners, count, piece))
    table = lax.all_to_all(copies, "req", 0, 0)
    sent, rest, inward = select(
        table, latents, pack_docs[None], w_in, time_terms, w_heads
    )
    arrived = lax.all_to_all(sent, "tm", 0, 0)
    inward, outward, lines, gram, small = fold_weights(
        place, step_sizes, time_terms, w_in, w_heads, w_last, w_proj[0], query_gain, key_gain,
        segment_ids, rest, inward,
    )
    sums, residual = run_heads(
        arrived, lines, w_in, w_last, w_heads, gram, small, inward, outward
    )
    parts = lax.all_to_all(sums, "tm", 0, 0)
    return (residual + jnp.sum(parts.astype(F32), axis=0))[None]


def solution(mesh):
    in_specs = (
        P("tm", None, "req"),
        P(),
        P(),
        P("req", "tm"),
        P("req"),
        P("req", None),
        P(),
        P(None, None, "tm", None),
        P("tm", None),
        P("tm", None),
        P("tm", None, None),
        P(),
    )
    out_specs = P("tm", None, "req")
    return jax.shard_map(local, mesh=mesh, in_specs=in_specs, out_specs=out_specs, check_vma=False)
```

```python
import jax
import jax.numpy as jnp
from jax import lax
from jax.experimental import pallas as pl
from jax.experimental.pallas import tpu as pltpu
from jax.sharding import PartitionSpec as P

EPS = 1e-06
EARLY = 3
MASKED = -1e30
LOG2E = 1.4426950408889634
BF16, F32 = jnp.bfloat16, jnp.float32
NN = (((1,), (0,)), ((), ()))
NT = (((1,), (1,)), ((), ()))
VMEM = pl.BlockSpec(memory_space=pltpu.VMEM)
SMEM = pl.BlockSpec(memory_space=pltpu.SMEM)
HBM = pl.BlockSpec(memory_space=pltpu.HBM)
PARAMS = pltpu.CompilerParams(vmem_limit_bytes=24 * 2**20)


def dot(left, right, dims=NN, precision=None):
    return lax.dot_general(left, right, dims, precision=precision, preferred_element_type=F32)


def two_parts(values):
    high = values.astype(BF16)
    return high, (values - high.astype(F32)).astype(BF16)


def stack_rows(*parts):
    return jnp.concatenate([p.astype(F32) for p in parts], axis=0).astype(BF16)


def centre(values):
    return values - jnp.mean(values, axis=-1, keepdims=True)


def pinned(*arrays):
    return tuple(pltpu.with_memory_space_constraint(a, pltpu.HBM) for a in arrays)


def fetch(pairs, sems):
    copies = [pltpu.make_async_copy(a, b, sems.at[i]) for i, (a, b) in enumerate(pairs)]
    for copy in copies:
        copy.start()
    return copies


def first_core():
    return lax.rem(lax.axis_index("req"), 2) == 0


def fold_inward(steps, centred, terms, w_qkv, rows, inward):
    chans, head = centred.shape[0], w_qkv.shape[2]
    for step in steps:
        for j in range(4):
            scaled = centred[...] * (1.0 + terms[step * 4 + j, 2:3, :])
            rows[step % 2, j * chans : (j + 1) * chans, :] = scaled.astype(BF16)
        for c in range(3):
            turned = dot(rows[step % 2], w_qkv[c]).T.astype(BF16)
            inward[2 * step, c * head : (c + 1) * head, :] = turned[:, : 2 * chans]
            inward[2 * step + 1, c * head : (c + 1) * head, :] = turned[:, 2 * chans :]


def select_kernel(
    table, latents, pack_docs, w_in, terms, w_qkv,
    sent, rest, inward,
    latents_v, packs_v, rest_v, staged, sems, out_sems,
    w_in_v, terms_v, w_qkv_v, centred, line_rows, inward_v, fold_sems,
):
    early = first_core()
    folds = [(w_in, w_in_v), (terms, terms_v), (w_qkv, w_qkv_v)]
    times, rows, lanes = sent.shape
    chans = latents_v.shape[1]
    owners, count, piece = table.shape
    copies = fetch([(latents, latents_v), (pack_docs, packs_v)], sems)

    @pl.when(early)
    def _():
        fetch(folds, fold_sems)

    copies[0].wait()
    values = latents_v[0]
    high = values.astype(BF16)
    for i in range(times):
        staged[i, :chans, :] = high
    rest_v[...] = values - high.astype(F32)
    left = fetch(
        [(rest_v, rest), (staged.at[:, pl.ds(0, chans)], sent.at[:, pl.ds(0, chans)])], out_sems
    )
    copies[1].wait()
    column = jnp.broadcast_to(packs_v[...].astype(F32), (count, count))
    eye = lax.broadcasted_iota(jnp.int32, (count, count), 0) == lax.broadcasted_iota(
        jnp.int32, (count, count), 1
    )
    column = jnp.sum(jnp.where(eye, column, 0.0), axis=1, keepdims=True)
    places = lax.broadcasted_iota(jnp.int32, (count, owners * count), 1).astype(F32)
    pick = jnp.where(places == column, 1.0, 0.0)
    pick = stack_rows(pick, jnp.zeros_like(pick))
    chosen = dot(pick, table[...].reshape(owners * count, piece))[:count]
    tail = jnp.concatenate(
        [chosen[:, lanes:], jnp.zeros((count, 2 * lanes - piece), F32)], axis=1
    )
    chosen = stack_rows(chosen[:, :lanes], tail)
    for i in range(times):
        staged[i, chans:, :] = chosen
    last = pl.ds(chans, 2 * count)
    left += fetch([(staged.at[:, last], sent.at[:, last])], out_sems.at[pl.ds(2, 1)])

    @pl.when(early)
    def _():
        for i, (source, target) in enumerate(folds):
            pltpu.make_async_copy(source, target, fold_sems.at[i]).wait()
        centred[...] = centre(w_in_v[...].astype(F32))
        fold_inward(range(EARLY), centred, terms_v, w_qkv_v, line_rows, inward_v)
        done = pl.ds(0, 2 * EARLY)
        fetch([(inward_v.at[done], inward.at[done])], fold_sems)[0].wait()

    for copy in left:
        copy.wait()


def small_rows(times, chans, head, tokens, count):
    sizes = [
        ("query_gain", head), ("key_gain", head), ("bias", tokens), ("member", count),
        ("direct", chans), ("earlier", chans), ("cross", times), ("shifts", 3 * times),
        ("rest", chans), ("weights", times),
    ]
    places, at = {}, 0
    for name, rows in sizes:
        places[name] = (at, at + rows)
        at += rows
    return places, at


def weights_kernel(
    here, steps, terms, w_in, w_qkv, w_final, w_proj, query_gain, key_gain, segments, rest,
    begun, inward, outward, lines, gram, small,
    terms_v, w_in_v, w_qkv_v, w_final_v, w_proj_v, gains_v, segments_v, rest_v,
    centred, pieces, rows, inward_v, outward_v, lines_v, gram_v, small_v, sems, out_sems,
):
    del begun
    times, chans, head = outward.shape
    tokens, count = segments_v.shape[1], 8
    wide = w_in_v.shape[1]
    places, _ = small_rows(times, chans, head, tokens, count)
    copies = fetch(
        [
            (w_in, w_in_v), (terms, terms_v), (w_qkv, w_qkv_v), (w_final, w_final_v),
            (w_proj, w_proj_v), (query_gain, gains_v.at[0]), (key_gain, gains_v.at[1]),
            (segments, segments_v), (rest, rest_v),
        ],
        sems,
    )
    copies[0].wait()
    centred[...] = centre(w_in_v[...].astype(F32))
    high, low = two_parts(centred[...])
    pieces[:chans, :] = high
    pieces[chans:, :] = low
    copies[1].wait()
    copies[2].wait()
    left = []

    @pl.when(first_core())
    def _():
        fold_inward(range(EARLY, times // 4), centred, terms_v, w_qkv_v, rows, inward_v)
        done = pl.ds(2 * EARLY, times // 2 - 2 * EARLY)
        fetch([(inward_v.at[done], inward.at[done])], out_sems)[0].wait()

    @pl.when(jnp.logical_not(first_core()))
    def _():
        fold_inward(range(times // 4), centred, terms_v, w_qkv_v, rows, inward_v)
        fetch([(inward_v, inward)], out_sems)[0].wait()

    copies[3].wait()
    copies[4].wait()
    for step in range(times // 4):
        for j in range(4):
            gated = w_final_v[...].astype(F32) * terms_v[step * 4 + j, 3:4, :]
            rows[step % 2, j * chans : (j + 1) * chans, :] = gated.astype(BF16)
        back = dot(rows[step % 2], w_proj_v[...], NT)
        for j in range(4):
            t = step * 4 + j
            outward_v[t] = (back[j * chans : (j + 1) * chans] * steps[t]).astype(BF16)
    left += fetch([(outward_v, outward)], out_sems.at[pl.ds(1, 1)])
    moved, means = [], []
    past = jnp.zeros((1, wide), F32)
    for t in range(times):
        moved.append(terms_v[t, 1:2, :])
        means.append(centre(terms_v[t, 0:1, :]))
        lines_v[times + t : times + t + 1, :] = 1.0 + terms_v[t, 2:3, :]
        past = past + jnp.where(t < here[0], steps[t], 0.0) * terms_v[t, 0:1, :]
    moved, means = jnp.concatenate(moved, axis=0), jnp.concatenate(means, axis=0)
    lines_v[:times, :] = means
    left += fetch([(lines_v, lines)], out_sems.at[pl.ds(2, 1)])

    def put(name, values):
        first, last = places[name]
        small_v[first:last, :] = jnp.concatenate(
            [values, jnp.zeros((values.shape[0], small_v.shape[1] - values.shape[1]), F32)], axis=1
        ) if values.shape[1] < small_v.shape[1] else values

    both = pieces[...]
    square = dot(both, both, NT)
    square = square[:chans, :chans] + square[chans:, :chans] + square[:chans, chans:]
    high, low = two_parts(square)
    gram_v[:chans, :] = high
    gram_v[chans:, :] = low
    left += fetch([(gram_v, gram)], out_sems.at[pl.ds(3, 1)])
    high, low = two_parts(means)
    mixed = dot(stack_rows(high, low), both, NT)
    put("cross", mixed[:times, :chans] + mixed[times:, :chans] + mixed[:times, chans:])
    high, low = two_parts(moved)
    split = stack_rows(high, low)
    shifts = []
    for c in range(3):
        shift = dot(split, w_qkv_v[c])
        shifts.append(shift[:times] + shift[times:])
    put("shifts", jnp.concatenate(shifts, axis=0))
    final = w_final_v[...]
    put("direct", dot(final, w_in_v[...], NT))
    high = past.astype(BF16)
    middle, low = two_parts(past - high.astype(F32))
    parts = stack_rows(high, middle, low, jnp.zeros((5, wide), F32))
    earlier = jnp.sum(dot(final, parts, NT), axis=-1, keepdims=True)
    put("earlier", jnp.broadcast_to(earlier, (chans, small_v.shape[1])))
    for copy in copies[5:]:
        copy.wait()
    put("query_gain", jnp.broadcast_to(gains_v[0] * (head**-0.5 * LOG2E), (head, head)).T)
    put("key_gain", jnp.broadcast_to(gains_v[1], (head, head)).T)
    ids = jnp.broadcast_to(segments_v[...].astype(F32), (tokens, tokens))
    put("bias", jnp.where(ids == ids.T, 0.0, MASKED))
    numbers = lax.broadcasted_iota(jnp.int32, (count, tokens), 0).astype(F32)
    put("rest", jnp.where(here[0] == 0, rest_v[...], 0.0))
    ones = jnp.ones((1, tokens), F32)
    passed = [ones * jnp.where(t < here[0], steps[t], 0.0) for t in range(times)]
    put("weights", jnp.concatenate(passed, axis=0))
    put("member", jnp.where(numbers == ids[:count], 1.0, 0.0))
    left += fetch([(small_v, small)], out_sems.at[pl.ds(4, 1)])
    for copy in left:
        copy.wait()


def gather_documents(arrived, chans, count, piece):
    parts = []
    for i in range(arrived.shape[0]):
        block = arrived[i, chans:, :].astype(F32)
        parts.append(block[:count])
        parts.append(block[count:, : piece - block.shape[1]])
    return jnp.concatenate(parts, axis=1)


def heads_kernel(
    arrived,
    lines_h, w_in_h, w_final_h, w_qkv_h, gram_h, small_h, inward_h, outward_h,
    out, residual,
    lines, w_in, w_final, w_qkv, gram, small, inward, outward,
    rows, queries, keys, values, raised, mass, attended, sems,
):
    times, chans, head = outward.shape
    tokens = arrived.shape[2]
    count = (arrived.shape[1] - chans) // 2
    wide = w_in.shape[1]
    places, _ = small_rows(times, chans, head, tokens, count)
    copies = fetch(
        [
            (lines_h, lines), (w_in_h, w_in), (w_final_h, w_final), (w_qkv_h, w_qkv),
            (gram_h, gram), (small_h, small), (inward_h, inward), (outward_h, outward),
        ],
        sems,
    )

    def table(name, lanes=None):
        first, last = places[name]
        return small[first:last, :lanes]

    documents = gather_documents(arrived, chans, count, wide // times)
    exact = stack_rows(documents, jnp.zeros_like(documents))
    documents = centre(documents)
    copies[0].wait()
    powers = []
    for t in range(0, times, 2):
        pair = []
        for j in range(2):
            row = documents + lines[t + j : t + j + 1, :]
            powers.append(jnp.sum(row * row, axis=-1, keepdims=True))
            pair.append(row * lines[times + t + j : times + t + j + 1, :])
        rows[t * count : (t + 2) * count, :] = jnp.concatenate(pair, axis=0).astype(BF16)
    copies[1].wait()
    copies[2].wait()
    narrow = dot(w_final[...], exact, NT)[:, :count]
    high, low = two_parts(documents)
    near = dot(stack_rows(high, low), w_in[...], NT)
    near = near[:count] + near[count:]
    copies[3].wait()
    base = dot(rows[...], jnp.concatenate([w_qkv[c] for c in range(3)], axis=1))
    for copy in copies[4:]:
        copy.wait()
    shifts = table("shifts")
    shifts = jnp.concatenate([shifts[c * times : (c + 1) * times] for c in range(3)], axis=1)
    turned = []
    for half in range(2):
        span = slice(half * 8 * count, (half + 1) * 8 * count)
        block = [base[span], shifts[half * 8 : (half + 1) * 8, :]]
        left = head - 8 * count - 8
        block.append(jnp.zeros((left, 3 * head), F32))
        turned.append(jnp.concatenate(block, axis=0).T.astype(BF16))

    belongs = table("member")
    cross = table("cross", chans)
    weights = table("weights")
    past = jnp.zeros((chans, tokens), F32)
    for t in range(times):
        past = past + weights[t : t + 1, :] * arrived[t, :chans, :].astype(F32)
    whole = jnp.sum(weights[:, :count], axis=0, keepdims=True)
    highest = lax.Precision.HIGHEST
    near_docs = dot(whole * narrow + table("earlier", count), belongs, NN, highest)
    first_rest = table("rest")
    residual[...] = (
        dot(table("direct", chans), past, NN, highest)
        + near_docs
        + arrived[0, :chans, :].astype(F32)
        + first_rest
    )

    scaled_low, rates = [], []
    for pair in range(0, times, 2):
        left = [gram[...]]
        for t in (pair, pair + 1):
            high, low = two_parts(2.0 * (near + cross[t : t + 1, :]))
            left.append(stack_rows(high, low))
        blocks = [arrived[t, :chans, :] for t in (pair, pair + 1)]
        products = dot(jnp.concatenate(left, axis=0), jnp.concatenate(blocks, axis=1))
        for k in range(2):
            product = products[:, k * tokens : (k + 1) * tokens]
            both = product[:chans] + product[chans : 2 * chans]
            block = blocks[k].astype(F32)
            at = 2 * chans + 2 * k * count
            other = product[at : at + count] + product[at + count : at + 2 * count]
            spread = jnp.sum(both * block, axis=0, keepdims=True) + jnp.sum(
                belongs * (other + powers[pair + k]), axis=0, keepdims=True
            )
            rate = lax.rsqrt(spread / wide + EPS)
            rates.append(rate)
            scaled_low.append((block * rate).astype(BF16))

    def unit(block, gain):
        power = jnp.mean(block * block, axis=0, keepdims=True)
        return block * (lax.rsqrt(power + EPS) * gain)

    empty = jnp.zeros((chans, tokens), BF16)
    for pair in range(0, times, 2):
        left = jnp.concatenate([inward[pair // 2], turned[pair // 8]], axis=1)
        columns = []
        for t in (pair, pair + 1):
            j = t % 8
            first = [scaled_low[t], empty] if t == pair else [empty, scaled_low[t]]
            ones = lax.broadcasted_iota(jnp.int32, (8, tokens), 0) == j
            second = [jnp.zeros((j * count, tokens), F32)] if j else []
            second.append(belongs * rates[t])
            if j < 7:
                second.append(jnp.zeros(((7 - j) * count, tokens), F32))
            second.append(jnp.where(ones, 1.0, 0.0))
            second.append(jnp.zeros((head - 8 * count - 8, tokens), F32))
            second = jnp.concatenate(second, axis=0).astype(BF16)
            columns.append(jnp.concatenate(first + [second], axis=0))
        right = jnp.concatenate(columns, axis=1)
        for c in range(3):
            products = dot(left[c * head : (c + 1) * head], right)
            for k in range(2):
                block = products[:, k * tokens : (k + 1) * tokens]
                if c == 0:
                    queries[pair + k] = unit(block, table("query_gain")).astype(BF16)
                elif c == 1:
                    keys[pair + k] = unit(block, table("key_gain")).astype(BF16).T
                else:
                    values[pair + k] = block.astype(BF16)
    for t in range(times):
        scores = dot(keys[t], queries[t]) + table("bias")
        powered = jnp.exp2(scores - jnp.max(scores, axis=0, keepdims=True))
        mass[t : t + 1, :] = 1.0 / jnp.sum(powered, axis=0, keepdims=True)
        raised[t] = powered.astype(BF16)
    for t in range(times):
        attended[t] = (dot(values[t], raised[t]) * mass[t : t + 1, :]).astype(BF16)
    out[0] = jnp.zeros((chans, tokens), BF16)
    total = first_rest
    for t in range(times - 1):
        total = total + dot(outward[t], attended[t])
        out[t + 1] = total.astype(BF16)


def select(table, latents, pack_docs, w_in, terms, w_qkv):
    block, count = latents.shape[1:], pack_docs.shape[1]
    times, (chans, wide), head = terms.shape[0], w_in.shape, w_qkv.shape[2]
    folded = ((times // 2, 3 * head, 2 * chans), BF16)
    return pl.pallas_call(
        select_kernel,
        out_shape=(
            pltpu.HBM((times, block[0] + 2 * count, block[1]), BF16),
            pltpu.HBM(block, F32),
            pltpu.HBM(*folded),
        ),
        in_specs=[VMEM] + [HBM] * 5,
        out_specs=(HBM,) * 3,
        scratch_shapes=[
            pltpu.VMEM(latents.shape, F32),
            pltpu.VMEM(pack_docs.shape, jnp.int32),
            pltpu.VMEM(block, F32),
            pltpu.VMEM((times, block[0] + 2 * count, block[1]), BF16),
            pltpu.SemaphoreType.DMA((2,)),
            pltpu.SemaphoreType.DMA((3,)),
            pltpu.VMEM(w_in.shape, BF16),
            pltpu.VMEM(terms.shape, F32),
            pltpu.VMEM(w_qkv.shape, BF16),
            pltpu.VMEM(w_in.shape, F32),
            pltpu.VMEM((2, 4 * chans, wide), BF16),
            pltpu.VMEM(*folded),
            pltpu.SemaphoreType.DMA((3,)),
        ],
        compiler_params=PARAMS,
        name="select",
    )(table, *pinned(latents, pack_docs, w_in, terms, w_qkv))


def fold_weights(
    here, steps, terms, w_in, w_qkv, w_final, w_proj, query_gain, key_gain, segments, rest, inward
):
    times, wide = terms.shape[0], terms.shape[2]
    chans, head, tokens = w_final.shape[0], w_proj.shape[0], segments.shape[1]
    count = 8
    shapes = [
        ((times // 2, 3 * head, 2 * chans), BF16),
        ((times, chans, head), BF16),
        ((2 * times, wide), F32),
        ((2 * chans, chans), BF16),
        ((small_rows(times, chans, head, tokens, count)[1], tokens), F32),
    ]
    return pl.pallas_call(
        weights_kernel,
        out_shape=tuple(pltpu.HBM(*s) for s in shapes),
        in_specs=[SMEM] * 2 + [HBM] * 10,
        out_specs=(HBM,) * 5,
        input_output_aliases={11: 0},
        scratch_shapes=[
            pltpu.VMEM(a.shape, a.dtype) for a in (terms, w_in, w_qkv, w_final, w_proj)
        ]
        + [
            pltpu.VMEM((2,) + query_gain.shape, F32),
            pltpu.VMEM(segments.shape, jnp.int32),
            pltpu.VMEM(rest.shape, F32),
            pltpu.VMEM((chans, wide), F32),
            pltpu.VMEM((2 * chans, wide), BF16),
            pltpu.VMEM((2, 4 * chans, wide), BF16),
        ]
        + [pltpu.VMEM(*s) for s in shapes]
        + [pltpu.SemaphoreType.DMA((9,)), pltpu.SemaphoreType.DMA((5,))],
        compiler_params=PARAMS,
        name="fold_weights",
    )(
        here,
        steps,
        *pinned(terms, w_in, w_qkv, w_final, w_proj, query_gain, key_gain, segments, rest, inward),
    )


def run_heads(arrived, *operands):
    outward = operands[-1]
    times, chans, head = outward.shape
    tokens = arrived.shape[2]
    rows = times * (arrived.shape[1] - chans) // 2
    wide = operands[0].shape[1]
    square = pltpu.VMEM((times, head, tokens), BF16)
    return pl.pallas_call(
        heads_kernel,
        out_shape=(
            jax.ShapeDtypeStruct((times, chans, tokens), BF16),
            jax.ShapeDtypeStruct((chans, tokens), F32),
        ),
        in_specs=[VMEM] + [HBM] * len(operands),
        out_specs=(VMEM, VMEM),
        scratch_shapes=[pltpu.VMEM(a.shape, a.dtype) for a in operands]
        + [
            pltpu.VMEM((rows, wide), BF16),
            square, square, square, square,
            pltpu.VMEM((times, tokens), F32),
            square,
            pltpu.SemaphoreType.DMA((len(operands),)),
        ],
        compiler_params=PARAMS,
        name="run_heads",
    )(arrived, *pinned(*operands))


def local(
    latents,
    time_terms,
    step_sizes,
    doc_embed,
    pack_docs,
    segment_ids,
    w_in,
    w_qkv,
    query_gain,
    key_gain,
    w_proj,
    w_final,
):
    here = lax.axis_index("tm")
    place = here.astype(jnp.int32).reshape(1)
    owners = lax.axis_size("req")
    count, piece = doc_embed.shape
    w_heads = w_qkv[:, :, 0, :].transpose(1, 0, 2)
    w_last = w_final.T

    copies = jnp.broadcast_to(doc_embed[None], (owners, count, piece))
    table = lax.all_to_all(copies, "req", 0, 0)
    sent, rest, inward = select(
        table, latents, pack_docs[None], w_in, time_terms, w_heads
    )
    arrived = lax.all_to_all(sent, "tm", 0, 0)
    inward, outward, lines, gram, small = fold_weights(
        place, step_sizes, time_terms, w_in, w_heads, w_last, w_proj[0], query_gain, key_gain,
        segment_ids, rest, inward,
    )
    sums, residual = run_heads(
        arrived, lines, w_in, w_last, w_heads, gram, small, inward, outward
    )
    parts = lax.all_to_all(sums, "tm", 0, 0)
    return (residual + jnp.sum(parts.astype(F32), axis=0))[None]


def solution(mesh):
    in_specs = (
        P("tm", None, "req"),
        P(),
        P(),
        P("req", "tm"),
        P("req"),
        P("req", None),
        P(),
        P(None, None, "tm", None),
        P("tm", None),
        P("tm", None),
        P("tm", None, None),
        P(),
    )
    out_specs = P("tm", None, "req")
    return jax.shard_map(local, mesh=mesh, in_specs=in_specs, out_specs=out_specs, check_vma=False)
```

```python
import jax
import jax.numpy as jnp
from jax import lax
from jax.experimental import pallas as pl
from jax.experimental.pallas import tpu as pltpu
from jax.sharding import PartitionSpec as P

EPS = 1e-06
EARLY = 2
MASKED = -1e30
LOG2E = 1.4426950408889634
BF16, F32 = jnp.bfloat16, jnp.float32
NN = (((1,), (0,)), ((), ()))
NT = (((1,), (1,)), ((), ()))
VMEM = pl.BlockSpec(memory_space=pltpu.VMEM)
SMEM = pl.BlockSpec(memory_space=pltpu.SMEM)
HBM = pl.BlockSpec(memory_space=pltpu.HBM)
PARAMS = pltpu.CompilerParams(vmem_limit_bytes=24 * 2**20)


def dot(left, right, dims=NN, precision=None):
    return lax.dot_general(left, right, dims, precision=precision, preferred_element_type=F32)


def two_parts(values):
    high = values.astype(BF16)
    return high, (values - high.astype(F32)).astype(BF16)


def stack_rows(*parts):
    return jnp.concatenate([p.astype(F32) for p in parts], axis=0).astype(BF16)


def centre(values):
    return values - jnp.mean(values, axis=-1, keepdims=True)


def pinned(*arrays):
    return tuple(pltpu.with_memory_space_constraint(a, pltpu.HBM) for a in arrays)


def fetch(pairs, sems):
    copies = [pltpu.make_async_copy(a, b, sems.at[i]) for i, (a, b) in enumerate(pairs)]
    for copy in copies:
        copy.start()
    return copies


def first_core():
    return lax.rem(lax.axis_index("req"), 2) == 0


def fold_inward(steps, centred, terms, w_qkv, rows, inward):
    chans, head = centred.shape[0], w_qkv.shape[2]
    for step in steps:
        for j in range(4):
            scaled = centred[...] * (1.0 + terms[step * 4 + j, 2:3, :])
            rows[step % 2, j * chans : (j + 1) * chans, :] = scaled.astype(BF16)
        for c in range(3):
            turned = dot(rows[step % 2], w_qkv[c]).T.astype(BF16)
            inward[2 * step, c * head : (c + 1) * head, :] = turned[:, : 2 * chans]
            inward[2 * step + 1, c * head : (c + 1) * head, :] = turned[:, 2 * chans :]


def select_kernel(
    table, latents, pack_docs, w_in, terms, w_qkv,
    sent, rest, inward,
    latents_v, packs_v, rest_v, staged, sems, out_sems,
    w_in_v, terms_v, w_qkv_v, centred, line_rows, inward_v, fold_sems,
):
    early = first_core()
    folds = [(w_in, w_in_v), (terms, terms_v), (w_qkv, w_qkv_v)]
    times, rows, lanes = sent.shape
    chans = latents_v.shape[1]
    owners, count, piece = table.shape
    copies = fetch([(latents, latents_v), (pack_docs, packs_v)], sems)

    @pl.when(early)
    def _():
        fetch(folds, fold_sems)

    copies[0].wait()
    values = latents_v[0]
    high = values.astype(BF16)
    for i in range(times):
        staged[i, :chans, :] = high
    rest_v[...] = values - high.astype(F32)
    left = fetch(
        [(rest_v, rest), (staged.at[:, pl.ds(0, chans)], sent.at[:, pl.ds(0, chans)])], out_sems
    )
    copies[1].wait()
    column = jnp.broadcast_to(packs_v[...].astype(F32), (count, count))
    eye = lax.broadcasted_iota(jnp.int32, (count, count), 0) == lax.broadcasted_iota(
        jnp.int32, (count, count), 1
    )
    column = jnp.sum(jnp.where(eye, column, 0.0), axis=1, keepdims=True)
    places = lax.broadcasted_iota(jnp.int32, (count, owners * count), 1).astype(F32)
    pick = jnp.where(places == column, 1.0, 0.0)
    pick = stack_rows(pick, jnp.zeros_like(pick))
    chosen = dot(pick, table[...].reshape(owners * count, piece))[:count]
    tail = jnp.concatenate(
        [chosen[:, lanes:], jnp.zeros((count, 2 * lanes - piece), F32)], axis=1
    )
    chosen = stack_rows(chosen[:, :lanes], tail)
    for i in range(times):
        staged[i, chans:, :] = chosen
    last = pl.ds(chans, 2 * count)
    left += fetch([(staged.at[:, last], sent.at[:, last])], out_sems.at[pl.ds(2, 1)])

    @pl.when(early)
    def _():
        for i, (source, target) in enumerate(folds):
            pltpu.make_async_copy(source, target, fold_sems.at[i]).wait()
        centred[...] = centre(w_in_v[...].astype(F32))
        fold_inward(range(EARLY), centred, terms_v, w_qkv_v, line_rows, inward_v)
        done = pl.ds(0, 2 * EARLY)
        fetch([(inward_v.at[done], inward.at[done])], fold_sems)[0].wait()

    for copy in left:
        copy.wait()


def small_rows(times, chans, head, tokens, count):
    sizes = [
        ("query_gain", head), ("key_gain", head), ("bias", tokens), ("member", count),
        ("direct", chans), ("earlier", chans), ("cross", times), ("shifts", 3 * times),
        ("rest", chans), ("weights", times),
    ]
    places, at = {}, 0
    for name, rows in sizes:
        places[name] = (at, at + rows)
        at += rows
    return places, at


def weights_kernel(
    here, steps, terms, w_in, w_qkv, w_final, w_proj, query_gain, key_gain, segments, rest,
    begun, inward, outward, lines, gram, small,
    terms_v, w_in_v, w_qkv_v, w_final_v, w_proj_v, gains_v, segments_v, rest_v,
    centred, pieces, rows, inward_v, outward_v, lines_v, gram_v, small_v, sems, out_sems,
):
    del begun
    times, chans, head = outward.shape
    tokens, count = segments_v.shape[1], 8
    wide = w_in_v.shape[1]
    places, _ = small_rows(times, chans, head, tokens, count)
    copies = fetch(
        [
            (w_in, w_in_v), (terms, terms_v), (w_qkv, w_qkv_v), (w_final, w_final_v),
            (w_proj, w_proj_v), (query_gain, gains_v.at[0]), (key_gain, gains_v.at[1]),
            (segments, segments_v), (rest, rest_v),
        ],
        sems,
    )
    copies[0].wait()
    centred[...] = centre(w_in_v[...].astype(F32))
    high, low = two_parts(centred[...])
    pieces[:chans, :] = high
    pieces[chans:, :] = low
    copies[1].wait()
    copies[2].wait()
    left = []

    @pl.when(first_core())
    def _():
        fold_inward(range(EARLY, times // 4), centred, terms_v, w_qkv_v, rows, inward_v)
        done = pl.ds(2 * EARLY, times // 2 - 2 * EARLY)
        fetch([(inward_v.at[done], inward.at[done])], out_sems)[0].wait()

    @pl.when(jnp.logical_not(first_core()))
    def _():
        fold_inward(range(times // 4), centred, terms_v, w_qkv_v, rows, inward_v)
        fetch([(inward_v, inward)], out_sems)[0].wait()

    copies[3].wait()
    copies[4].wait()
    for step in range(times // 4):
        for j in range(4):
            gated = w_final_v[...].astype(F32) * terms_v[step * 4 + j, 3:4, :]
            rows[step % 2, j * chans : (j + 1) * chans, :] = gated.astype(BF16)
        back = dot(rows[step % 2], w_proj_v[...], NT)
        for j in range(4):
            t = step * 4 + j
            outward_v[t] = (back[j * chans : (j + 1) * chans] * steps[t]).astype(BF16)
    left += fetch([(outward_v, outward)], out_sems.at[pl.ds(1, 1)])
    moved, means = [], []
    past = jnp.zeros((1, wide), F32)
    for t in range(times):
        moved.append(terms_v[t, 1:2, :])
        means.append(centre(terms_v[t, 0:1, :]))
        lines_v[times + t : times + t + 1, :] = 1.0 + terms_v[t, 2:3, :]
        past = past + jnp.where(t < here[0], steps[t], 0.0) * terms_v[t, 0:1, :]
    moved, means = jnp.concatenate(moved, axis=0), jnp.concatenate(means, axis=0)
    lines_v[:times, :] = means
    left += fetch([(lines_v, lines)], out_sems.at[pl.ds(2, 1)])

    def put(name, values):
        first, last = places[name]
        small_v[first:last, :] = jnp.concatenate(
            [values, jnp.zeros((values.shape[0], small_v.shape[1] - values.shape[1]), F32)], axis=1
        ) if values.shape[1] < small_v.shape[1] else values

    both = pieces[...]
    square = dot(both, both, NT)
    square = square[:chans, :chans] + square[chans:, :chans] + square[:chans, chans:]
    high, low = two_parts(square)
    gram_v[:chans, :] = high
    gram_v[chans:, :] = low
    left += fetch([(gram_v, gram)], out_sems.at[pl.ds(3, 1)])
    high, low = two_parts(means)
    mixed = dot(stack_rows(high, low), both, NT)
    put("cross", mixed[:times, :chans] + mixed[times:, :chans] + mixed[:times, chans:])
    high, low = two_parts(moved)
    split = stack_rows(high, low)
    shifts = []
    for c in range(3):
        shift = dot(split, w_qkv_v[c])
        shifts.append(shift[:times] + shift[times:])
    put("shifts", jnp.concatenate(shifts, axis=0))
    final = w_final_v[...]
    put("direct", dot(final, w_in_v[...], NT))
    high = past.astype(BF16)
    middle, low = two_parts(past - high.astype(F32))
    parts = stack_rows(high, middle, low, jnp.zeros((5, wide), F32))
    earlier = jnp.sum(dot(final, parts, NT), axis=-1, keepdims=True)
    put("earlier", jnp.broadcast_to(earlier, (chans, small_v.shape[1])))
    for copy in copies[5:]:
        copy.wait()
    put("query_gain", jnp.broadcast_to(gains_v[0] * (head**-0.5 * LOG2E), (head, head)).T)
    put("key_gain", jnp.broadcast_to(gains_v[1], (head, head)).T)
    ids = jnp.broadcast_to(segments_v[...].astype(F32), (tokens, tokens))
    put("bias", jnp.where(ids == ids.T, 0.0, MASKED))
    numbers = lax.broadcasted_iota(jnp.int32, (count, tokens), 0).astype(F32)
    put("rest", jnp.where(here[0] == 0, rest_v[...], 0.0))
    ones = jnp.ones((1, tokens), F32)
    passed = [ones * jnp.where(t < here[0], steps[t], 0.0) for t in range(times)]
    put("weights", jnp.concatenate(passed, axis=0))
    put("member", jnp.where(numbers == ids[:count], 1.0, 0.0))
    left += fetch([(small_v, small)], out_sems.at[pl.ds(4, 1)])
    for copy in left:
        copy.wait()


def gather_documents(arrived, chans, count, piece):
    parts = []
    for i in range(arrived.shape[0]):
        block = arrived[i, chans:, :].astype(F32)
        parts.append(block[:count])
        parts.append(block[count:, : piece - block.shape[1]])
    return jnp.concatenate(parts, axis=1)


def heads_kernel(
    arrived,
    lines_h, w_in_h, w_final_h, w_qkv_h, gram_h, small_h, inward_h, outward_h,
    out, residual,
    lines, w_in, w_final, w_qkv, gram, small, inward, outward,
    rows, queries, keys, values, raised, mass, attended, sems,
):
    times, chans, head = outward.shape
    tokens = arrived.shape[2]
    count = (arrived.shape[1] - chans) // 2
    wide = w_in.shape[1]
    places, _ = small_rows(times, chans, head, tokens, count)
    copies = fetch(
        [
            (lines_h, lines), (w_in_h, w_in), (w_final_h, w_final), (w_qkv_h, w_qkv),
            (gram_h, gram), (small_h, small), (inward_h, inward), (outward_h, outward),
        ],
        sems,
    )

    def table(name, lanes=None):
        first, last = places[name]
        return small[first:last, :lanes]

    documents = gather_documents(arrived, chans, count, wide // times)
    exact = stack_rows(documents, jnp.zeros_like(documents))
    documents = centre(documents)
    copies[0].wait()
    powers = []
    for t in range(0, times, 2):
        pair = []
        for j in range(2):
            row = documents + lines[t + j : t + j + 1, :]
            powers.append(jnp.sum(row * row, axis=-1, keepdims=True))
            pair.append(row * lines[times + t + j : times + t + j + 1, :])
        rows[t * count : (t + 2) * count, :] = jnp.concatenate(pair, axis=0).astype(BF16)
    copies[1].wait()
    copies[2].wait()
    narrow = dot(w_final[...], exact, NT)[:, :count]
    high, low = two_parts(documents)
    near = dot(stack_rows(high, low), w_in[...], NT)
    near = near[:count] + near[count:]
    copies[3].wait()
    base = dot(rows[...], jnp.concatenate([w_qkv[c] for c in range(3)], axis=1))
    for copy in copies[4:]:
        copy.wait()
    shifts = table("shifts")
    shifts = jnp.concatenate([shifts[c * times : (c + 1) * times] for c in range(3)], axis=1)
    turned = []
    for half in range(2):
        span = slice(half * 8 * count, (half + 1) * 8 * count)
        block = [base[span], shifts[half * 8 : (half + 1) * 8, :]]
        left = head - 8 * count - 8
        block.append(jnp.zeros((left, 3 * head), F32))
        turned.append(jnp.concatenate(block, axis=0).T.astype(BF16))

    belongs = table("member")
    cross = table("cross", chans)
    weights = table("weights")
    past = jnp.zeros((chans, tokens), F32)
    for t in range(times):
        past = past + weights[t : t + 1, :] * arrived[t, :chans, :].astype(F32)
    whole = jnp.sum(weights[:, :count], axis=0, keepdims=True)
    highest = lax.Precision.HIGHEST
    near_docs = dot(whole * narrow + table("earlier", count), belongs, NN, highest)
    first_rest = table("rest")
    residual[...] = (
        dot(table("direct", chans), past, NN, highest)
        + near_docs
        + arrived[0, :chans, :].astype(F32)
        + first_rest
    )

    scaled_low, rates = [], []
    for pair in range(0, times, 2):
        left = [gram[...]]
        for t in (pair, pair + 1):
            high, low = two_parts(2.0 * (near + cross[t : t + 1, :]))
            left.append(stack_rows(high, low))
        blocks = [arrived[t, :chans, :] for t in (pair, pair + 1)]
        products = dot(jnp.concatenate(left, axis=0), jnp.concatenate(blocks, axis=1))
        for k in range(2):
            product = products[:, k * tokens : (k + 1) * tokens]
            both = product[:chans] + product[chans : 2 * chans]
            block = blocks[k].astype(F32)
            at = 2 * chans + 2 * k * count
            other = product[at : at + count] + product[at + count : at + 2 * count]
            spread = jnp.sum(both * block, axis=0, keepdims=True) + jnp.sum(
                belongs * (other + powers[pair + k]), axis=0, keepdims=True
            )
            rate = lax.rsqrt(spread / wide + EPS)
            rates.append(rate)
            scaled_low.append((block * rate).astype(BF16))

    def unit(block, gain):
        power = jnp.mean(block * block, axis=0, keepdims=True)
        return block * (lax.rsqrt(power + EPS) * gain)

    empty = jnp.zeros((chans, tokens), BF16)
    for pair in range(0, times, 2):
        left = jnp.concatenate([inward[pair // 2], turned[pair // 8]], axis=1)
        columns = []
        for t in (pair, pair + 1):
            j = t % 8
            first = [scaled_low[t], empty] if t == pair else [empty, scaled_low[t]]
            ones = lax.broadcasted_iota(jnp.int32, (8, tokens), 0) == j
            second = [jnp.zeros((j * count, tokens), F32)] if j else []
            second.append(belongs * rates[t])
            if j < 7:
                second.append(jnp.zeros(((7 - j) * count, tokens), F32))
            second.append(jnp.where(ones, 1.0, 0.0))
            second.append(jnp.zeros((head - 8 * count - 8, tokens), F32))
            second = jnp.concatenate(second, axis=0).astype(BF16)
            columns.append(jnp.concatenate(first + [second], axis=0))
        right = jnp.concatenate(columns, axis=1)
        for c in range(3):
            products = dot(left[c * head : (c + 1) * head], right)
            for k in range(2):
                block = products[:, k * tokens : (k + 1) * tokens]
                if c == 0:
                    queries[pair + k] = unit(block, table("query_gain")).astype(BF16)
                elif c == 1:
                    keys[pair + k] = unit(block, table("key_gain")).astype(BF16).T
                else:
                    values[pair + k] = block.astype(BF16)
    for t in range(times):
        scores = dot(keys[t], queries[t]) + table("bias")
        powered = jnp.exp2(scores - jnp.max(scores, axis=0, keepdims=True))
        mass[t : t + 1, :] = 1.0 / jnp.sum(powered, axis=0, keepdims=True)
        raised[t] = powered.astype(BF16)
    for t in range(times):
        attended[t] = (dot(values[t], raised[t]) * mass[t : t + 1, :]).astype(BF16)
    out[0] = jnp.zeros((chans, tokens), BF16)
    total = first_rest
    for t in range(times - 1):
        total = total + dot(outward[t], attended[t])
        out[t + 1] = total.astype(BF16)


def select(table, latents, pack_docs, w_in, terms, w_qkv):
    block, count = latents.shape[1:], pack_docs.shape[1]
    times, (chans, wide), head = terms.shape[0], w_in.shape, w_qkv.shape[2]
    folded = ((times // 2, 3 * head, 2 * chans), BF16)
    return pl.pallas_call(
        select_kernel,
        out_shape=(
            pltpu.HBM((times, block[0] + 2 * count, block[1]), BF16),
            pltpu.HBM(block, F32),
            pltpu.HBM(*folded),
        ),
        in_specs=[VMEM] + [HBM] * 5,
        out_specs=(HBM,) * 3,
        scratch_shapes=[
            pltpu.VMEM(latents.shape, F32),
            pltpu.VMEM(pack_docs.shape, jnp.int32),
            pltpu.VMEM(block, F32),
            pltpu.VMEM((times, block[0] + 2 * count, block[1]), BF16),
            pltpu.SemaphoreType.DMA((2,)),
            pltpu.SemaphoreType.DMA((3,)),
            pltpu.VMEM(w_in.shape, BF16),
            pltpu.VMEM(terms.shape, F32),
            pltpu.VMEM(w_qkv.shape, BF16),
            pltpu.VMEM(w_in.shape, F32),
            pltpu.VMEM((2, 4 * chans, wide), BF16),
            pltpu.VMEM(*folded),
            pltpu.SemaphoreType.DMA((3,)),
        ],
        compiler_params=PARAMS,
        name="select",
    )(table, *pinned(latents, pack_docs, w_in, terms, w_qkv))


def fold_weights(
    here, steps, terms, w_in, w_qkv, w_final, w_proj, query_gain, key_gain, segments, rest, inward
):
    times, wide = terms.shape[0], terms.shape[2]
    chans, head, tokens = w_final.shape[0], w_proj.shape[0], segments.shape[1]
    count = 8
    shapes = [
        ((times // 2, 3 * head, 2 * chans), BF16),
        ((times, chans, head), BF16),
        ((2 * times, wide), F32),
        ((2 * chans, chans), BF16),
        ((small_rows(times, chans, head, tokens, count)[1], tokens), F32),
    ]
    return pl.pallas_call(
        weights_kernel,
        out_shape=tuple(pltpu.HBM(*s) for s in shapes),
        in_specs=[SMEM] * 2 + [HBM] * 10,
        out_specs=(HBM,) * 5,
        input_output_aliases={11: 0},
        scratch_shapes=[
            pltpu.VMEM(a.shape, a.dtype) for a in (terms, w_in, w_qkv, w_final, w_proj)
        ]
        + [
            pltpu.VMEM((2,) + query_gain.shape, F32),
            pltpu.VMEM(segments.shape, jnp.int32),
            pltpu.VMEM(rest.shape, F32),
            pltpu.VMEM((chans, wide), F32),
            pltpu.VMEM((2 * chans, wide), BF16),
            pltpu.VMEM((2, 4 * chans, wide), BF16),
        ]
        + [pltpu.VMEM(*s) for s in shapes]
        + [pltpu.SemaphoreType.DMA((9,)), pltpu.SemaphoreType.DMA((5,))],
        compiler_params=PARAMS,
        name="fold_weights",
    )(
        here,
        steps,
        *pinned(terms, w_in, w_qkv, w_final, w_proj, query_gain, key_gain, segments, rest, inward),
    )


def run_heads(arrived, *operands):
    outward = operands[-1]
    times, chans, head = outward.shape
    tokens = arrived.shape[2]
    rows = times * (arrived.shape[1] - chans) // 2
    wide = operands[0].shape[1]
    square = pltpu.VMEM((times, head, tokens), BF16)
    return pl.pallas_call(
        heads_kernel,
        out_shape=(
            jax.ShapeDtypeStruct((times, chans, tokens), BF16),
            jax.ShapeDtypeStruct((chans, tokens), F32),
        ),
        in_specs=[VMEM] + [HBM] * len(operands),
        out_specs=(VMEM, VMEM),
        scratch_shapes=[pltpu.VMEM(a.shape, a.dtype) for a in operands]
        + [
            pltpu.VMEM((rows, wide), BF16),
            square, square, square, square,
            pltpu.VMEM((times, tokens), F32),
            square,
            pltpu.SemaphoreType.DMA((len(operands),)),
        ],
        compiler_params=PARAMS,
        name="run_heads",
    )(arrived, *pinned(*operands))


def local(
    latents,
    time_terms,
    step_sizes,
    doc_embed,
    pack_docs,
    segment_ids,
    w_in,
    w_qkv,
    query_gain,
    key_gain,
    w_proj,
    w_final,
):
    here = lax.axis_index("tm")
    place = here.astype(jnp.int32).reshape(1)
    owners = lax.axis_size("req")
    count, piece = doc_embed.shape
    w_heads = w_qkv[:, :, 0, :].transpose(1, 0, 2)
    w_last = w_final.T

    copies = jnp.broadcast_to(doc_embed[None], (owners, count, piece))
    table = lax.all_to_all(copies, "req", 0, 0)
    sent, rest, inward = select(
        table, latents, pack_docs[None], w_in, time_terms, w_heads
    )
    arrived = lax.all_to_all(sent, "tm", 0, 0)
    inward, outward, lines, gram, small = fold_weights(
        place, step_sizes, time_terms, w_in, w_heads, w_last, w_proj[0], query_gain, key_gain,
        segment_ids, rest, inward,
    )
    sums, residual = run_heads(
        arrived, lines, w_in, w_last, w_heads, gram, small, inward, outward
    )
    parts = lax.all_to_all(sums, "tm", 0, 0)
    return (residual + jnp.sum(parts.astype(F32), axis=0))[None]


def solution(mesh):
    in_specs = (
        P("tm", None, "req"),
        P(),
        P(),
        P("req", "tm"),
        P("req"),
        P("req", None),
        P(),
        P(None, None, "tm", None),
        P("tm", None),
        P("tm", None),
        P("tm", None, None),
        P(),
    )
    out_specs = P("tm", None, "req")
    return jax.shard_map(local, mesh=mesh, in_specs=in_specs, out_specs=out_specs, check_vma=False)
```

```python
import jax
import jax.numpy as jnp
from jax import lax
from jax.experimental import pallas as pl
from jax.experimental.pallas import tpu as pltpu
from jax.sharding import PartitionSpec as P

EPS = 1e-06
EARLY = 3
MASKED = -1e30
LOG2E = 1.4426950408889634
BF16, F32 = jnp.bfloat16, jnp.float32
NN = (((1,), (0,)), ((), ()))
NT = (((1,), (1,)), ((), ()))
VMEM = pl.BlockSpec(memory_space=pltpu.VMEM)
SMEM = pl.BlockSpec(memory_space=pltpu.SMEM)
HBM = pl.BlockSpec(memory_space=pltpu.HBM)
PARAMS = pltpu.CompilerParams(vmem_limit_bytes=24 * 2**20)


def dot(left, right, dims=NN, precision=None):
    return lax.dot_general(left, right, dims, precision=precision, preferred_element_type=F32)


def two_parts(values):
    high = values.astype(BF16)
    return high, (values - high.astype(F32)).astype(BF16)


def stack_rows(*parts):
    return jnp.concatenate([p.astype(F32) for p in parts], axis=0).astype(BF16)


def centre(values):
    return values - jnp.mean(values, axis=-1, keepdims=True)


def pinned(*arrays):
    return tuple(pltpu.with_memory_space_constraint(a, pltpu.HBM) for a in arrays)


def fetch(pairs, sems):
    copies = [pltpu.make_async_copy(a, b, sems.at[i]) for i, (a, b) in enumerate(pairs)]
    for copy in copies:
        copy.start()
    return copies


def first_core():
    return lax.rem(lax.axis_index("req"), 2) == 0


def fold_inward(steps, centred, terms, w_qkv, rows, inward):
    chans = centred.shape[0]
    for step in steps:
        for j in range(4):
            scaled = centred[...] * (1.0 + terms[step * 4 + j, 2:3, :])
            rows[step % 2, j * chans : (j + 1) * chans, :] = scaled.astype(BF16)
        wide = jnp.concatenate([w_qkv[c] for c in range(3)], axis=1)
        turned = dot(rows[step % 2], wide).T.astype(BF16)
        inward[2 * step] = turned[:, : 2 * chans]
        inward[2 * step + 1] = turned[:, 2 * chans :]


def select_kernel(
    table, latents, pack_docs, w_in, terms, w_qkv,
    sent, rest, inward,
    latents_v, packs_v, rest_v, staged, sems, out_sems,
    w_in_v, terms_v, w_qkv_v, centred, line_rows, inward_v, fold_sems,
):
    early = first_core()
    folds = [(w_in, w_in_v), (terms, terms_v), (w_qkv, w_qkv_v)]
    times, rows, lanes = sent.shape
    chans = latents_v.shape[1]
    owners, count, piece = table.shape
    copies = fetch([(latents, latents_v), (pack_docs, packs_v)], sems)

    @pl.when(early)
    def _():
        fetch(folds, fold_sems)

    copies[0].wait()
    values = latents_v[0]
    high = values.astype(BF16)
    for i in range(times):
        staged[i, :chans, :] = high
    rest_v[...] = values - high.astype(F32)
    left = fetch(
        [(rest_v, rest), (staged.at[:, pl.ds(0, chans)], sent.at[:, pl.ds(0, chans)])], out_sems
    )
    copies[1].wait()
    column = jnp.broadcast_to(packs_v[...].astype(F32), (count, count))
    eye = lax.broadcasted_iota(jnp.int32, (count, count), 0) == lax.broadcasted_iota(
        jnp.int32, (count, count), 1
    )
    column = jnp.sum(jnp.where(eye, column, 0.0), axis=1, keepdims=True)
    places = lax.broadcasted_iota(jnp.int32, (count, owners * count), 1).astype(F32)
    pick = jnp.where(places == column, 1.0, 0.0)
    pick = stack_rows(pick, jnp.zeros_like(pick))
    chosen = dot(pick, table[...].reshape(owners * count, piece))[:count]
    tail = jnp.concatenate(
        [chosen[:, lanes:], jnp.zeros((count, 2 * lanes - piece), F32)], axis=1
    )
    chosen = stack_rows(chosen[:, :lanes], tail)
    for i in range(times):
        staged[i, chans:, :] = chosen
    last = pl.ds(chans, 2 * count)
    left += fetch([(staged.at[:, last], sent.at[:, last])], out_sems.at[pl.ds(2, 1)])

    @pl.when(early)
    def _():
        for i, (source, target) in enumerate(folds):
            pltpu.make_async_copy(source, target, fold_sems.at[i]).wait()
        centred[...] = centre(w_in_v[...].astype(F32))
        fold_inward(range(EARLY), centred, terms_v, w_qkv_v, line_rows, inward_v)
        done = pl.ds(0, 2 * EARLY)
        fetch([(inward_v.at[done], inward.at[done])], fold_sems)[0].wait()

    for copy in left:
        copy.wait()


def small_rows(times, chans, head, tokens, count):
    sizes = [
        ("query_gain", head), ("key_gain", head), ("bias", tokens), ("member", count),
        ("direct", chans), ("earlier", chans), ("cross", times), ("shifts", 3 * times),
        ("rest", chans), ("weights", times),
    ]
    places, at = {}, 0
    for name, rows in sizes:
        places[name] = (at, at + rows)
        at += rows
    return places, at


def weights_kernel(
    here, steps, terms, w_in, w_qkv, w_final, w_proj, query_gain, key_gain, segments, rest,
    begun, inward, outward, lines, gram, small,
    terms_v, w_in_v, w_qkv_v, w_final_v, w_proj_v, gains_v, segments_v, rest_v,
    centred, pieces, rows, inward_v, outward_v, lines_v, gram_v, small_v, sems, out_sems,
):
    del begun
    times, chans, head = outward.shape
    tokens, count = segments_v.shape[1], 8
    wide = w_in_v.shape[1]
    places, _ = small_rows(times, chans, head, tokens, count)
    copies = fetch(
        [
            (w_in, w_in_v), (terms, terms_v), (w_qkv, w_qkv_v), (w_final, w_final_v),
            (w_proj, w_proj_v), (query_gain, gains_v.at[0]), (key_gain, gains_v.at[1]),
            (segments, segments_v), (rest, rest_v),
        ],
        sems,
    )
    copies[0].wait()
    centred[...] = centre(w_in_v[...].astype(F32))
    high, low = two_parts(centred[...])
    pieces[:chans, :] = high
    pieces[chans:, :] = low
    copies[1].wait()
    copies[2].wait()
    left = []

    @pl.when(first_core())
    def _():
        fold_inward(range(EARLY, times // 4), centred, terms_v, w_qkv_v, rows, inward_v)
        done = pl.ds(2 * EARLY, times // 2 - 2 * EARLY)
        fetch([(inward_v.at[done], inward.at[done])], out_sems)[0].wait()

    @pl.when(jnp.logical_not(first_core()))
    def _():
        fold_inward(range(times // 4), centred, terms_v, w_qkv_v, rows, inward_v)
        fetch([(inward_v, inward)], out_sems)[0].wait()

    copies[3].wait()
    copies[4].wait()
    for step in range(times // 4):
        for j in range(4):
            gated = w_final_v[...].astype(F32) * terms_v[step * 4 + j, 3:4, :]
            rows[step % 2, j * chans : (j + 1) * chans, :] = gated.astype(BF16)
        back = dot(rows[step % 2], w_proj_v[...], NT)
        for j in range(4):
            t = step * 4 + j
            outward_v[t] = (back[j * chans : (j + 1) * chans] * steps[t]).astype(BF16)
    left += fetch([(outward_v, outward)], out_sems.at[pl.ds(1, 1)])
    moved, means = [], []
    past = jnp.zeros((1, wide), F32)
    for t in range(times):
        moved.append(terms_v[t, 1:2, :])
        means.append(centre(terms_v[t, 0:1, :]))
        lines_v[times + t : times + t + 1, :] = 1.0 + terms_v[t, 2:3, :]
        past = past + jnp.where(t < here[0], steps[t], 0.0) * terms_v[t, 0:1, :]
    moved, means = jnp.concatenate(moved, axis=0), jnp.concatenate(means, axis=0)
    lines_v[:times, :] = means
    left += fetch([(lines_v, lines)], out_sems.at[pl.ds(2, 1)])

    def put(name, values):
        first, last = places[name]
        small_v[first:last, :] = jnp.concatenate(
            [values, jnp.zeros((values.shape[0], small_v.shape[1] - values.shape[1]), F32)], axis=1
        ) if values.shape[1] < small_v.shape[1] else values

    both = pieces[...]
    square = dot(both, both, NT)
    square = square[:chans, :chans] + square[chans:, :chans] + square[:chans, chans:]
    high, low = two_parts(square)
    gram_v[:chans, :] = high
    gram_v[chans:, :] = low
    left += fetch([(gram_v, gram)], out_sems.at[pl.ds(3, 1)])
    high, low = two_parts(means)
    mixed = dot(stack_rows(high, low), both, NT)
    put("cross", mixed[:times, :chans] + mixed[times:, :chans] + mixed[:times, chans:])
    high, low = two_parts(moved)
    split = stack_rows(high, low)
    shifts = []
    for c in range(3):
        shift = dot(split, w_qkv_v[c])
        shifts.append(shift[:times] + shift[times:])
    put("shifts", jnp.concatenate(shifts, axis=0))
    final = w_final_v[...]
    put("direct", dot(final, w_in_v[...], NT))
    high = past.astype(BF16)
    middle, low = two_parts(past - high.astype(F32))
    parts = stack_rows(high, middle, low, jnp.zeros((5, wide), F32))
    earlier = jnp.sum(dot(final, parts, NT), axis=-1, keepdims=True)
    put("earlier", jnp.broadcast_to(earlier, (chans, small_v.shape[1])))
    for copy in copies[5:]:
        copy.wait()
    put("query_gain", jnp.broadcast_to(gains_v[0] * (head**-0.5 * LOG2E), (head, head)).T)
    put("key_gain", jnp.broadcast_to(gains_v[1], (head, head)).T)
    ids = jnp.broadcast_to(segments_v[...].astype(F32), (tokens, tokens))
    put("bias", jnp.where(ids == ids.T, 0.0, MASKED))
    numbers = lax.broadcasted_iota(jnp.int32, (count, tokens), 0).astype(F32)
    put("rest", jnp.where(here[0] == 0, rest_v[...], 0.0))
    ones = jnp.ones((1, tokens), F32)
    passed = [ones * jnp.where(t < here[0], steps[t], 0.0) for t in range(times)]
    put("weights", jnp.concatenate(passed, axis=0))
    put("member", jnp.where(numbers == ids[:count], 1.0, 0.0))
    left += fetch([(small_v, small)], out_sems.at[pl.ds(4, 1)])
    for copy in left:
        copy.wait()


def gather_documents(arrived, chans, count, piece):
    parts = []
    for i in range(arrived.shape[0]):
        block = arrived[i, chans:, :].astype(F32)
        parts.append(block[:count])
        parts.append(block[count:, : piece - block.shape[1]])
    return jnp.concatenate(parts, axis=1)


def heads_kernel(
    arrived,
    lines_h, w_in_h, w_final_h, w_qkv_h, gram_h, small_h, inward_h, outward_h,
    out, residual,
    lines, w_in, w_final, w_qkv, gram, small, inward, outward,
    rows, queries, keys, values, raised, mass, attended, sems,
):
    times, chans, head = outward.shape
    tokens = arrived.shape[2]
    count = (arrived.shape[1] - chans) // 2
    wide = w_in.shape[1]
    places, _ = small_rows(times, chans, head, tokens, count)
    copies = fetch(
        [
            (lines_h, lines), (w_in_h, w_in), (w_final_h, w_final), (w_qkv_h, w_qkv),
            (gram_h, gram), (small_h, small), (inward_h, inward), (outward_h, outward),
        ],
        sems,
    )

    def table(name, lanes=None):
        first, last = places[name]
        return small[first:last, :lanes]

    documents = gather_documents(arrived, chans, count, wide // times)
    exact = stack_rows(documents, jnp.zeros_like(documents))
    documents = centre(documents)
    copies[0].wait()
    powers = []
    for t in range(0, times, 2):
        pair = []
        for j in range(2):
            row = documents + lines[t + j : t + j + 1, :]
            powers.append(jnp.sum(row * row, axis=-1, keepdims=True))
            pair.append(row * lines[times + t + j : times + t + j + 1, :])
        rows[t * count : (t + 2) * count, :] = jnp.concatenate(pair, axis=0).astype(BF16)
    copies[1].wait()
    copies[2].wait()
    narrow = dot(w_final[...], exact, NT)[:, :count]
    high, low = two_parts(documents)
    near = dot(stack_rows(high, low), w_in[...], NT)
    near = near[:count] + near[count:]
    copies[3].wait()
    base = dot(rows[...], jnp.concatenate([w_qkv[c] for c in range(3)], axis=1))
    for copy in copies[4:]:
        copy.wait()
    shifts = table("shifts")
    shifts = jnp.concatenate([shifts[c * times : (c + 1) * times] for c in range(3)], axis=1)
    turned = []
    for half in range(2):
        span = slice(half * 8 * count, (half + 1) * 8 * count)
        block = [base[span], shifts[half * 8 : (half + 1) * 8, :]]
        left = head - 8 * count - 8
        block.append(jnp.zeros((left, 3 * head), F32))
        turned.append(jnp.concatenate(block, axis=0).T.astype(BF16))

    belongs = table("member")
    cross = table("cross", chans)
    weights = table("weights")
    past = jnp.zeros((chans, tokens), F32)
    for t in range(times):
        past = past + weights[t : t + 1, :] * arrived[t, :chans, :].astype(F32)
    whole = jnp.sum(weights[:, :count], axis=0, keepdims=True)
    highest = lax.Precision.HIGHEST
    near_docs = dot(whole * narrow + table("earlier", count), belongs, NN, highest)
    first_rest = table("rest")
    residual[...] = (
        dot(table("direct", chans), past, NN, highest)
        + near_docs
        + arrived[0, :chans, :].astype(F32)
        + first_rest
    )

    scaled_low, rates = [], []
    for pair in range(0, times, 2):
        left = [gram[...]]
        for t in (pair, pair + 1):
            high, low = two_parts(2.0 * (near + cross[t : t + 1, :]))
            left.append(stack_rows(high, low))
        blocks = [arrived[t, :chans, :] for t in (pair, pair + 1)]
        products = dot(jnp.concatenate(left, axis=0), jnp.concatenate(blocks, axis=1))
        for k in range(2):
            product = products[:, k * tokens : (k + 1) * tokens]
            both = product[:chans] + product[chans : 2 * chans]
            block = blocks[k].astype(F32)
            at = 2 * chans + 2 * k * count
            other = product[at : at + count] + product[at + count : at + 2 * count]
            spread = jnp.sum(both * block, axis=0, keepdims=True) + jnp.sum(
                belongs * (other + powers[pair + k]), axis=0, keepdims=True
            )
            rate = lax.rsqrt(spread / wide + EPS)
            rates.append(rate)
            scaled_low.append((block * rate).astype(BF16))

    def unit(block, gain):
        power = jnp.mean(block * block, axis=0, keepdims=True)
        return block * (lax.rsqrt(power + EPS) * gain)

    empty = jnp.zeros((chans, tokens), BF16)
    for pair in range(0, times, 2):
        left = jnp.concatenate([inward[pair // 2], turned[pair // 8]], axis=1)
        columns = []
        for t in (pair, pair + 1):
            j = t % 8
            first = [scaled_low[t], empty] if t == pair else [empty, scaled_low[t]]
            ones = lax.broadcasted_iota(jnp.int32, (8, tokens), 0) == j
            second = [jnp.zeros((j * count, tokens), F32)] if j else []
            second.append(belongs * rates[t])
            if j < 7:
                second.append(jnp.zeros(((7 - j) * count, tokens), F32))
            second.append(jnp.where(ones, 1.0, 0.0))
            second.append(jnp.zeros((head - 8 * count - 8, tokens), F32))
            second = jnp.concatenate(second, axis=0).astype(BF16)
            columns.append(jnp.concatenate(first + [second], axis=0))
        right = jnp.concatenate(columns, axis=1)
        for c in range(3):
            products = dot(left[c * head : (c + 1) * head], right)
            for k in range(2):
                block = products[:, k * tokens : (k + 1) * tokens]
                if c == 0:
                    queries[pair + k] = unit(block, table("query_gain")).astype(BF16)
                elif c == 1:
                    keys[pair + k] = unit(block, table("key_gain")).astype(BF16).T
                else:
                    values[pair + k] = block.astype(BF16)
    for t in range(times):
        scores = dot(keys[t], queries[t]) + table("bias")
        powered = jnp.exp2(scores - jnp.max(scores, axis=0, keepdims=True))
        mass[t : t + 1, :] = 1.0 / jnp.sum(powered, axis=0, keepdims=True)
        raised[t] = powered.astype(BF16)
    for t in range(times):
        attended[t] = (dot(values[t], raised[t]) * mass[t : t + 1, :]).astype(BF16)
    out[0] = jnp.zeros((chans, tokens), BF16)
    total = first_rest
    for t in range(times - 1):
        total = total + dot(outward[t], attended[t])
        out[t + 1] = total.astype(BF16)


def select(table, latents, pack_docs, w_in, terms, w_qkv):
    block, count = latents.shape[1:], pack_docs.shape[1]
    times, (chans, wide), head = terms.shape[0], w_in.shape, w_qkv.shape[2]
    folded = ((times // 2, 3 * head, 2 * chans), BF16)
    return pl.pallas_call(
        select_kernel,
        out_shape=(
            pltpu.HBM((times, block[0] + 2 * count, block[1]), BF16),
            pltpu.HBM(block, F32),
            pltpu.HBM(*folded),
        ),
        in_specs=[VMEM] + [HBM] * 5,
        out_specs=(HBM,) * 3,
        scratch_shapes=[
            pltpu.VMEM(latents.shape, F32),
            pltpu.VMEM(pack_docs.shape, jnp.int32),
            pltpu.VMEM(block, F32),
            pltpu.VMEM((times, block[0] + 2 * count, block[1]), BF16),
            pltpu.SemaphoreType.DMA((2,)),
            pltpu.SemaphoreType.DMA((3,)),
            pltpu.VMEM(w_in.shape, BF16),
            pltpu.VMEM(terms.shape, F32),
            pltpu.VMEM(w_qkv.shape, BF16),
            pltpu.VMEM(w_in.shape, F32),
            pltpu.VMEM((2, 4 * chans, wide), BF16),
            pltpu.VMEM(*folded),
            pltpu.SemaphoreType.DMA((3,)),
        ],
        compiler_params=PARAMS,
        name="select",
    )(table, *pinned(latents, pack_docs, w_in, terms, w_qkv))


def fold_weights(
    here, steps, terms, w_in, w_qkv, w_final, w_proj, query_gain, key_gain, segments, rest, inward
):
    times, wide = terms.shape[0], terms.shape[2]
    chans, head, tokens = w_final.shape[0], w_proj.shape[0], segments.shape[1]
    count = 8
    shapes = [
        ((times // 2, 3 * head, 2 * chans), BF16),
        ((times, chans, head), BF16),
        ((2 * times, wide), F32),
        ((2 * chans, chans), BF16),
        ((small_rows(times, chans, head, tokens, count)[1], tokens), F32),
    ]
    return pl.pallas_call(
        weights_kernel,
        out_shape=tuple(pltpu.HBM(*s) for s in shapes),
        in_specs=[SMEM] * 2 + [HBM] * 10,
        out_specs=(HBM,) * 5,
        input_output_aliases={11: 0},
        scratch_shapes=[
            pltpu.VMEM(a.shape, a.dtype) for a in (terms, w_in, w_qkv, w_final, w_proj)
        ]
        + [
            pltpu.VMEM((2,) + query_gain.shape, F32),
            pltpu.VMEM(segments.shape, jnp.int32),
            pltpu.VMEM(rest.shape, F32),
            pltpu.VMEM((chans, wide), F32),
            pltpu.VMEM((2 * chans, wide), BF16),
            pltpu.VMEM((2, 4 * chans, wide), BF16),
        ]
        + [pltpu.VMEM(*s) for s in shapes]
        + [pltpu.SemaphoreType.DMA((9,)), pltpu.SemaphoreType.DMA((5,))],
        compiler_params=PARAMS,
        name="fold_weights",
    )(
        here,
        steps,
        *pinned(terms, w_in, w_qkv, w_final, w_proj, query_gain, key_gain, segments, rest, inward),
    )


def run_heads(arrived, *operands):
    outward = operands[-1]
    times, chans, head = outward.shape
    tokens = arrived.shape[2]
    rows = times * (arrived.shape[1] - chans) // 2
    wide = operands[0].shape[1]
    square = pltpu.VMEM((times, head, tokens), BF16)
    return pl.pallas_call(
        heads_kernel,
        out_shape=(
            jax.ShapeDtypeStruct((times, chans, tokens), BF16),
            jax.ShapeDtypeStruct((chans, tokens), F32),
        ),
        in_specs=[VMEM] + [HBM] * len(operands),
        out_specs=(VMEM, VMEM),
        scratch_shapes=[pltpu.VMEM(a.shape, a.dtype) for a in operands]
        + [
            pltpu.VMEM((rows, wide), BF16),
            square, square, square, square,
            pltpu.VMEM((times, tokens), F32),
            square,
            pltpu.SemaphoreType.DMA((len(operands),)),
        ],
        compiler_params=PARAMS,
        name="run_heads",
    )(arrived, *pinned(*operands))


def local(
    latents,
    time_terms,
    step_sizes,
    doc_embed,
    pack_docs,
    segment_ids,
    w_in,
    w_qkv,
    query_gain,
    key_gain,
    w_proj,
    w_final,
):
    here = lax.axis_index("tm")
    place = here.astype(jnp.int32).reshape(1)
    owners = lax.axis_size("req")
    count, piece = doc_embed.shape
    w_heads = w_qkv[:, :, 0, :].transpose(1, 0, 2)
    w_last = w_final.T

    copies = jnp.broadcast_to(doc_embed[None], (owners, count, piece))
    table = lax.all_to_all(copies, "req", 0, 0)
    sent, rest, inward = select(
        table, latents, pack_docs[None], w_in, time_terms, w_heads
    )
    arrived = lax.all_to_all(sent, "tm", 0, 0)
    inward, outward, lines, gram, small = fold_weights(
        place, step_sizes, time_terms, w_in, w_heads, w_last, w_proj[0], query_gain, key_gain,
        segment_ids, rest, inward,
    )
    sums, residual = run_heads(
        arrived, lines, w_in, w_last, w_heads, gram, small, inward, outward
    )
    parts = lax.all_to_all(sums, "tm", 0, 0)
    return (residual + jnp.sum(parts.astype(F32), axis=0))[None]


def solution(mesh):
    in_specs = (
        P("tm", None, "req"),
        P(),
        P(),
        P("req", "tm"),
        P("req"),
        P("req", None),
        P(),
        P(None, None, "tm", None),
        P("tm", None),
        P("tm", None),
        P("tm", None, None),
        P(),
    )
    out_specs = P("tm", None, "req")
    return jax.shard_map(local, mesh=mesh, in_specs=in_specs, out_specs=out_specs, check_vma=False)
```
